32 devices in a mesh: seq: 8 (over z, y), head: 4 (over x, core).
Axes of the slice: x: 2, y: 2, z: 4, core: 2. Of those that a mesh axis runs over, the one named last changes fastest.
Arguments:
- tokens: bfloat16 [6, 2048, 2048], P(None, 'seq'), may hold values from -6 to 6
- doc_reset: int32 [6, 2048], P(None, 'seq'), may hold values from 0 to 1, as said below
- gain_attn: bfloat16 [2048], P('seq'), may hold values from 0.5 to 1.5
- gain_ffn: bfloat16 [2048], P('seq'), may hold values from 0.5 to 1.5
- query_weight: bfloat16 [2048, 256], P('seq', 'head'), may hold values from -0.125 to 0.125
- key_weight: bfloat16 [2048, 256], P('seq', 'head'), may hold values from -0.125 to 0.125
- value_weight: bfloat16 [2048, 2048], P('seq', 'head'), may hold values from -0.125 to 0.125
- out_weight: bfloat16 [2048, 2048], P('head', 'seq'), may hold values from -3 to 3
- gate_weight: bfloat16 [2048, 5632], P('seq', 'head'), may hold values from -0.125 to 0.125
- up_weight: bfloat16 [2048, 5632], P('seq', 'head'), may hold values from -0.125 to 0.125
- down_weight: bfloat16 [5632, 2048], P('head', 'seq'), may hold values from -0.078125 to 0.078125
- grad_out: bfloat16 [6, 2048, 2048], P(None, 'seq'), may hold values from -6 to 6
Outputs:
- block_out: bfloat16 [6, 2048, 2048], P(None, 'seq')
- grad_tokens: float32 [6, 2048, 2048], P(None, 'seq')
- grad_gain_attn: float32 [2048], P('seq')
- grad_gain_ffn: float32 [2048], P('seq')
- grad_query_weight: float32 [2048, 256], P('seq', 'head')
- grad_key_weight: float32 [2048, 256], P('seq', 'head')
- grad_value_weight: float32 [2048, 2048], P('seq', 'head')
- grad_out_weight: float32 [2048, 2048], P('head', 'seq')
- grad_gate_weight: float32 [2048, 5632], P('seq', 'head')
- grad_up_weight: float32 [2048, 5632], P('seq', 'head')
- grad_down_weight: float32 [5632, 2048], P('head', 'seq')
The draws below stay inside these ranges and needn't reach their ends.
Inputs may be any that keep to these rules, and one draw needn't show every extreme that they name: `doc_reset`: 1 marks a token that begins a new document; the first token of a row always begins one and is marked 0. Each micro-batch of 3 rows holds a row without any mark, and every other row has 1 to 4 marks.
All inputs are finite; a program needn't handle non-finite values.
Results may differ from the reference program's by a relative error of at most 0.017.
Values may be sent and summed in bfloat16 or wider, within the bound.
No kernel may reach another device: no remote copies, remote signals or barrier semaphores. Data moves between devices by JAX's collectives and lax.ppermute only.
A program may use at most 448 MiB of HBM per device.

```python
import jax
import jax.numpy as jnp
from jax import lax

D = 2048
HEADS = 16
FEAT = 16
VHEAD = 128
FF = 5632
LEN = 2048
MB = 2
ROWS_MB = 3
ROWS = 6


def draw_doc_reset(key, part):
    key = jax.random.fold_in(key, 11)
    key_place, key_live, key_pick = jax.random.split(key, 3)
    places = jax.random.randint(key_place, (ROWS, 4), 1, LEN)
    active = jax.random.randint(key_live, (ROWS, 4), 0, 2)
    active = active.at[:, 0].set(1)
    chosen = jax.random.randint(key_pick, (MB,), 0, ROWS_MB)
    row_index = jnp.arange(ROWS)
    marked = row_index % ROWS_MB != chosen[row_index // ROWS_MB]
    token_index = jnp.arange(LEN)
    hits = (places[:, :, None] == token_index[None, None, :]) & (active[:, :, None] == 1) & marked[:, None, None]
    return jnp.any(hits, axis=1).astype(jnp.int32)


def level_of(own_key, extent, cuts, least, largest):
    level, own = 1.0, jax.random.fold_in(own_key, 6)
    for dim, blocks in cuts:
        draws = jnp.exp(jax.random.uniform(jax.random.fold_in(own, dim), (blocks,), jnp.float32, least / len(cuts), largest / len(cuts)))
        level = level * jnp.repeat(draws, extent[dim] // blocks).reshape([-1 if axis == dim else 1 for axis in range(len(extent))])
    return level


def normal_values(stream_key, extent, scale, most, cuts=(), dtype=jnp.bfloat16):
    values = jax.random.normal(stream_key, extent, jnp.float32) * scale
    if len(cuts) > 0:
        values = level_of(stream_key, extent, cuts, -0.22, 0.18) * values
    return jnp.clip(values, min=-most, max=most).astype(dtype)


def setup_inputs(seed: int = 0) -> dict:
    key_of = jax.random.split(jax.random.key(seed), 13)
    tokens = normal_values(key_of[0], (ROWS, LEN, D), 1.0, 6.0, ((1, 8),))
    doc_reset = draw_doc_reset(jax.random.fold_in(key_of[12], 71), 0)
    gain_attn = jnp.clip(1.0 + 0.1 * jax.random.normal(key_of[2], (D,), jnp.float32), 0.5, 1.5).astype(jnp.bfloat16)
    gain_ffn = jnp.clip(1.0 + 0.1 * jax.random.normal(key_of[3], (D,), jnp.float32), 0.5, 1.5).astype(jnp.bfloat16)
    query_weight = normal_values(key_of[4], (D, HEADS * FEAT), D ** -0.5, 0.125, ((0, 8), (1, 4)))
    key_weight = normal_values(key_of[5], (D, HEADS * FEAT), D ** -0.5, 0.125, ((0, 8), (1, 4)))
    value_weight = normal_values(key_of[6], (D, HEADS * VHEAD), D ** -0.5, 0.125, ((0, 8), (1, 4)))
    out_weight = normal_values(key_of[7], (HEADS * VHEAD, D), (max(D // 512, 1)) ** -0.5, 3.0, ((0, 4), (1, 8)))
    gate_weight = normal_values(key_of[8], (D, FF), D ** -0.5, 0.125, ((0, 8), (1, 4)))
    up_weight = normal_values(key_of[9], (D, FF), D ** -0.5, 0.125, ((0, 8), (1, 4)))
    down_weight = normal_values(key_of[10], (FF, D), FF ** -0.5, 0.078125, ((0, 4), (1, 8)))
    grad_out = normal_values(key_of[11], (ROWS, LEN, D), 1.0, 6.0, ((1, 8),))
    return dict(tokens=tokens, doc_reset=doc_reset, gain_attn=gain_attn, gain_ffn=gain_ffn, query_weight=query_weight, key_weight=key_weight, value_weight=value_weight, out_weight=out_weight, gate_weight=gate_weight, up_weight=up_weight, down_weight=down_weight, grad_out=grad_out)


epsilon = 1e-06
highest = lax.Precision.HIGHEST

@jax.custom_vjp
def low(v):
    return lax.optimization_barrier(v.astype(jnp.bfloat16)).astype(jnp.float32)

@jax.custom_vjp
def low_back(v):
    return v

def low_keep(v):
    return (low(v), None)

def low_pass(kept, grad):
    return (grad,)

def back_keep(v):
    return (v, None)

def back_low(kept, grad):
    return (low(grad),)
low.defvjp(low_keep, low_pass)
low_back.defvjp(back_keep, back_low)

def matmul(left_operand, right_operand):
    return jnp.dot(left_operand, right_operand, precision=highest, preferred_element_type=jnp.float32)

def rms_scale(values, gain):
    return values * lax.rsqrt(lax.optimization_barrier(jnp.mean(values * values, axis=-1, keepdims=True)) + epsilon) * gain

def taylor_attention(queries, key_vecs, values, doc_ids):
    length = queries.shape[0]
    scores = jnp.einsum('thf,shf->hts', queries, key_vecs, precision=highest) * 0.25
    causal = jnp.arange(length)[:, None] >= jnp.arange(length)[None, :]
    same_doc = doc_ids[:, None] == doc_ids[None, :]
    weights = jnp.where((causal & same_doc)[None], 1.0 + scores + 0.5 * scores * scores, 0.0)
    numerator = jnp.einsum('hts,shv->thv', weights, values, precision=highest)
    denominator = lax.optimization_barrier(jnp.sum(weights, axis=-1)).T
    return numerator / denominator[:, :, None]

def block_row(row_pair, weight_set):
    row_in, doc_ids = row_pair
    gain_attn, gain_ffn, query_weight, key_weight, value_weight, out_weight, gate_weight, up_weight, down_weight = weight_set
    length = row_in.shape[0]
    normed_one = low(rms_scale(row_in, gain_attn))
    queries = low(low_back(matmul(normed_one, query_weight))).reshape(length, HEADS, FEAT)
    key_vecs = low(low_back(matmul(normed_one, key_weight))).reshape(length, HEADS, FEAT)
    values = low(low_back(matmul(normed_one, value_weight))).reshape(length, HEADS, VHEAD)
    attended = low(taylor_attention(queries, key_vecs, values, doc_ids).reshape(length, HEADS * VHEAD))
    branch = low_back(matmul(attended, out_weight))
    hidden_one = row_in + branch
    normed_two = low(rms_scale(hidden_one, gain_ffn))
    gate_act = low_back(matmul(normed_two, gate_weight))
    up_act = low_back(matmul(normed_two, up_weight))
    mixed_act = low(jax.nn.silu(gate_act) * up_act)
    return hidden_one + matmul(mixed_act, down_weight)

def forward(doc_ids, tokens, *weight_set):
    row_step = jax.checkpoint(lambda row_pair: block_row(row_pair, weight_set))
    return lax.map(row_step, (tokens, doc_ids))

def reference(tokens, doc_reset, gain_attn, gain_ffn, query_weight, key_weight, value_weight, out_weight, gate_weight, up_weight, down_weight, grad_out):
    doc_ids = jnp.cumsum(doc_reset, axis=1).astype(jnp.int32)
    floats = tuple((item.astype(jnp.float32) for item in (tokens, gain_attn, gain_ffn, query_weight, key_weight, value_weight, out_weight, gate_weight, up_weight, down_weight)))
    result, pullback = jax.vjp(lambda *items: forward(doc_ids, *items), *floats)
    gradients = pullback(grad_out.astype(jnp.float32))
    return (result.astype(jnp.bfloat16), gradients[0], gradients[1], gradients[2], gradients[3], gradients[4], gradients[5], gradients[6], gradients[7], gradients[8], gradients[9])
```

```python
import functools

import jax
import jax.numpy as jnp
import numpy as np
from jax import lax
from jax.experimental import pallas as pl
from jax.experimental.pallas import tpu as pltpu
from jax.sharding import PartitionSpec as P

FEAT = 16
VHEAD = 128
EPSILON = 1e-06
PAIRS = [(a, b) for a in range(FEAT + 1) for b in range(a, FEAT + 1)]
WIDE = 256
TALL = 160
NORM_ROW = len(PAIRS)
FLAG_ROW = NORM_ROW + 2
BLOCKS = 8
bf16, f32 = jnp.bfloat16, jnp.float32


def feature_tables(heads):
    lanes = 2 * heads * FEAT
    tables = {name: np.zeros((lanes, heads * WIDE), np.float32) for name in ("qa", "qb", "ka", "kb")}
    rows = np.zeros((8, heads * WIDE), np.float32)
    to_key = np.zeros((lanes, heads * lanes), np.float32)
    to_query = np.zeros((lanes, heads * lanes), np.float32)
    for head in range(heads):
        for place, (a, b) in enumerate(PAIRS):
            column = head * WIDE + place
            for name, entry, row in (("a", a, 0), ("b", b, 1)):
                if entry == 0:
                    rows[row, column] = 1.0
                else:
                    lane = head * FEAT + entry - 1
                    tables["q" + name][lane, column] = 1.0
                    tables["k" + name][heads * FEAT + lane, column] = 1.0
            rows[2, column] = 1.0 if b == 0 else 0.25 if a == 0 else 1 / 32 if a == b else 1 / 16
        for feat in range(FEAT):
            lane = head * FEAT + feat
            to_key[lane, head * lanes + heads * FEAT + lane] = 0.25
            to_query[heads * FEAT + lane, head * lanes + lane] = 0.25
    tables = {name: jnp.asarray(item, bf16) for name, item in tables.items()}
    return tables, jnp.asarray(rows), jnp.asarray(to_key, bf16), jnp.asarray(to_query, bf16)


def nn(left, right):
    return lax.dot_general(left, right, (((1,), (0,)), ((), ())), preferred_element_type=f32)


def nt(left, right):
    return lax.dot_general(left, right, (((1,), (1,)), ((), ())), preferred_element_type=f32)


def tn(left, right):
    return lax.dot_general(left, right, (((0,), (0,)), ((), ())), preferred_element_type=f32)


def params(mib=32):
    return pltpu.CompilerParams(vmem_limit_bytes=mib << 20)


def cost(flops, nbytes):
    return pl.CostEstimate(flops=int(flops), bytes_accessed=int(nbytes), transcendentals=0)


def whole_spec(array):
    zeros = (0,) * array.ndim
    return pl.BlockSpec(array.shape, lambda *_: zeros)


def row_spec(array):
    zeros = (0,) * (array.ndim - 1)
    return pl.BlockSpec((1,) + array.shape[1:], lambda row, *_: (row,) + zeros)


def pack_state(state, norm_row, flag):
    place = lax.broadcasted_iota(jnp.int32, (TALL, VHEAD), 0)
    block = state[:TALL]
    block = jnp.where(place == NORM_ROW, norm_row[:, :VHEAD], block)
    block = jnp.where(place == NORM_ROW + 1, norm_row[:, VHEAD:], block)
    return jnp.where(place == FLAG_ROW, flag, block).astype(bf16)


def unpack_state(block):
    tail = block[TALL - 16 :].astype(f32)
    base = TALL - 16
    low = tail[NORM_ROW - base : NORM_ROW - base + 1]
    high = tail[NORM_ROW + 1 - base : NORM_ROW + 2 - base]
    full = jnp.concatenate([block, jnp.zeros((WIDE - TALL, VHEAD), block.dtype)], axis=0)
    return full, jnp.concatenate([low, high], axis=1)


def state_kernel(heads, qkv_ref, edge_ref, ka_ref, kb_ref, rows_ref, out_ref):
    keys = qkv_ref[0, :, : 2 * heads * FEAT]
    edges = edge_ref[0]
    last, flag = edges[:, 2:3], edges[0:1, 3:4]
    for head in range(heads):
        cols = slice(head * WIDE, (head + 1) * WIDE)
        phi = (nn(keys, ka_ref[:, cols]) + rows_ref[0:1, cols]) * (nn(keys, kb_ref[:, cols]) + rows_ref[1:2, cols])
        phi = phi * last
        start = 2 * heads * FEAT + head * VHEAD
        state = tn(phi.astype(bf16), qkv_ref[0, :, start : start + VHEAD])
        out_ref[0, head] = pack_state(state, jnp.sum(phi, axis=0, keepdims=True), flag)


def local_mask(edges, docs):
    length = edges.shape[0]
    later = lax.broadcasted_iota(jnp.int32, (length, length), 0) >= lax.broadcasted_iota(jnp.int32, (length, length), 1)
    return later & (edges[:, 0:1] == docs)


def inside_kernel(heads, qkv_ref, edge_ref, doc_ref, key_ref, num_ref, den_ref):
    lanes = 2 * heads * FEAT
    both = qkv_ref[0, :, :lanes]
    mask = local_mask(edge_ref[0], doc_ref[0, 0:1])
    moved = nn(both, key_ref[...]).astype(bf16)
    dens = []
    for head in range(heads):
        scores = nt(moved[:, head * lanes : (head + 1) * lanes], both)
        weights = jnp.where(mask, 1.0 + scores + 0.5 * scores * scores, 0.0)
        dens.append(jnp.sum(weights, axis=1, keepdims=True))
        start = lanes + head * VHEAD
        num_ref[0, :, head * VHEAD : (head + 1) * VHEAD] = nn(
            weights.astype(bf16), qkv_ref[0, :, start : start + VHEAD]
        )
    den_ref[0] = jnp.concatenate(dens, axis=1)


def block_at(place_ref, states_ref, row, heads, head):
    per = states_ref.shape[1]
    index = row * heads + head
    return states_ref[place_ref[index // per], index % per]


def query_features(both, qa, qb, rows, first):
    left = nn(both, qa) + rows[0:1]
    right = nn(both, qb) + rows[1:2]
    return left, right, left * right * rows[2:3] * first


def attend_kernel(heads, place_ref, qkv_ref, edge_ref, num_ref, den_ref, states_ref, qa_ref, qb_ref, rows_ref, att_ref, rden_ref):
    both = qkv_ref[0, :, : 2 * heads * FEAT]
    first = edge_ref[0][:, 1:2]
    rdens = []
    for head in range(heads):
        cols = slice(head * WIDE, (head + 1) * WIDE)
        _, _, phi = query_features(both, qa_ref[:, cols], qb_ref[:, cols], rows_ref[:, cols], first)
        factor, norm = unpack_state(block_at(place_ref, states_ref, pl.program_id(0), heads, head))
        den = den_ref[0][:, head : head + 1] + jnp.sum(phi * norm, axis=1, keepdims=True)
        rden = 1.0 / den
        out = slice(head * VHEAD, (head + 1) * VHEAD)
        att_ref[0, :, out] = ((num_ref[0, :, out] + nn(phi.astype(bf16), factor)) * rden).astype(bf16)
        rdens.append(rden)
    rden_ref[0] = jnp.concatenate(rdens, axis=1)


def carry_kernel(heads, qkv_ref, edge_ref, ga_ref, att_ref, rden_ref, qa_ref, qb_ref, rows_ref, carry_ref, gnum_ref, gden_ref):
    both = qkv_ref[0, :, : 2 * heads * FEAT]
    edges = edge_ref[0]
    first, flag = edges[:, 1:2], edges[0:1, 3:4]
    gdens = []
    for head in range(heads):
        cols = slice(head * WIDE, (head + 1) * WIDE)
        out = slice(head * VHEAD, (head + 1) * VHEAD)
        _, _, phi = query_features(both, qa_ref[:, cols], qb_ref[:, cols], rows_ref[:, cols], first)
        grad = ga_ref[0, :, out].astype(f32)
        rden = rden_ref[0][:, head : head + 1]
        gnum = (grad * rden).astype(bf16)
        gden = -jnp.sum(grad * att_ref[0, :, out].astype(f32), axis=1, keepdims=True) * rden
        gnum_ref[0, :, out] = gnum
        carry_ref[0, head] = pack_state(
            tn(phi.astype(bf16), gnum), jnp.sum(phi * gden, axis=0, keepdims=True), flag
        )
        gdens.append(gden)
    gden_ref[0] = jnp.concatenate(gdens, axis=1)


def inside_back_kernel(
    heads, place_ref, qkv_ref, edge_ref, doc_ref, gnum_ref, gden_ref, states_ref, key_ref, query_ref, qa_ref, qb_ref,
    rows_ref, gboth_ref, gval_ref,
):
    lanes = 2 * heads * FEAT
    both = qkv_ref[0, :, :lanes]
    edges = edge_ref[0]
    first = edges[:, 1:2]
    mask = local_mask(edges, doc_ref[0, 0:1])
    moved = nn(both, key_ref[...]).astype(bf16)
    back = nn(both, query_ref[...]).astype(bf16)
    total = jnp.zeros((both.shape[0], lanes), f32)
    for head in range(heads):
        cols = slice(head * WIDE, (head + 1) * WIDE)
        out = slice(head * VHEAD, (head + 1) * VHEAD)
        own = slice(head * lanes, (head + 1) * lanes)
        start = lanes + head * VHEAD
        values = qkv_ref[0, :, start : start + VHEAD]
        gnum = gnum_ref[0, :, out]
        gden = gden_ref[0][:, head : head + 1]
        scores = nt(moved[:, own], both)
        weights = jnp.where(mask, 1.0 + scores + 0.5 * scores * scores, 0.0).astype(bf16)
        gval_ref[0, :, out] = tn(weights, gnum)
        gscores = jnp.where(mask, (nt(gnum, values) + gden) * (1.0 + scores), 0.0).astype(bf16)
        total = total + nn(gscores, back[:, own]) + tn(gscores, moved[:, own])
        left, right, _ = query_features(both, qa_ref[:, cols], qb_ref[:, cols], rows_ref[:, cols], first)
        factor, norm = unpack_state(block_at(place_ref, states_ref, pl.program_id(0), heads, head))
        place = lax.broadcasted_iota(jnp.int32, (1, WIDE), 1)
        gphi = jnp.where(place < NORM_ROW, (nt(gnum, factor) + norm * gden) * rows_ref[2:3, cols], 0.0) * first
        total = total + nt((gphi * right).astype(bf16), qa_ref[:, cols]) + nt((gphi * left).astype(bf16), qb_ref[:, cols])
    gboth_ref[0] = total


def finish_back_kernel(
    heads, place_ref, qkv_ref, edge_ref, carry_ref, gboth_ref, gval_ref, ka_ref, kb_ref, rows_ref, out_ref
):
    lanes = 2 * heads * FEAT
    both = qkv_ref[0, :, :lanes]
    last = edge_ref[0][:, 2:3]
    total = gboth_ref[0]
    for head in range(heads):
        cols = slice(head * WIDE, (head + 1) * WIDE)
        start = lanes + head * VHEAD
        values = qkv_ref[0, :, start : start + VHEAD]
        left = nn(both, ka_ref[:, cols]) + rows_ref[0:1, cols]
        right = nn(both, kb_ref[:, cols]) + rows_ref[1:2, cols]
        factor, norm = unpack_state(block_at(place_ref, carry_ref, pl.program_id(0), heads, head))
        phi = (left * right * last).astype(bf16)
        gval = gval_ref[0, :, head * VHEAD : (head + 1) * VHEAD] + nn(phi, factor)
        out_ref[0, :, start : start + VHEAD] = gval.astype(bf16)
        place = lax.broadcasted_iota(jnp.int32, (1, WIDE), 1)
        gphi = jnp.where(place < NORM_ROW, nt(values, factor) + norm, 0.0) * last
        total = total + nt((gphi * right).astype(bf16), ka_ref[:, cols]) + nt((gphi * left).astype(bf16), kb_ref[:, cols])
    out_ref[0, :, :lanes] = total.astype(bf16)


def by_row(kernel, rows, inputs, outputs, place=None, flops=0):
    arrays = [array for array, _ in inputs]
    specs = [row_spec(array) if per_row else whole_spec(array) for array, per_row in inputs]
    shapes = [jax.ShapeDtypeStruct((rows,) + shape, kind) for shape, kind in outputs]
    nbytes = sum(item.size * item.dtype.itemsize for item in arrays + shapes)
    return pl.pallas_call(
        kernel,
        out_shape=shapes,
        grid_spec=pltpu.PrefetchScalarGridSpec(
            num_scalar_prefetch=0 if place is None else 1,
            grid=(rows,),
            in_specs=specs,
            out_specs=[row_spec(shape) for shape in shapes],
        ),
        compiler_params=params(40),
        cost_estimate=cost(flops, nbytes),
    )(*([] if place is None else [place]), *arrays)


def scan_kernel(backward, count, me_ref, *refs):
    pieces, outs, (held, ahead) = refs[:count], refs[count : 2 * count], refs[2 * count :]
    for rel in range(count):
        held[rel] = pieces[rel][...]
    me = me_ref[0]
    for block in range(held.shape[1]):
        run = jnp.zeros(held.shape[2:], f32)
        for step in range(count):
            rel = me ^ (count - 1 - step if backward else step)
            ahead[rel, block] = run.astype(bf16)
            own = held[rel, block].astype(f32)
            run = own + (1.0 - own[FLAG_ROW : FLAG_ROW + 1]) * run
    for rel in range(count):
        outs[rel][...] = ahead[rel]


def exclusive_scan(states, backward, me, count):
    blocks = states.shape[0] * states.shape[1]
    flat = states.reshape(blocks, TALL, VHEAD)
    if count == 8 and blocks % 8 == 0:
        per = blocks // 8
        split = flat.reshape(8, per * TALL, VHEAD)
        pieces = []
        for rel in range(8):
            part = lax.dynamic_index_in_dim(split, me ^ rel, 0, keepdims=False)
            if rel:
                part = lax.ppermute(part, "seq", [(i, i ^ rel) for i in range(8)])
            pieces.append(part.reshape(per, TALL, VHEAD))
        shape = jax.ShapeDtypeStruct((per, TALL, VHEAD), bf16)
        outs = pl.pallas_call(
            functools.partial(scan_kernel, backward, 8),
            out_shape=[shape] * 8,
            in_specs=[pl.BlockSpec(memory_space=pltpu.SMEM)] + [pl.BlockSpec(memory_space=pltpu.VMEM)] * 8,
            out_specs=[pl.BlockSpec(memory_space=pltpu.VMEM)] * 8,
            scratch_shapes=[pltpu.VMEM((8, per, TALL, VHEAD), bf16)] * 2,
            compiler_params=params(),
        )(me.reshape(1), *pieces)
        back = [outs[0]]
        for rel in range(1, 8):
            back.append(lax.ppermute(outs[rel], "seq", [(i, i ^ rel) for i in range(8)]))
        return jnp.stack(back), me ^ jnp.arange(8, dtype=jnp.int32)
    every = lax.all_gather(flat, "seq").astype(f32)
    keep = 1.0 - every[:, :, FLAG_ROW : FLAG_ROW + 1]
    run = jnp.zeros(flat.shape, f32)
    for step in range(count):
        at = count - 1 - step if backward else step
        reached = at > me if backward else at < me
        run = jnp.where(reached, every[at] + keep[at] * run, run)
    return run.astype(bf16)[None], jnp.zeros((1,), jnp.int32)


SWAP = [(i, i ^ 1) for i in range(8)]


def up_pairs(least):
    return [(i, i + 2) for i in range(6) if i // 2 >= least]


def down_pairs(most):
    return [(i + 2, i) for i in range(6) if i // 2 + 1 <= most]


def send(value, axis, pairs):
    return lax.ppermute(value, axis, pairs)


def join_rows(pieces):
    return jnp.concatenate(pieces, axis=0)


def gather_rows(shard, count, me):
    if count != 8:
        return lax.all_gather(shard, "seq", axis=0, tiled=True)
    z = me // 2
    up, down = [shard], [shard]
    for step in range(3):
        up.append(send(up[-1], "seq", up_pairs(step)))
        down.append(send(down[-1], "seq", down_pairs(3 - step)))
    other = send(shard, "seq", SWAP)
    pieces = [shard, other]
    for k in range(1, 4):
        below, above = up[4 - k], down[k]
        low = [pair for pair in SWAP if pair[0] // 2 >= 4 - k]
        high = [pair for pair in SWAP if pair[0] // 2 < 4 - k]
        from_above = z + k <= 3
        pieces.append(jnp.where(from_above, above, below))
        pieces.append(jnp.where(from_above, send(above, "seq", high), send(below, "seq", low)))
    return join_rows(pieces)


def scatter_rows(whole, count):
    if count != 8:
        return lax.psum_scatter(whole, "seq", scatter_dimension=0, tiled=True).astype(f32)
    rows = whole.shape[0] // 8
    parts = [whole[place * rows : (place + 1) * rows].astype(f32) for place in range(8)]
    low = lambda value: value.astype(bf16)
    pair = [None] * 4
    for k in (3, 1, 2, 0):
        pair[k] = parts[2 * k] + send(whole[(2 * k + 1) * rows : (2 * k + 2) * rows], "seq", SWAP).astype(f32)
    up = send(low(pair[3]), "seq", [(i, i + 2) for i in (0, 1)])
    down = send(low(pair[1]), "seq", [(i + 2, i) for i in (4, 5)])
    up = send(low(pair[2] + up.astype(f32)), "seq", [(i, i + 2) for i in range(4)])
    down = send(low(pair[2] + down.astype(f32)), "seq", [(i + 2, i) for i in range(2, 6)])
    up = send(low(pair[1] + up.astype(f32)), "seq", [(i, i + 2) for i in range(6)])
    down = send(low(pair[3] + down.astype(f32)), "seq", [(i + 2, i) for i in range(6)])
    return pair[0] + up.astype(f32) + down.astype(f32)


CORE = [(i, i ^ 1) for i in range(4)]
ACROSS = [(i, i ^ 2) for i in range(4)]
ORDER = (0, 2, 1, 3)


def scatter_head(partial):
    rows = partial.shape[0] // 4
    quarter = [partial[i * rows : (i + 1) * rows] for i in range(4)]
    far = send(quarter[3], "head", CORE)
    across = send((quarter[1].astype(f32) + far.astype(f32)).astype(bf16), "head", ACROSS)
    near = send(quarter[2], "head", CORE)
    return quarter[0].astype(f32) + near.astype(f32) + across.astype(f32)


def gather_head(own):
    across = send(own, "head", ACROSS)
    core = send(own, "head", CORE)
    both = send(across, "head", CORE)
    return join_rows([own, across, core, both])


def to_own_order(array, me):
    split = array.reshape((4, array.shape[0] // 4) + array.shape[1:])
    return join_rows([lax.dynamic_index_in_dim(split, me ^ mask, 0, keepdims=False) for mask in ORDER])


def to_token_order(array, me):
    split = array.reshape((4, array.shape[0] // 4) + array.shape[1:])
    pieces = []
    for quarter in range(4):
        mask = quarter ^ me
        pieces.append(lax.dynamic_index_in_dim(split, (mask & 1) * 2 + (mask >> 1), 0, keepdims=False))
    return join_rows(pieces)


def move_kernel(split, rows_ref, cols_ref, in_ref, out_ref):
    width = in_ref.shape[1] // BLOCKS
    for block in range(BLOCKS):
        start = pl.multiple_of(cols_ref[block] * width, 128)
        out_ref[:, block * width : (block + 1) * width] = in_ref[:, pl.ds(start, width)].astype(out_ref.dtype)


def move_blocks(array, row_blocks, col_blocks, out_type, quarter):
    width = array.shape[1]
    split = 2 if quarter % 32 == 0 else 1
    tile = quarter // split
    count = row_blocks.shape[0]
    shape = jax.ShapeDtypeStruct((count * quarter, width), out_type)
    return pl.pallas_call(
        functools.partial(move_kernel, split),
        out_shape=shape,
        grid_spec=pltpu.PrefetchScalarGridSpec(
            num_scalar_prefetch=2,
            grid=(count, split),
            in_specs=[pl.BlockSpec((tile, width), lambda i, j, rows, cols: (rows[i] * split + j, 0))],
            out_specs=pl.BlockSpec((tile, width), lambda i, j, rows, cols: (i * split + j, 0)),
        ),
        compiler_params=params(),
        cost_estimate=cost(0, shape.size * (array.dtype.itemsize + shape.dtype.itemsize)),
    )(row_blocks, col_blocks, array)


def unit_kernel(cols_ref, in_ref, out_ref):
    values = in_ref[...].astype(f32)
    rstd = lax.rsqrt(jnp.mean(values * values, axis=1, keepdims=True) + EPSILON)
    width = in_ref.shape[1] // BLOCKS
    for block in range(BLOCKS):
        start = pl.multiple_of(cols_ref[block] * width, 128)
        out_ref[:, block * width : (block + 1) * width] = (in_ref[:, pl.ds(start, width)].astype(f32) * rstd).astype(bf16)


def unit_rows(array, col_blocks, tile):
    rows, width = array.shape
    return pl.pallas_call(
        unit_kernel,
        out_shape=jax.ShapeDtypeStruct((rows, width), bf16),
        grid_spec=pltpu.PrefetchScalarGridSpec(
            num_scalar_prefetch=1,
            grid=(rows // tile,),
            in_specs=[pl.BlockSpec((tile, width), lambda i, cols: (i, 0))],
            out_specs=pl.BlockSpec((tile, width), lambda i, cols: (i, 0)),
        ),
        compiler_params=params(),
        cost_estimate=cost(0, 4 * rows * width),
    )(col_blocks, array)


def ffn_kernel(step, unit_ref, dy_ref, gate_ref, up_ref, down_ref, mixed_ref, ggate_ref, gup_ref):
    width = gate_ref.shape[1]
    unit, dy = unit_ref[...], dy_ref[...]
    for start in range(0, width, step):
        cols = slice(start, min(start + step, width))
        gate = nn(unit, gate_ref[:, cols])
        up = nn(unit, up_ref[:, cols])
        gmixed = nn(dy, down_ref[:, cols])
        sig = jax.nn.sigmoid(gate)
        silu = gate * sig
        mixed_ref[:, cols] = (silu * up).astype(bf16)
        ggate_ref[:, cols] = (gmixed * up * (sig * (1.0 + gate * (1.0 - sig)))).astype(bf16)
        gup_ref[:, cols] = (gmixed * silu).astype(bf16)


def feed_forward(unit, dy, gate_w, up_w, down_w):
    tokens, width = unit.shape
    hidden = gate_w.shape[1]
    tile = 256 if tokens % 256 == 0 else 128
    once = pl.BlockSpec((width, hidden), lambda i: (0, 0), pipeline_mode=pl.Buffered(1))
    lines = pl.BlockSpec((tile, width), lambda i: (i, 0))
    out = pl.BlockSpec((tile, hidden), lambda i: (i, 0))
    return pl.pallas_call(
        functools.partial(ffn_kernel, 256),
        out_shape=[jax.ShapeDtypeStruct((tokens, hidden), bf16)] * 3,
        grid=(tokens // tile,),
        in_specs=[lines, lines, once, once, once],
        out_specs=[out, out, out],
        compiler_params=params(56),
        cost_estimate=cost(6 * tokens * width * hidden, 2 * (2 * tokens * width + 3 * (tokens + width) * hidden)),
    )(unit, dy, gate_w, up_w, down_w)


def per_device(
    n_seq,
    n_head,
    tokens,
    doc_reset,
    gain_attn,
    gain_ffn,
    query_weight,
    key_weight,
    value_weight,
    out_weight,
    gate_weight,
    up_weight,
    down_weight,
    grad_out,
):
    rows, length, width = tokens.shape
    heads = query_weight.shape[1] // FEAT
    count = rows * length
    quarter = count // 4
    me = lax.axis_index("seq").astype(jnp.int32)
    head_me = lax.axis_index("head").astype(jnp.int32)
    ids = jnp.arange(BLOCKS, dtype=jnp.int32)
    if n_seq == 8:
        z, y = me // 2, me % 2
        to_rel = ((z + ids // 2) % 4) * 2 + (y ^ (ids % 2))
        to_abs = ((ids // 2 - z) % 4) * 2 + (y ^ (ids % 2))
    else:
        to_rel = to_abs = ids
    own_order = head_me ^ jnp.array(ORDER, jnp.int32)
    masks = head_me ^ jnp.arange(4, dtype=jnp.int32)
    token_order = (masks & 1) * 2 + (masks >> 1)

    gain_one = gain_attn.astype(f32)[:, None]
    gain_two = gain_ffn.astype(f32)[:, None]
    scaled = lambda weight, gain: (weight.astype(f32) * gain).astype(bf16)
    qkv_own = jnp.concatenate([query_weight, key_weight, value_weight], axis=1)
    gather = functools.partial(gather_rows, count=n_seq, me=me)
    qkv_w = gather(scaled(qkv_own, gain_one))
    out_w = gather(out_weight.T)
    gate_w = gather(scaled(gate_weight, gain_two))
    up_w = gather(scaled(up_weight, gain_two))
    down_w = gather(down_weight.T)

    flat = tokens.reshape(count, width)
    unit_one = unit_rows(flat, to_rel, quarter // 2)
    x_own = move_blocks(flat, own_order[:1], to_rel, f32, quarter)
    dy = move_blocks(grad_out.reshape(count, width), own_order, to_rel, bf16, quarter)
    rstd_one = lax.rsqrt(jnp.mean(x_own * x_own, axis=1, keepdims=True) + EPSILON)

    docs = jnp.cumsum(doc_reset, axis=1)
    final = docs[:, -1:]
    flag = jnp.broadcast_to(final > 0, docs.shape)
    edges = jnp.stack([docs, docs == 0, docs == final, flag] + [jnp.zeros_like(docs)] * 4, axis=2).astype(f32)
    doc_rows = jnp.broadcast_to(docs[:, None, :], (rows, 8, length)).astype(f32)
    tables, feat_rows, to_key, to_query = feature_tables(heads)

    lanes = 2 * heads * FEAT
    values = heads * VHEAD
    unit_flops = 2 * rows * heads * length * WIDE * VHEAD
    qkv = nn(unit_one, qkv_w).astype(bf16).reshape(rows, length, lanes + values)
    (states,) = by_row(
        functools.partial(state_kernel, heads),
        rows,
        [(qkv, True), (edges, True), (tables["ka"], False), (tables["kb"], False), (feat_rows, False)],
        [((heads, TALL, VHEAD), bf16)],
        flops=3 * unit_flops,
    )
    numerator, denominator = by_row(
        functools.partial(inside_kernel, heads),
        rows,
        [(qkv, True), (edges, True), (doc_rows, True), (to_key, False)],
        [((length, values), f32), ((length, heads), f32)],
        flops=3 * unit_flops,
    )
    state_in, place = exclusive_scan(states, False, me, n_seq)
    query_tables = [(tables["qa"], False), (tables["qb"], False), (feat_rows, False)]
    key_tables = [(tables["ka"], False), (tables["kb"], False), (feat_rows, False)]
    attended, rden = by_row(
        functools.partial(attend_kernel, heads),
        rows,
        [(qkv, True), (edges, True), (numerator, True), (denominator, True), (state_in, False)] + query_tables,
        [((length, values), bf16), ((length, heads), f32)],
        place=place,
        flops=3 * unit_flops,
    )
    attended_own = to_own_order(attended.reshape(count, values), head_me)
    branch = nt(attended_own, out_w).astype(bf16)
    hidden = x_own + scatter_head(branch)
    rstd_two = lax.rsqrt(jnp.mean(hidden * hidden, axis=1, keepdims=True) + EPSILON)
    unit_two_own = hidden * rstd_two
    unit_two = gather_head(unit_two_own.astype(bf16))

    mixed, ggate, gup = feed_forward(unit_two, dy, gate_w, up_w, down_w)
    scaled_two = scatter_head((nt(ggate, gate_w) + nt(gup, up_w)).astype(bf16))
    grad_gate = scatter_rows(tn(unit_two, ggate).astype(bf16), n_seq)
    grad_up = scatter_rows(tn(unit_two, gup).astype(bf16), n_seq)
    grad_down = scatter_rows(tn(dy, mixed).astype(bf16), n_seq)

    dy_own = dy[:quarter].astype(f32)
    grad_hidden = dy_own + rstd_two * (
        scaled_two - unit_two_own * jnp.mean(scaled_two * unit_two_own, axis=1, keepdims=True)
    )
    grad_branch = gather_head(grad_hidden.astype(bf16))

    block_own = hidden + scatter_head(nt(mixed, down_w).astype(bf16))
    block_all = gather_head(block_own.astype(bf16))

    grad_att = to_token_order(nn(grad_branch, out_w).astype(bf16), head_me).reshape(rows, length, values)
    carry, gnum, gden = by_row(
        functools.partial(carry_kernel, heads),
        rows,
        [(qkv, True), (edges, True), (grad_att, True), (attended, True), (rden, True)] + query_tables,
        [((heads, TALL, VHEAD), bf16), ((length, values), bf16), ((length, heads), f32)],
        flops=3 * unit_flops,
    )
    gboth, gval = by_row(
        functools.partial(inside_back_kernel, heads),
        rows,
        [(qkv, True), (edges, True), (doc_rows, True), (gnum, True), (gden, True), (state_in, False)]
        + [(to_key, False), (to_query, False)]
        + query_tables,
        [((length, lanes), f32), ((length, values), f32)],
        place=place,
        flops=11 * unit_flops,
    )
    grad_out_w = scatter_rows(tn(grad_branch, attended_own).astype(bf16), n_seq)
    carry_in, place_back = exclusive_scan(carry, True, me, n_seq)
    (gqkv,) = by_row(
        functools.partial(finish_back_kernel, heads),
        rows,
        [(qkv, True), (edges, True), (carry_in, False), (gboth, True), (gval, True)] + key_tables,
        [((length, lanes + values), bf16)],
        place=place_back,
        flops=6 * unit_flops,
    )
    gqkv = gqkv.reshape(count, lanes + values)
    scaled_one = scatter_head(nt(to_own_order(gqkv, head_me), qkv_w).astype(bf16))
    grad_qkv = scatter_rows(tn(unit_one, gqkv).astype(bf16), n_seq)
    unit_one_own = x_own * rstd_one
    grad_x = grad_hidden + rstd_one * (
        scaled_one - unit_one_own * jnp.mean(scaled_one * unit_one_own, axis=1, keepdims=True)
    )
    grad_x_all = gather_head(grad_x.astype(bf16))

    back = lambda value, kind: move_blocks(value, token_order, to_abs, kind, quarter).reshape(rows, length, width)
    gain_sums = jnp.stack(
        [
            jnp.sum(qkv_own.astype(f32) * grad_qkv, axis=1),
            jnp.sum(gate_weight.astype(f32) * grad_gate + up_weight.astype(f32) * grad_up, axis=1),
        ]
    )
    gain_sums = gain_sums + send(gain_sums, "head", CORE)
    gain_sums = gain_sums + send(gain_sums, "head", ACROSS)
    grad_qkv = grad_qkv * gain_one
    narrow = heads * FEAT
    return (
        back(block_all, bf16),
        back(grad_x_all, f32),
        gain_sums[0],
        gain_sums[1],
        grad_qkv[:, :narrow],
        grad_qkv[:, narrow:lanes],
        grad_qkv[:, lanes:],
        grad_out_w.T,
        grad_gate * gain_two,
        grad_up * gain_two,
        grad_down.T,
    )


def solution(mesh):
    placed = (
        P(None, "seq", None),
        P(None, "seq"),
        P("seq"),
        P("seq"),
        P("seq", "head"),
        P("seq", "head"),
        P("seq", "head"),
        P("head", "seq"),
        P("seq", "head"),
        P("seq", "head"),
        P("head", "seq"),
        P(None, "seq", None),
    )
    return jax.shard_map(
        functools.partial(per_device, mesh.shape["seq"], mesh.shape["head"]),
        mesh=mesh,
        in_specs=placed,
        out_specs=(P(None, "seq", None), P(None, "seq", None)) + placed[2:11],
        check_vma=False,
    )
```

```python
import functools

import jax
import jax.numpy as jnp
import numpy as np
from jax import lax
from jax.experimental import pallas as pl
from jax.experimental.pallas import tpu as pltpu
from jax.sharding import PartitionSpec as P

FEAT = 16
VHEAD = 128
EPSILON = 1e-06
PAIRS = [(a, b) for a in range(FEAT + 1) for b in range(a, FEAT + 1)]
WIDE = 256
TALL = 160
NORM_ROW = len(PAIRS)
FLAG_ROW = NORM_ROW + 2
BLOCKS = 8
bf16, f32 = jnp.bfloat16, jnp.float32


def feature_tables(heads):
    lanes = 2 * heads * FEAT
    tables = {name: np.zeros((lanes, heads * WIDE), np.float32) for name in ("qa", "qb", "ka", "kb")}
    rows = np.zeros((8, heads * WIDE), np.float32)
    to_key = np.zeros((lanes, heads * lanes), np.float32)
    to_query = np.zeros((lanes, heads * lanes), np.float32)
    for head in range(heads):
        for place, (a, b) in enumerate(PAIRS):
            column = head * WIDE + place
            for name, entry, row in (("a", a, 0), ("b", b, 1)):
                if entry == 0:
                    rows[row, column] = 1.0
                else:
                    lane = head * FEAT + entry - 1
                    tables["q" + name][lane, column] = 1.0
                    tables["k" + name][heads * FEAT + lane, column] = 1.0
            rows[2, column] = 1.0 if b == 0 else 0.25 if a == 0 else 1 / 32 if a == b else 1 / 16
        for feat in range(FEAT):
            lane = head * FEAT + feat
            to_key[lane, head * lanes + heads * FEAT + lane] = 0.25
            to_query[heads * FEAT + lane, head * lanes + lane] = 0.25
    tables = {name: jnp.asarray(item, bf16) for name, item in tables.items()}
    return tables, jnp.asarray(rows), jnp.asarray(to_key, bf16), jnp.asarray(to_query, bf16)


def nn(left, right):
    return lax.dot_general(left, right, (((1,), (0,)), ((), ())), preferred_element_type=f32)


def nt(left, right):
    return lax.dot_general(left, right, (((1,), (1,)), ((), ())), preferred_element_type=f32)


def tn(left, right):
    return lax.dot_general(left, right, (((0,), (0,)), ((), ())), preferred_element_type=f32)


def params(mib=32):
    return pltpu.CompilerParams(vmem_limit_bytes=mib << 20)


def cost(flops, nbytes):
    return pl.CostEstimate(flops=int(flops) // 32, bytes_accessed=int(nbytes) // 32, transcendentals=0)


def whole_spec(array):
    zeros = (0,) * array.ndim
    return pl.BlockSpec(array.shape, lambda *_: zeros)


def row_spec(array):
    zeros = (0,) * (array.ndim - 1)
    return pl.BlockSpec((1,) + array.shape[1:], lambda row, *_: (row,) + zeros)


def pack_state(state, norm_row, flag):
    place = lax.broadcasted_iota(jnp.int32, (TALL, VHEAD), 0)
    block = state[:TALL]
    block = jnp.where(place == NORM_ROW, norm_row[:, :VHEAD], block)
    block = jnp.where(place == NORM_ROW + 1, norm_row[:, VHEAD:], block)
    return jnp.where(place == FLAG_ROW, flag, block).astype(bf16)


def unpack_state(block):
    tail = block[TALL - 16 :].astype(f32)
    base = TALL - 16
    low = tail[NORM_ROW - base : NORM_ROW - base + 1]
    high = tail[NORM_ROW + 1 - base : NORM_ROW + 2 - base]
    full = jnp.concatenate([block, jnp.zeros((WIDE - TALL, VHEAD), block.dtype)], axis=0)
    return full, jnp.concatenate([low, high], axis=1)


def state_kernel(heads, qkv_ref, edge_ref, ka_ref, kb_ref, rows_ref, out_ref):
    keys = qkv_ref[0, :, : 2 * heads * FEAT]
    edges = edge_ref[0]
    last, flag = edges[:, 2:3], edges[0:1, 3:4]
    for head in range(heads):
        cols = slice(head * WIDE, (head + 1) * WIDE)
        phi = (nn(keys, ka_ref[:, cols]) + rows_ref[0:1, cols]) * (nn(keys, kb_ref[:, cols]) + rows_ref[1:2, cols])
        phi = phi * last
        start = 2 * heads * FEAT + head * VHEAD
        state = tn(phi.astype(bf16), qkv_ref[0, :, start : start + VHEAD])
        out_ref[0, head] = pack_state(state, jnp.sum(phi, axis=0, keepdims=True), flag)


def local_mask(edges, docs):
    length = edges.shape[0]
    later = lax.broadcasted_iota(jnp.int32, (length, length), 0) >= lax.broadcasted_iota(jnp.int32, (length, length), 1)
    return later & (edges[:, 0:1] == docs)


def inside_kernel(heads, qkv_ref, edge_ref, doc_ref, key_ref, num_ref, den_ref):
    lanes = 2 * heads * FEAT
    both = qkv_ref[0, :, :lanes]
    mask = local_mask(edge_ref[0], doc_ref[0, 0:1])
    moved = nn(both, key_ref[...]).astype(bf16)
    dens = []
    for head in range(heads):
        scores = nt(moved[:, head * lanes : (head + 1) * lanes], both)
        weights = jnp.where(mask, 1.0 + scores + 0.5 * scores * scores, 0.0)
        dens.append(jnp.sum(weights, axis=1, keepdims=True))
        start = lanes + head * VHEAD
        num_ref[0, :, head * VHEAD : (head + 1) * VHEAD] = nn(
            weights.astype(bf16), qkv_ref[0, :, start : start + VHEAD]
        )
    den_ref[0] = jnp.concatenate(dens, axis=1)


def block_at(place_ref, states_ref, row, heads, head):
    per = states_ref.shape[1]
    index = row * heads + head
    return states_ref[place_ref[index // per], index % per]


def query_features(both, qa, qb, rows, first):
    left = nn(both, qa) + rows[0:1]
    right = nn(both, qb) + rows[1:2]
    return left, right, left * right * rows[2:3] * first


def attend_kernel(heads, place_ref, qkv_ref, edge_ref, num_ref, den_ref, states_ref, qa_ref, qb_ref, rows_ref, att_ref, rden_ref):
    both = qkv_ref[0, :, : 2 * heads * FEAT]
    first = edge_ref[0][:, 1:2]
    rdens = []
    for head in range(heads):
        cols = slice(head * WIDE, (head + 1) * WIDE)
        _, _, phi = query_features(both, qa_ref[:, cols], qb_ref[:, cols], rows_ref[:, cols], first)
        factor, norm = unpack_state(block_at(place_ref, states_ref, pl.program_id(0), heads, head))
        den = den_ref[0][:, head : head + 1] + jnp.sum(phi * norm, axis=1, keepdims=True)
        rden = 1.0 / den
        out = slice(head * VHEAD, (head + 1) * VHEAD)
        att_ref[0, :, out] = ((num_ref[0, :, out] + nn(phi.astype(bf16), factor)) * rden).astype(bf16)
        rdens.append(rden)
    rden_ref[0] = jnp.concatenate(rdens, axis=1)


def carry_kernel(heads, qkv_ref, edge_ref, ga_ref, att_ref, rden_ref, qa_ref, qb_ref, rows_ref, carry_ref, gnum_ref, gden_ref):
    both = qkv_ref[0, :, : 2 * heads * FEAT]
    edges = edge_ref[0]
    first, flag = edges[:, 1:2], edges[0:1, 3:4]
    gdens = []
    for head in range(heads):
        cols = slice(head * WIDE, (head + 1) * WIDE)
        out = slice(head * VHEAD, (head + 1) * VHEAD)
        _, _, phi = query_features(both, qa_ref[:, cols], qb_ref[:, cols], rows_ref[:, cols], first)
        grad = ga_ref[0, :, out].astype(f32)
        rden = rden_ref[0][:, head : head + 1]
        gnum = (grad * rden).astype(bf16)
        gden = -jnp.sum(grad * att_ref[0, :, out].astype(f32), axis=1, keepdims=True) * rden
        gnum_ref[0, :, out] = gnum
        carry_ref[0, head] = pack_state(
            tn(phi.astype(bf16), gnum), jnp.sum(phi * gden, axis=0, keepdims=True), flag
        )
        gdens.append(gden)
    gden_ref[0] = jnp.concatenate(gdens, axis=1)


def inside_back_kernel(
    heads, place_ref, qkv_ref, edge_ref, doc_ref, gnum_ref, gden_ref, states_ref, key_ref, query_ref, qa_ref, qb_ref,
    rows_ref, gboth_ref, gval_ref,
):
    lanes = 2 * heads * FEAT
    both = qkv_ref[0, :, :lanes]
    edges = edge_ref[0]
    first = edges[:, 1:2]
    mask = local_mask(edges, doc_ref[0, 0:1])
    moved = nn(both, key_ref[...]).astype(bf16)
    back = nn(both, query_ref[...]).astype(bf16)
    total = jnp.zeros((both.shape[0], lanes), f32)
    for head in range(heads):
        cols = slice(head * WIDE, (head + 1) * WIDE)
        out = slice(head * VHEAD, (head + 1) * VHEAD)
        own = slice(head * lanes, (head + 1) * lanes)
        start = lanes + head * VHEAD
        values = qkv_ref[0, :, start : start + VHEAD]
        gnum = gnum_ref[0, :, out]
        gden = gden_ref[0][:, head : head + 1]
        scores = nt(moved[:, own], both)
        weights = jnp.where(mask, 1.0 + scores + 0.5 * scores * scores, 0.0).astype(bf16)
        gval_ref[0, :, out] = tn(weights, gnum)
        gscores = jnp.where(mask, (nt(gnum, values) + gden) * (1.0 + scores), 0.0).astype(bf16)
        total = total + nn(gscores, back[:, own]) + tn(gscores, moved[:, own])
        left, right, _ = query_features(both, qa_ref[:, cols], qb_ref[:, cols], rows_ref[:, cols], first)
        factor, norm = unpack_state(block_at(place_ref, states_ref, pl.program_id(0), heads, head))
        place = lax.broadcasted_iota(jnp.int32, (1, WIDE), 1)
        gphi = jnp.where(place < NORM_ROW, (nt(gnum, factor) + norm * gden) * rows_ref[2:3, cols], 0.0) * first
        total = total + nt((gphi * right).astype(bf16), qa_ref[:, cols]) + nt((gphi * left).astype(bf16), qb_ref[:, cols])
    gboth_ref[0] = total


def finish_back_kernel(
    heads, place_ref, qkv_ref, edge_ref, carry_ref, gboth_ref, gval_ref, ka_ref, kb_ref, rows_ref, out_ref
):
    lanes = 2 * heads * FEAT
    both = qkv_ref[0, :, :lanes]
    last = edge_ref[0][:, 2:3]
    total = gboth_ref[0]
    for head in range(heads):
        cols = slice(head * WIDE, (head + 1) * WIDE)
        start = lanes + head * VHEAD
        values = qkv_ref[0, :, start : start + VHEAD]
        left = nn(both, ka_ref[:, cols]) + rows_ref[0:1, cols]
        right = nn(both, kb_ref[:, cols]) + rows_ref[1:2, cols]
        factor, norm = unpack_state(block_at(place_ref, carry_ref, pl.program_id(0), heads, head))
        phi = (left * right * last).astype(bf16)
        gval = gval_ref[0, :, head * VHEAD : (head + 1) * VHEAD] + nn(phi, factor)
        out_ref[0, :, start : start + VHEAD] = gval.astype(bf16)
        place = lax.broadcasted_iota(jnp.int32, (1, WIDE), 1)
        gphi = jnp.where(place < NORM_ROW, nt(values, factor) + norm, 0.0) * last
        total = total + nt((gphi * right).astype(bf16), ka_ref[:, cols]) + nt((gphi * left).astype(bf16), kb_ref[:, cols])
    out_ref[0, :, :lanes] = total.astype(bf16)


def by_row(kernel, rows, inputs, outputs, place=None, flops=0):
    arrays = [array for array, _ in inputs]
    specs = [row_spec(array) if per_row else whole_spec(array) for array, per_row in inputs]
    shapes = [jax.ShapeDtypeStruct((rows,) + shape, kind) for shape, kind in outputs]
    nbytes = sum(item.size * item.dtype.itemsize for item in arrays + shapes)
    return pl.pallas_call(
        kernel,
        out_shape=shapes,
        grid_spec=pltpu.PrefetchScalarGridSpec(
            num_scalar_prefetch=0 if place is None else 1,
            grid=(rows,),
            in_specs=specs,
            out_specs=[row_spec(shape) for shape in shapes],
        ),
        compiler_params=params(40),
        cost_estimate=cost(flops, nbytes),
    )(*([] if place is None else [place]), *arrays)


def scan_kernel(backward, count, me_ref, *refs):
    pieces, outs, (held, ahead) = refs[:count], refs[count : 2 * count], refs[2 * count :]
    for rel in range(count):
        held[rel] = pieces[rel][...]
    me = me_ref[0]
    for block in range(held.shape[1]):
        run = jnp.zeros(held.shape[2:], f32)
        for step in range(count):
            rel = me ^ (count - 1 - step if backward else step)
            ahead[rel, block] = run.astype(bf16)
            own = held[rel, block].astype(f32)
            run = own + (1.0 - own[FLAG_ROW : FLAG_ROW + 1]) * run
    for rel in range(count):
        outs[rel][...] = ahead[rel]


def scan_begin(states, backward, me, count, earlier=()):
    blocks = states.shape[0] * states.shape[1]
    flat = states.reshape(blocks, TALL, VHEAD)
    if count != 8 or blocks % 8:
        return lax.all_gather(flat, "seq").astype(f32)
    per = blocks // 8
    split = flat.reshape(8, per * TALL, VHEAD)
    pieces = []
    for rel in range(8):
        part = lax.dynamic_index_in_dim(split, me ^ rel, 0, keepdims=False)
        if rel:
            part = send(part, "seq", rel, 8)
        pieces.append(part.reshape(per, TALL, VHEAD))
    pieces[0] = after(pieces[0], *earlier)
    return pl.pallas_call(
        functools.partial(scan_kernel, backward, 8),
        out_shape=[jax.ShapeDtypeStruct((per, TALL, VHEAD), bf16)] * 8,
        in_specs=[pl.BlockSpec(memory_space=pltpu.SMEM)] + [pl.BlockSpec(memory_space=pltpu.VMEM)] * 8,
        out_specs=[pl.BlockSpec(memory_space=pltpu.VMEM)] * 8,
        scratch_shapes=[pltpu.VMEM((8, per, TALL, VHEAD), bf16)] * 2,
        compiler_params=params(),
    )(me.reshape(1), *pieces)


def scan_end(found, backward, me, count):
    if isinstance(found, (list, tuple)):
        back = [found[0]] + [send(found[rel], "seq", rel, 8) for rel in range(1, 8)]
        return jnp.stack(back), me ^ jnp.arange(8, dtype=jnp.int32)
    keep = 1.0 - found[:, :, FLAG_ROW : FLAG_ROW + 1]
    run = jnp.zeros(found.shape[1:], f32)
    for step in range(count):
        at = count - 1 - step if backward else step
        reached = at > me if backward else at < me
        run = jnp.where(reached, found[at] + keep[at] * run, run)
    return run.astype(bf16)[None], jnp.zeros((1,), jnp.int32)


def send(value, axis, mask, count):
    return lax.ppermute(value, axis, [(i, i ^ mask) for i in range(count)])


def gather_rows(shard, count):
    if count != 8:
        return [lax.all_gather(shard, "seq", axis=0, tiled=True)]
    pieces = [shard, send(shard, "seq", 1, 8)]
    for mask in (2, 4, 6):
        piece = send(shard, "seq", mask, 8)
        pieces += [piece, send(piece, "seq", 1, 8)]
    return pieces


def after(value, *earlier):
    return lax.optimization_barrier((value, earlier))[0]


def scatter_begin(whole):
    rows = whole.shape[0] // 8
    part = lambda i: whole[i * rows : (i + 1) * rows]
    pairs = [part(mask).astype(f32) + send(part(mask + 1), "seq", 1, 8).astype(f32) for mask in (2, 4, 6, 0)]
    return [pair.astype(bf16) for pair in pairs[:3]] + [pairs[3]]


def scatter_end(pairs):
    total = pairs[3]
    for pair, mask in zip(pairs, (2, 4, 6)):
        total = total + send(pair, "seq", mask, 8).astype(f32)
    return total


def scatter_rows(whole):
    return lax.psum_scatter(whole, "seq", scatter_dimension=0, tiled=True).astype(f32)


def join_rows(pieces):
    return pieces[0] if len(pieces) == 1 else jnp.concatenate(pieces, axis=0)


CORE, ACROSS = 1, 2


def scatter_head(near_half, far_half, beside=None):
    rows = near_half.shape[0] // 2
    core = send(far_half[rows:], "head", CORE, 4)
    summed = (far_half[:rows].astype(f32) + core.astype(f32)).astype(bf16)
    across = send(summed, "head", ACROSS, 4)
    near = near_half[:rows].astype(f32) + send(near_half[rows:], "head", CORE, 4).astype(f32)
    if beside is None:
        return near + across.astype(f32)
    found = beside(summed)
    return near + after(across, found).astype(f32), found


def gather_head(own, between=lambda near: ()):
    near = join_rows([own, send(own, "head", CORE, 4)])
    across = after(send(own, "head", ACROSS, 4), *between(near))
    return near, join_rows([across, send(across, "head", CORE, 4)])


def swap_quarters(array, me):
    split = array.reshape((4, array.shape[0] // 4) + array.shape[1:])
    return join_rows([lax.dynamic_index_in_dim(split, me ^ mask, 0, keepdims=False) for mask in range(4)])


def swap_blocks(array, order):
    split = array.reshape((BLOCKS, array.shape[0] // BLOCKS) + array.shape[1:])
    return join_rows([lax.dynamic_index_in_dim(split, order[i], 0, keepdims=False) for i in range(BLOCKS)])


def move_kernel(split, rows_ref, cols_ref, in_ref, out_ref):
    width = in_ref.shape[1] // BLOCKS
    for block in range(BLOCKS):
        start = pl.multiple_of(cols_ref[block] * width, 128)
        out_ref[:, block * width : (block + 1) * width] = in_ref[:, pl.ds(start, width)].astype(out_ref.dtype)


def move_blocks(array, row_blocks, col_blocks, out_type, quarter):
    width = array.shape[1]
    split = 2 if quarter % 32 == 0 else 1
    tile = quarter // split
    count = row_blocks.shape[0]
    shape = jax.ShapeDtypeStruct((count * quarter, width), out_type)
    return pl.pallas_call(
        functools.partial(move_kernel, split),
        out_shape=shape,
        grid_spec=pltpu.PrefetchScalarGridSpec(
            num_scalar_prefetch=2,
            grid=(count, split),
            in_specs=[pl.BlockSpec((tile, width), lambda i, j, rows, cols: (rows[i] * split + j, 0))],
            out_specs=pl.BlockSpec((tile, width), lambda i, j, rows, cols: (i * split + j, 0)),
        ),
        compiler_params=params(),
        cost_estimate=cost(0, shape.size * (array.dtype.itemsize + shape.dtype.itemsize)),
    )(row_blocks, col_blocks, array)


def unit_kernel(cols_ref, in_ref, out_ref):
    values = in_ref[...].astype(f32)
    rstd = lax.rsqrt(jnp.mean(values * values, axis=1, keepdims=True) + EPSILON)
    width = in_ref.shape[1] // BLOCKS
    for block in range(BLOCKS):
        start = pl.multiple_of(cols_ref[block] * width, 128)
        out_ref[:, block * width : (block + 1) * width] = (in_ref[:, pl.ds(start, width)].astype(f32) * rstd).astype(bf16)


def unit_rows(array, col_blocks, tile):
    rows, width = array.shape
    return pl.pallas_call(
        unit_kernel,
        out_shape=jax.ShapeDtypeStruct((rows, width), bf16),
        grid_spec=pltpu.PrefetchScalarGridSpec(
            num_scalar_prefetch=1,
            grid=(rows // tile,),
            in_specs=[pl.BlockSpec((tile, width), lambda i, cols: (i, 0))],
            out_specs=pl.BlockSpec((tile, width), lambda i, cols: (i, 0)),
        ),
        compiler_params=params(),
        cost_estimate=cost(0, 4 * rows * width),
    )(col_blocks, array)


def ffn_kernel(n_gate, step, order_ref, unit_ref, dy_ref, *refs):
    pieces, down_hbm = refs[:n_gate], refs[n_gate]
    mixed_ref, ggate_ref, gup_ref, gunit_ref, out_ref, gate_ref, up_ref, down_ref, sems = refs[n_gate + 1 :]
    width, hidden = gate_ref.shape
    copies = []
    rows = width // n_gate
    for place, held in ((0, gate_ref), (hidden, up_ref)):
        for i, piece in enumerate(pieces):
            copies.append((piece.at[:, pl.ds(place, hidden)], held.at[pl.ds(i * rows, rows)]))
    rows = width // BLOCKS
    for i in range(BLOCKS):
        start = pl.multiple_of(order_ref[i] * rows, rows)
        source = down_hbm.at[pl.ds(start, rows), pl.ds(down_hbm.shape[1] - hidden, hidden)]
        copies.append((source, down_ref.at[pl.ds(i * rows, rows)]))
    copies = [pltpu.make_async_copy(*ends, sems.at[i]) for i, ends in enumerate(copies)]

    @pl.when(pl.program_id(0) == 0)
    def _():
        for copy in copies:
            copy.start()
        for copy in copies:
            copy.wait()

    unit, dy = unit_ref[...], dy_ref[...]
    for start in range(0, hidden, step):
        cols = slice(start, min(start + step, hidden))
        gate = nn(unit, gate_ref[:, cols])
        up = nn(unit, up_ref[:, cols])
        gmixed = nn(dy, down_ref[:, cols])
        sig = jax.nn.sigmoid(gate)
        silu = gate * sig
        mixed_ref[:, cols] = (silu * up).astype(bf16)
        ggate_ref[:, cols] = (gmixed * up * (sig * (1.0 + gate * (1.0 - sig)))).astype(bf16)
        gup_ref[:, cols] = (gmixed * silu).astype(bf16)
    ggate, gup, mixed = ggate_ref[...], gup_ref[...], mixed_ref[...]
    for start in range(0, width, 512):
        cols = slice(start, start + 512)
        gunit_ref[:, cols] = (nt(ggate, gate_ref[cols]) + nt(gup, up_ref[cols])).astype(bf16)
        out_ref[:, cols] = nt(mixed, down_ref[cols]).astype(bf16)


def feed_forward(unit, dy, half, pieces, turned, order, tile):
    tokens, width = unit.shape
    hidden = pieces[0].shape[1] // 2
    steps = tokens // tile
    anywhere = pl.BlockSpec(memory_space=pl.ANY)
    line = lambda cols, first=0: pl.BlockSpec((tile, cols), lambda i, order: (i + first, 0))
    out_cols = [hidden] * 3 + [width] * 2
    return pl.pallas_call(
        functools.partial(ffn_kernel, len(pieces), 256),
        out_shape=[jax.ShapeDtypeStruct((tokens, cols), bf16) for cols in out_cols],
        grid_spec=pltpu.PrefetchScalarGridSpec(
            num_scalar_prefetch=1,
            grid=(steps,),
            in_specs=[line(width), line(width, half * steps)] + [anywhere] * (len(pieces) + 1),
            out_specs=[line(cols) for cols in out_cols],
            scratch_shapes=[pltpu.VMEM((width, hidden), bf16)] * 3
            + [pltpu.SemaphoreType.DMA((2 * len(pieces) + BLOCKS,))],
        ),
        compiler_params=params(58),
        cost_estimate=cost(12 * tokens * width * hidden, 2 * (4 * tokens * width + 3 * (tokens + width) * hidden)),
    )(order, unit, dy, *pieces, turned)


def weight_kernel(n_parts, order_ref, *refs):
    lefts, rights, out = refs[:n_parts], refs[n_parts:-1], refs[-1]
    turned = [left[...].T for left in lefts]
    start = 0
    for place in range(0, len(rights), n_parts):
        total = nn(turned[0], rights[place][...])
        for part in range(1, n_parts):
            total = total + nn(turned[part], rights[place + part][...])
        out[:, start : start + total.shape[1]] = total.astype(bf16)
        start += total.shape[1]


def weight_grads(lefts, rights, order):
    width = lefts[0].shape[1]
    rows = width // BLOCKS
    flat = [part for right in rights for part in right]
    cols = sum(right[0].shape[1] for right in rights)
    tokens = sum(left.shape[0] for left in lefts)
    return pl.pallas_call(
        functools.partial(weight_kernel, len(lefts)),
        out_shape=jax.ShapeDtypeStruct((width, cols), bf16),
        grid_spec=pltpu.PrefetchScalarGridSpec(
            num_scalar_prefetch=1,
            grid=(BLOCKS,),
            in_specs=[pl.BlockSpec((left.shape[0], rows), lambda i, order: (0, i)) for left in lefts]
            + [pl.BlockSpec(part.shape, lambda i, order: (0, 0), pipeline_mode=pl.Buffered(1)) for part in flat],
            out_specs=pl.BlockSpec((rows, cols), lambda i, order: (order[i], 0)),
        ),
        compiler_params=params(48),
        cost_estimate=cost(2 * tokens * width * cols, 2 * (tokens + width) * (width + cols)),
    )(order, *lefts, *flat)


def per_device(
    n_seq,
    n_head,
    tokens,
    doc_reset,
    gain_attn,
    gain_ffn,
    query_weight,
    key_weight,
    value_weight,
    out_weight,
    gate_weight,
    up_weight,
    down_weight,
    grad_out,
):
    rows, length, width = tokens.shape
    heads = query_weight.shape[1] // FEAT
    count = rows * length
    quarter = count // 4
    half = 2 * quarter
    me = lax.axis_index("seq").astype(jnp.int32)
    head_me = lax.axis_index("head").astype(jnp.int32)
    order = jnp.arange(BLOCKS, dtype=jnp.int32)
    if n_seq == 8:
        order = me ^ order
    quarters = head_me ^ jnp.arange(4, dtype=jnp.int32)

    gain_one = gain_attn.astype(f32)[:, None]
    gain_two = gain_ffn.astype(f32)[:, None]
    scaled = lambda weight, gain: (weight.astype(f32) * gain).astype(bf16)
    qkv_own = jnp.concatenate([query_weight, key_weight, value_weight], axis=1)
    qkv_w = gather_rows(scaled(qkv_own, gain_one), n_seq)
    pair_own = jnp.concatenate([scaled(gate_weight, gain_two), scaled(up_weight, gain_two)], axis=1)
    if n_seq == 8:
        pair_own = after(pair_own, qkv_w[2], qkv_w[4], qkv_w[6])
        pair_one = send(pair_own, "seq", 2, 8)
        pair_two = send(after(pair_own, pair_one), "seq", 4, 8)
        pair_three = send(after(pair_own, pair_two), "seq", 6, 8)
        pair_w = []
        for piece in (pair_own, pair_one, pair_two, pair_three):
            pair_w += [piece, send(piece, "seq", 1, 8)]
        stages = [(pair_one,), (pair_two, pair_w[1]), (pair_w[3], pair_three)]
    else:
        pair_w = gather_rows(pair_own, n_seq)
        stages = [(), (), ()]
    qkv_w = join_rows(qkv_w)
    turned = jnp.concatenate([out_weight.T, down_weight.T], axis=1)
    turned = lax.all_gather(turned, "seq", axis=0, tiled=True)
    out_w = swap_blocks(turned[:, : out_weight.shape[0]], order)

    flat = tokens.reshape(count, width)
    unit_one = unit_rows(flat, order, quarter // 2)
    x_own = move_blocks(flat, quarters[:1], order, f32, quarter)
    dy = move_blocks(grad_out.reshape(count, width), quarters, order, bf16, quarter)
    rstd_one = lax.rsqrt(jnp.mean(x_own * x_own, axis=1, keepdims=True) + EPSILON)

    docs = jnp.cumsum(doc_reset, axis=1)
    final = docs[:, -1:]
    flag = jnp.broadcast_to(final > 0, docs.shape)
    edges = jnp.stack([docs, docs == 0, docs == final, flag] + [jnp.zeros_like(docs)] * 4, axis=2).astype(f32)
    doc_rows = jnp.broadcast_to(docs[:, None, :], (rows, 8, length)).astype(f32)
    tables, feat_rows, to_key, to_query = feature_tables(heads)

    lanes = 2 * heads * FEAT
    values = heads * VHEAD
    unit_flops = 2 * rows * heads * length * WIDE * VHEAD
    qkv = nn(unit_one, qkv_w).astype(bf16).reshape(rows, length, lanes + values)
    (states,) = by_row(
        functools.partial(state_kernel, heads),
        rows,
        [(qkv, True), (edges, True), (tables["ka"], False), (tables["kb"], False), (feat_rows, False)],
        [((heads, TALL, VHEAD), bf16)],
        flops=3 * unit_flops,
    )
    numerator, denominator = by_row(
        functools.partial(inside_kernel, heads),
        rows,
        [(qkv, True), (edges, True), (doc_rows, True), (to_key, False)],
        [((length, values), f32), ((length, heads), f32)],
        flops=3 * unit_flops,
    )
    state_in, place = scan_end(scan_begin(states, False, me, n_seq, stages[0]), False, me, n_seq)
    query_tables = [(tables["qa"], False), (tables["qb"], False), (feat_rows, False)]
    key_tables = [(tables["ka"], False), (tables["kb"], False), (feat_rows, False)]
    attended, rden = by_row(
        functools.partial(attend_kernel, heads),
        rows,
        [(qkv, True), (edges, True), (numerator, True), (denominator, True), (state_in, False)] + query_tables,
        [((length, values), bf16), ((length, heads), f32)],
        place=place,
        flops=3 * unit_flops,
    )
    attended_own = after(swap_quarters(attended.reshape(count, values), head_me), *stages[1])
    far = nt(attended_own[half:], out_w).astype(bf16)
    near = nt(attended_own[:half], out_w).astype(bf16)
    hidden = x_own + scatter_head(near, far)
    rstd_two = lax.rsqrt(jnp.mean(hidden * hidden, axis=1, keepdims=True) + EPSILON)
    unit_two_own = hidden * rstd_two
    first_half = []

    def near_rows(unit):
        first_half.extend(feed_forward(unit, dy, 0, pair_w, turned, order, quarter))
        return first_half

    unit_two = gather_head(after(unit_two_own.astype(bf16), *stages[2]), near_rows)
    second_half = feed_forward(unit_two[1], dy, 1, pair_w, turned, order, quarter)
    mixed, ggate, gup, gunit, branch = zip(first_half, second_half)
    parts = [dy[:half], dy[half:]]

    def ffn_weights(sent):
        left = [after(unit_two[0], sent), unit_two[1]]
        first = weight_grads(left, [ggate, gup], order)
        left = [after(parts[0], first), parts[1]]
        return first, weight_grads(left, [mixed], order)

    scaled_two, found = scatter_head(*gunit, beside=ffn_weights)
    grad_pair, grad_down = [scatter_rows(item) for item in found]

    dy_own = dy[:quarter].astype(f32)
    grad_hidden = dy_own + rstd_two * (
        scaled_two - unit_two_own * jnp.mean(scaled_two * unit_two_own, axis=1, keepdims=True)
    )
    grad_branch = gather_head(grad_hidden.astype(bf16))


    grad_att = join_rows([nn(item, out_w).astype(bf16) for item in grad_branch])
    grad_att = swap_quarters(grad_att, head_me).reshape(rows, length, values)
    carry, gnum, gden = by_row(
        functools.partial(carry_kernel, heads),
        rows,
        [(qkv, True), (edges, True), (grad_att, True), (attended, True), (rden, True)] + query_tables,
        [((heads, TALL, VHEAD), bf16), ((length, values), bf16), ((length, heads), f32)],
        flops=3 * unit_flops,
    )
    gboth, gval = by_row(
        functools.partial(inside_back_kernel, heads),
        rows,
        [(qkv, True), (edges, True), (doc_rows, True), (gnum, True), (gden, True), (state_in, False)]
        + [(to_key, False), (to_query, False)]
        + query_tables,
        [((length, lanes), f32), ((length, values), f32)],
        place=place,
        flops=11 * unit_flops,
    )
    parts = [attended_own[:half], attended_own[half:]]
    grad_out_w = weight_grads(grad_branch, [parts], order ^ me if n_seq == 8 else order)
    out_pairs = scatter_begin(grad_out_w) if n_seq == 8 else [grad_out_w]
    found = scan_begin(carry, True, me, n_seq)
    block_own, _ = scatter_head(branch[0], after(branch[1], *grad_branch), beside=lambda _: found)
    block_own = (hidden + block_own).astype(bf16)
    carry_in, place_back = scan_end(found, True, me, n_seq)
    carry_in = after(carry_in, block_own)
    block_all = join_rows(gather_head(block_own))
    (gqkv,) = by_row(
        functools.partial(finish_back_kernel, heads),
        rows,
        [(qkv, True), (edges, True), (carry_in, False), (gboth, True), (gval, True)] + key_tables,
        [((length, lanes + values), bf16)],
        place=place_back,
        flops=6 * unit_flops,
    )
    gqkv = gqkv.reshape(count, lanes + values)
    gqkv_own = after(swap_quarters(gqkv, head_me), block_all, *out_pairs)
    grad_out_w = scatter_end(out_pairs) if n_seq == 8 else scatter_rows(out_pairs[0])
    far = nt(gqkv_own[half:], qkv_w).astype(bf16)
    near = nt(gqkv_own[:half], qkv_w).astype(bf16)
    scaled_one = scatter_head(near, far)
    if n_seq == 8:
        qkv_pairs = scatter_begin(weight_grads([unit_one], [[gqkv]], order ^ me))
        grad_qkv = scatter_end(qkv_pairs)
    else:
        qkv_pairs = []
        grad_qkv = scatter_rows(weight_grads([unit_one], [[gqkv]], order))
    unit_one_own = x_own * rstd_one
    grad_x = grad_hidden + rstd_one * (
        scaled_one - unit_one_own * jnp.mean(scaled_one * unit_one_own, axis=1, keepdims=True)
    )
    grad_x_all = join_rows(gather_head(after(grad_x.astype(bf16), grad_out_w, grad_pair, *qkv_pairs)))

    back = lambda value, kind: move_blocks(value, quarters, order, kind, quarter).reshape(rows, length, width)
    hidden_units = gate_weight.shape[1]
    grad_gate, grad_up = grad_pair[:, :hidden_units], grad_pair[:, hidden_units:]
    gain_sums = jnp.stack(
        [
            jnp.sum(qkv_own.astype(f32) * grad_qkv, axis=1),
            jnp.sum(gate_weight.astype(f32) * grad_gate + up_weight.astype(f32) * grad_up, axis=1),
        ]
    )
    gain_sums = gain_sums + send(gain_sums, "head", CORE, 4)
    gain_sums = gain_sums + send(gain_sums, "head", ACROSS, 4)
    grad_qkv = grad_qkv * gain_one
    narrow = heads * FEAT
    return (
        back(block_all, bf16),
        back(grad_x_all, f32),
        gain_sums[0],
        gain_sums[1],
        grad_qkv[:, :narrow],
        grad_qkv[:, narrow:lanes],
        grad_qkv[:, lanes:],
        grad_out_w.T,
        grad_gate * gain_two,
        grad_up * gain_two,
        grad_down.T,
    )


def solution(mesh):
    placed = (
        P(None, "seq", None),
        P(None, "seq"),
        P("seq"),
        P("seq"),
        P("seq", "head"),
        P("seq", "head"),
        P("seq", "head"),
        P("head", "seq"),
        P("seq", "head"),
        P("seq", "head"),
        P("head", "seq"),
        P(None, "seq", None),
    )
    return jax.shard_map(
        functools.partial(per_device, mesh.shape["seq"], mesh.shape["head"]),
        mesh=mesh,
        in_specs=placed,
        out_specs=(P(None, "seq", None), P(None, "seq", None)) + placed[2:11],
        check_vma=False,
    )
```

```python
import functools

import jax
import jax.numpy as jnp
import numpy as np
from jax import lax
from jax.experimental import pallas as pl
from jax.experimental.pallas import tpu as pltpu
from jax.sharding import PartitionSpec as P

FEAT = 16
VHEAD = 128
EPSILON = 1e-06
PAIRS = [(a, b) for a in range(FEAT + 1) for b in range(a, FEAT + 1)]
WIDE = 256
TALL = 160
NORM_ROW = len(PAIRS)
FLAG_ROW = NORM_ROW + 2
BLOCKS = 8
bf16, f32 = jnp.bfloat16, jnp.float32


def feature_tables(heads):
    lanes = 2 * heads * FEAT
    tables = {name: np.zeros((lanes, heads * WIDE), np.float32) for name in ("qa", "qb", "ka", "kb")}
    rows = np.zeros((8, heads * WIDE), np.float32)
    to_key = np.zeros((lanes, heads * lanes), np.float32)
    to_query = np.zeros((lanes, heads * lanes), np.float32)
    for head in range(heads):
        for place, (a, b) in enumerate(PAIRS):
            column = head * WIDE + place
            for name, entry, row in (("a", a, 0), ("b", b, 1)):
                if entry == 0:
                    rows[row, column] = 1.0
                else:
                    lane = head * FEAT + entry - 1
                    tables["q" + name][lane, column] = 1.0
                    tables["k" + name][heads * FEAT + lane, column] = 1.0
            rows[2, column] = 1.0 if b == 0 else 0.25 if a == 0 else 1 / 32 if a == b else 1 / 16
        for feat in range(FEAT):
            lane = head * FEAT + feat
            to_key[lane, head * lanes + heads * FEAT + lane] = 0.25
            to_query[heads * FEAT + lane, head * lanes + lane] = 0.25
    tables = {name: jnp.asarray(item, bf16) for name, item in tables.items()}
    return tables, jnp.asarray(rows), jnp.asarray(to_key, bf16), jnp.asarray(to_query, bf16)


def nn(left, right):
    return lax.dot_general(left, right, (((1,), (0,)), ((), ())), preferred_element_type=f32)


def nt(left, right):
    return lax.dot_general(left, right, (((1,), (1,)), ((), ())), preferred_element_type=f32)


def tn(left, right):
    return lax.dot_general(left, right, (((0,), (0,)), ((), ())), preferred_element_type=f32)


def params(mib=32):
    return pltpu.CompilerParams(vmem_limit_bytes=mib << 20)


def cost(flops, nbytes):
    return pl.CostEstimate(flops=int(flops) // 32, bytes_accessed=int(nbytes) // 32, transcendentals=0)


def whole_spec(array):
    zeros = (0,) * array.ndim
    return pl.BlockSpec(array.shape, lambda *_: zeros)


def row_spec(array):
    zeros = (0,) * (array.ndim - 1)
    return pl.BlockSpec((1,) + array.shape[1:], lambda row, *_: (row,) + zeros)


def pack_state(state, norm_row, flag):
    place = lax.broadcasted_iota(jnp.int32, (TALL, VHEAD), 0)
    block = state[:TALL]
    block = jnp.where(place == NORM_ROW, norm_row[:, :VHEAD], block)
    block = jnp.where(place == NORM_ROW + 1, norm_row[:, VHEAD:], block)
    return jnp.where(place == FLAG_ROW, flag, block).astype(bf16)


def unpack_state(block):
    tail = block[TALL - 16 :].astype(f32)
    base = TALL - 16
    low = tail[NORM_ROW - base : NORM_ROW - base + 1]
    high = tail[NORM_ROW + 1 - base : NORM_ROW + 2 - base]
    full = jnp.concatenate([block, jnp.zeros((WIDE - TALL, VHEAD), block.dtype)], axis=0)
    return full, jnp.concatenate([low, high], axis=1)


def state_kernel(heads, qkv_ref, edge_ref, ka_ref, kb_ref, rows_ref, out_ref):
    keys = qkv_ref[0, :, : 2 * heads * FEAT]
    edges = edge_ref[0]
    last, flag = edges[:, 2:3], edges[0:1, 3:4]
    for head in range(heads):
        cols = slice(head * WIDE, (head + 1) * WIDE)
        phi = (nn(keys, ka_ref[:, cols]) + rows_ref[0:1, cols]) * (nn(keys, kb_ref[:, cols]) + rows_ref[1:2, cols])
        phi = phi * last
        start = 2 * heads * FEAT + head * VHEAD
        state = tn(phi.astype(bf16), qkv_ref[0, :, start : start + VHEAD])
        out_ref[0, head] = pack_state(state, jnp.sum(phi, axis=0, keepdims=True), flag)


def local_mask(edges, docs):
    length = edges.shape[0]
    later = lax.broadcasted_iota(jnp.int32, (length, length), 0) >= lax.broadcasted_iota(jnp.int32, (length, length), 1)
    return later & (edges[:, 0:1] == docs)


def inside_kernel(heads, qkv_ref, edge_ref, doc_ref, key_ref, num_ref, den_ref):
    lanes = 2 * heads * FEAT
    both = qkv_ref[0, :, :lanes]
    mask = local_mask(edge_ref[0], doc_ref[0, 0:1])
    moved = nn(both, key_ref[...]).astype(bf16)
    dens = []
    for head in range(heads):
        scores = nt(moved[:, head * lanes : (head + 1) * lanes], both)
        weights = jnp.where(mask, 1.0 + scores + 0.5 * scores * scores, 0.0)
        dens.append(jnp.sum(weights, axis=1, keepdims=True))
        start = lanes + head * VHEAD
        num_ref[0, :, head * VHEAD : (head + 1) * VHEAD] = nn(
            weights.astype(bf16), qkv_ref[0, :, start : start + VHEAD]
        )
    den_ref[0] = jnp.concatenate(dens, axis=1)


def block_at(place_ref, states_ref, row, heads, head):
    per = states_ref.shape[1]
    index = row * heads + head
    return states_ref[place_ref[index // per], index % per]


def query_features(both, qa, qb, rows, first):
    left = nn(both, qa) + rows[0:1]
    right = nn(both, qb) + rows[1:2]
    return left, right, left * right * rows[2:3] * first


def attend_kernel(heads, place_ref, qkv_ref, edge_ref, num_ref, den_ref, states_ref, qa_ref, qb_ref, rows_ref, att_ref, rden_ref):
    both = qkv_ref[0, :, : 2 * heads * FEAT]
    first = edge_ref[0][:, 1:2]
    rdens = []
    for head in range(heads):
        cols = slice(head * WIDE, (head + 1) * WIDE)
        _, _, phi = query_features(both, qa_ref[:, cols], qb_ref[:, cols], rows_ref[:, cols], first)
        factor, norm = unpack_state(block_at(place_ref, states_ref, pl.program_id(0), heads, head))
        den = den_ref[0][:, head : head + 1] + jnp.sum(phi * norm, axis=1, keepdims=True)
        rden = 1.0 / den
        out = slice(head * VHEAD, (head + 1) * VHEAD)
        att_ref[0, :, out] = ((num_ref[0, :, out] + nn(phi.astype(bf16), factor)) * rden).astype(bf16)
        rdens.append(rden)
    rden_ref[0] = jnp.concatenate(rdens, axis=1)


def carry_kernel(heads, qkv_ref, edge_ref, ga_ref, att_ref, rden_ref, qa_ref, qb_ref, rows_ref, carry_ref, gnum_ref, gden_ref):
    both = qkv_ref[0, :, : 2 * heads * FEAT]
    edges = edge_ref[0]
    first, flag = edges[:, 1:2], edges[0:1, 3:4]
    gdens = []
    for head in range(heads):
        cols = slice(head * WIDE, (head + 1) * WIDE)
        out = slice(head * VHEAD, (head + 1) * VHEAD)
        _, _, phi = query_features(both, qa_ref[:, cols], qb_ref[:, cols], rows_ref[:, cols], first)
        grad = ga_ref[0, :, out].astype(f32)
        rden = rden_ref[0][:, head : head + 1]
        gnum = (grad * rden).astype(bf16)
        gden = -jnp.sum(grad * att_ref[0, :, out].astype(f32), axis=1, keepdims=True) * rden
        gnum_ref[0, :, out] = gnum
        carry_ref[0, head] = pack_state(
            tn(phi.astype(bf16), gnum), jnp.sum(phi * gden, axis=0, keepdims=True), flag
        )
        gdens.append(gden)
    gden_ref[0] = jnp.concatenate(gdens, axis=1)


def inside_back_kernel(
    heads, place_ref, qkv_ref, edge_ref, doc_ref, gnum_ref, gden_ref, states_ref, key_ref, query_ref, qa_ref, qb_ref,
    rows_ref, gboth_ref, gval_ref,
):
    lanes = 2 * heads * FEAT
    both = qkv_ref[0, :, :lanes]
    edges = edge_ref[0]
    first = edges[:, 1:2]
    mask = local_mask(edges, doc_ref[0, 0:1])
    moved = nn(both, key_ref[...]).astype(bf16)
    back = nn(both, query_ref[...]).astype(bf16)
    total = jnp.zeros((both.shape[0], lanes), f32)
    for head in range(heads):
        cols = slice(head * WIDE, (head + 1) * WIDE)
        out = slice(head * VHEAD, (head + 1) * VHEAD)
        own = slice(head * lanes, (head + 1) * lanes)
        start = lanes + head * VHEAD
        values = qkv_ref[0, :, start : start + VHEAD]
        gnum = gnum_ref[0, :, out]
        gden = gden_ref[0][:, head : head + 1]
        scores = nt(moved[:, own], both)
        weights = jnp.where(mask, 1.0 + scores + 0.5 * scores * scores, 0.0).astype(bf16)
        gval_ref[0, :, out] = tn(weights, gnum)
        gscores = jnp.where(mask, (nt(gnum, values) + gden) * (1.0 + scores), 0.0).astype(bf16)
        total = total + nn(gscores, back[:, own]) + tn(gscores, moved[:, own])
        left, right, _ = query_features(both, qa_ref[:, cols], qb_ref[:, cols], rows_ref[:, cols], first)
        factor, norm = unpack_state(block_at(place_ref, states_ref, pl.program_id(0), heads, head))
        place = lax.broadcasted_iota(jnp.int32, (1, WIDE), 1)
        gphi = jnp.where(place < NORM_ROW, (nt(gnum, factor) + norm * gden) * rows_ref[2:3, cols], 0.0) * first
        total = total + nt((gphi * right).astype(bf16), qa_ref[:, cols]) + nt((gphi * left).astype(bf16), qb_ref[:, cols])
    gboth_ref[0] = total


def finish_back_kernel(
    heads, place_ref, qkv_ref, edge_ref, carry_ref, gboth_ref, gval_ref, ka_ref, kb_ref, rows_ref, out_ref
):
    lanes = 2 * heads * FEAT
    both = qkv_ref[0, :, :lanes]
    last = edge_ref[0][:, 2:3]
    total = gboth_ref[0]
    for head in range(heads):
        cols = slice(head * WIDE, (head + 1) * WIDE)
        start = lanes + head * VHEAD
        values = qkv_ref[0, :, start : start + VHEAD]
        left = nn(both, ka_ref[:, cols]) + rows_ref[0:1, cols]
        right = nn(both, kb_ref[:, cols]) + rows_ref[1:2, cols]
        factor, norm = unpack_state(block_at(place_ref, carry_ref, pl.program_id(0), heads, head))
        phi = (left * right * last).astype(bf16)
        gval = gval_ref[0, :, head * VHEAD : (head + 1) * VHEAD] + nn(phi, factor)
        out_ref[0, :, start : start + VHEAD] = gval.astype(bf16)
        place = lax.broadcasted_iota(jnp.int32, (1, WIDE), 1)
        gphi = jnp.where(place < NORM_ROW, nt(values, factor) + norm, 0.0) * last
        total = total + nt((gphi * right).astype(bf16), ka_ref[:, cols]) + nt((gphi * left).astype(bf16), kb_ref[:, cols])
    out_ref[0, :, :lanes] = total.astype(bf16)


def by_row(kernel, rows, inputs, outputs, place=None, flops=0):
    arrays = [array for array, _ in inputs]
    specs = [row_spec(array) if per_row else whole_spec(array) for array, per_row in inputs]
    shapes = [jax.ShapeDtypeStruct((rows,) + shape, kind) for shape, kind in outputs]
    nbytes = sum(item.size * item.dtype.itemsize for item in arrays + shapes)
    return pl.pallas_call(
        kernel,
        out_shape=shapes,
        grid_spec=pltpu.PrefetchScalarGridSpec(
            num_scalar_prefetch=0 if place is None else 1,
            grid=(rows,),
            in_specs=specs,
            out_specs=[row_spec(shape) for shape in shapes],
        ),
        compiler_params=params(40),
        cost_estimate=cost(flops, nbytes),
    )(*([] if place is None else [place]), *arrays)


def scan_kernel(backward, count, me_ref, *refs):
    pieces, outs, (held, ahead) = refs[:count], refs[count : 2 * count], refs[2 * count :]
    for rel in range(count):
        held[rel] = pieces[rel][...]
    me = me_ref[0]
    for block in range(held.shape[1]):
        run = jnp.zeros(held.shape[2:], f32)
        for step in range(count):
            rel = me ^ (count - 1 - step if backward else step)
            ahead[rel, block] = run.astype(bf16)
            own = held[rel, block].astype(f32)
            run = own + (1.0 - own[FLAG_ROW : FLAG_ROW + 1]) * run
    for rel in range(count):
        outs[rel][...] = ahead[rel]


def scan_begin(states, backward, me, count, earlier=()):
    blocks = states.shape[0] * states.shape[1]
    flat = states.reshape(blocks, TALL, VHEAD)
    if count != 8 or blocks % 8:
        return lax.all_gather(flat, "seq").astype(f32)
    per = blocks // 8
    split = flat.reshape(8, per * TALL, VHEAD)
    pieces = []
    for rel in range(8):
        part = lax.dynamic_index_in_dim(split, me ^ rel, 0, keepdims=False)
        if rel:
            part = send(part, "seq", rel, 8)
        pieces.append(part.reshape(per, TALL, VHEAD))
    pieces[0] = after(pieces[0], *earlier)
    return pl.pallas_call(
        functools.partial(scan_kernel, backward, 8),
        out_shape=[jax.ShapeDtypeStruct((per, TALL, VHEAD), bf16)] * 8,
        in_specs=[pl.BlockSpec(memory_space=pltpu.SMEM)] + [pl.BlockSpec(memory_space=pltpu.VMEM)] * 8,
        out_specs=[pl.BlockSpec(memory_space=pltpu.VMEM)] * 8,
        scratch_shapes=[pltpu.VMEM((8, per, TALL, VHEAD), bf16)] * 2,
        compiler_params=params(),
    )(me.reshape(1), *pieces)


def scan_end(found, backward, me, count):
    if isinstance(found, (list, tuple)):
        back = [found[0]] + [send(found[rel], "seq", rel, 8) for rel in range(1, 8)]
        return jnp.stack(back), me ^ jnp.arange(8, dtype=jnp.int32)
    keep = 1.0 - found[:, :, FLAG_ROW : FLAG_ROW + 1]
    run = jnp.zeros(found.shape[1:], f32)
    for step in range(count):
        at = count - 1 - step if backward else step
        reached = at > me if backward else at < me
        run = jnp.where(reached, found[at] + keep[at] * run, run)
    return run.astype(bf16)[None], jnp.zeros((1,), jnp.int32)


def send(value, axis, mask, count):
    return lax.ppermute(value, axis, [(i, i ^ mask) for i in range(count)])


def gather_rows(shard, count):
    if count != 8:
        return [lax.all_gather(shard, "seq", axis=0, tiled=True)]
    pieces = [shard, send(shard, "seq", 1, 8)]
    for mask in (2, 4, 6):
        piece = send(shard, "seq", mask, 8)
        pieces += [piece, send(piece, "seq", 1, 8)]
    return pieces


def after(value, *earlier):
    return lax.optimization_barrier((value, earlier))[0]


def split_order(order, n_seq):
    return jnp.array([0, 4, 1, 5, 2, 6, 3, 7], jnp.int32) if n_seq == 8 else order


def scatter_begin(whole, n_seq):
    if n_seq != 8:
        return (lax.psum_scatter(whole, "seq", scatter_dimension=0, tiled=True).astype(f32),)
    rows = whole.shape[0] // 8
    other = send(whole[4 * rows :], "seq", 1, 8)
    pairs = [
        whole[i * rows : (i + 1) * rows].astype(f32) + other[i * rows : (i + 1) * rows].astype(f32) for i in range(4)
    ]
    return (pairs[0],) + tuple(pair.astype(bf16) for pair in pairs[1:])


def scatter_sends(pairs):
    return [send(pair, "seq", 2 * place + 2, 8) for place, pair in enumerate(pairs[1:])]


def scatter_end(pairs, terms):
    total = pairs[0]
    for term in terms:
        total = total + term.astype(f32)
    return total


def join_rows(pieces):
    return pieces[0] if len(pieces) == 1 else jnp.concatenate(pieces, axis=0)


CORE, ACROSS = 1, 2


def scatter_head(quarters, beside=None):
    core = send(quarters[3], "head", CORE, 4)
    summed = (quarters[2].astype(f32) + core.astype(f32)).astype(bf16)
    across = send(summed, "head", ACROSS, 4)
    near = send(quarters[1], "head", CORE, 4)
    found = () if beside is None else beside(summed)
    return (quarters[0], near, after(across, found)), found


def gather_head(own, between=lambda near: ()):
    near = [own, send(own, "head", CORE, 4)]
    across = after(send(own, "head", ACROSS, 4), *between(near))
    return near + [across, send(across, "head", CORE, 4)]


def move_columns(cols_ref, in_ref, out_ref):
    width = in_ref.shape[1] // BLOCKS
    for block in range(BLOCKS):
        start = pl.multiple_of(cols_ref[block] * width, 128)
        out_ref[:, block * width : (block + 1) * width] = in_ref[:, pl.ds(start, width)].astype(out_ref.dtype)


def move_kernel(rows_ref, cols_ref, in_ref, out_ref):
    move_columns(cols_ref, in_ref, out_ref)


def move_blocks(array, row_blocks, col_blocks, quarter):
    width = array.shape[1]
    split = 2 if quarter % 32 == 0 else 1
    tile = quarter // split
    count = row_blocks.shape[0]
    return pl.pallas_call(
        move_kernel,
        out_shape=jax.ShapeDtypeStruct((count * quarter, width), array.dtype),
        grid_spec=pltpu.PrefetchScalarGridSpec(
            num_scalar_prefetch=2,
            grid=(count, split),
            in_specs=[pl.BlockSpec((tile, width), lambda i, j, rows, cols: (rows[i] * split + j, 0))],
            out_specs=pl.BlockSpec((tile, width), lambda i, j, rows, cols: (i * split + j, 0)),
        ),
        compiler_params=params(),
        cost_estimate=cost(0, 2 * count * quarter * width * array.dtype.itemsize),
    )(row_blocks, col_blocks, array)


def place_kernel(rows_ref, cols_ref, *refs):
    pieces, out_ref = refs[:2], refs[-1]
    for place, piece in enumerate(pieces):
        pl.when(pl.program_id(0) == place)(functools.partial(move_columns, cols_ref, piece, out_ref))


def place_quarters(pieces, row_blocks, col_blocks, out_type):
    quarter, width = pieces[0].shape
    shape = jax.ShapeDtypeStruct((4 * quarter, width), out_type)
    whole = None
    for start in (0, 2):
        held = [] if whole is None else [whole]
        whole = pl.pallas_call(
            place_kernel,
            out_shape=shape,
            grid_spec=pltpu.PrefetchScalarGridSpec(
                num_scalar_prefetch=2,
                grid=(2,),
                in_specs=[pl.BlockSpec((quarter, width), lambda i, rows, cols: (0, 0))] * 2
                + [pl.BlockSpec(memory_space=pl.ANY)] * len(held),
                out_specs=pl.BlockSpec((quarter, width), lambda i, rows, cols, start=start: (rows[start + i], 0)),
            ),
            input_output_aliases={4: 0} if held else {},
            compiler_params=params(40),
            cost_estimate=cost(0, shape.size * 4),
        )(row_blocks, col_blocks, *pieces[start : start + 2], *held)
    return whole


def unit_kernel(cols_ref, in_ref, out_ref):
    values = in_ref[...].astype(f32)
    rstd = lax.rsqrt(jnp.mean(values * values, axis=1, keepdims=True) + EPSILON)
    width = in_ref.shape[1] // BLOCKS
    for block in range(BLOCKS):
        start = pl.multiple_of(cols_ref[block] * width, 128)
        out_ref[:, block * width : (block + 1) * width] = (in_ref[:, pl.ds(start, width)].astype(f32) * rstd).astype(bf16)


def unit_rows(array, col_blocks, tile):
    rows, width = array.shape
    return pl.pallas_call(
        unit_kernel,
        out_shape=jax.ShapeDtypeStruct((rows, width), bf16),
        grid_spec=pltpu.PrefetchScalarGridSpec(
            num_scalar_prefetch=1,
            grid=(rows // tile,),
            in_specs=[pl.BlockSpec((tile, width), lambda i, cols: (i, 0))],
            out_specs=pl.BlockSpec((tile, width), lambda i, cols: (i, 0)),
        ),
        compiler_params=params(),
        cost_estimate=cost(0, 4 * rows * width),
    )(col_blocks, array)


def fit(rows):
    return next(tile for tile in (128, 96, 64, 48, 32, 16) if rows % tile == 0)


def add_norm_kernel(base_ref, a_ref, b_ref, c_ref, sum_ref, unit_ref):
    total = base_ref[...].astype(f32) + (a_ref[...].astype(f32) + b_ref[...].astype(f32) + c_ref[...].astype(f32))
    rstd = lax.rsqrt(jnp.mean(total * total, axis=1, keepdims=True) + EPSILON)
    sum_ref[...] = total
    unit_ref[...] = (total * rstd).astype(bf16)


def norm_back_kernel(base_ref, rest_ref, a_ref, b_ref, c_ref, *outs):
    base = base_ref[...].astype(f32)
    rstd = lax.rsqrt(jnp.mean(base * base, axis=1, keepdims=True) + EPSILON)
    unit = base * rstd
    grad = a_ref[...].astype(f32) + b_ref[...].astype(f32) + c_ref[...].astype(f32)
    total = rest_ref[...].astype(f32) + rstd * (grad - unit * jnp.mean(grad * unit, axis=1, keepdims=True))
    for out in outs:
        out[...] = total.astype(out.dtype)


def on_quarter(kernel, arrays, rows, out_types):
    width = arrays[0].shape[1]
    tile = fit(rows)
    spec = pl.BlockSpec((tile, width), lambda i: (i, 0))
    return pl.pallas_call(
        kernel,
        out_shape=[jax.ShapeDtypeStruct((rows, width), kind) for kind in out_types],
        grid=(rows // tile,),
        in_specs=[spec] * len(arrays),
        out_specs=[spec] * len(out_types),
        compiler_params=params(),
        cost_estimate=cost(0, rows * width * 16),
    )(*arrays)


def first_kernel(n, unit_ref, *refs):
    pieces, (out_ref, joined_ref, held_ref, sems) = refs[:n], refs[n:]
    rows = held_ref.shape[0] // n

    @pl.when(pl.program_id(0) == 0)
    def _():
        copies = [pltpu.make_async_copy(pieces[i], held_ref.at[pl.ds(i * rows, rows)], sems.at[i]) for i in range(n)]
        for copy in copies:
            copy.start()
        for copy in copies:
            copy.wait()
        joined_ref[...] = held_ref[...]

    out_ref[...] = nn(unit_ref[...], held_ref[...]).astype(bf16)


def first_product(unit, pieces, tile):
    tokens, width = unit.shape
    cols = pieces[0].shape[1]
    return pl.pallas_call(
        functools.partial(first_kernel, len(pieces)),
        out_shape=[jax.ShapeDtypeStruct((tokens, cols), bf16), jax.ShapeDtypeStruct((width, cols), bf16)],
        grid=(tokens // tile,),
        in_specs=[pl.BlockSpec((tile, width), lambda i: (i, 0))] + [pl.BlockSpec(memory_space=pl.ANY)] * len(pieces),
        out_specs=[pl.BlockSpec((tile, cols), lambda i: (i, 0)), pl.BlockSpec((width, cols), lambda i: (0, 0))],
        scratch_shapes=[pltpu.VMEM((width, cols), bf16), pltpu.SemaphoreType.DMA((len(pieces),))],
        compiler_params=params(),
        cost_estimate=cost(2 * tokens * width * cols, 2 * (tokens + width) * (width + cols)),
    )(unit, *pieces)


def quarter_kernel(order_ref, in_ref, weight_ref, *outs):
    values = in_ref[...]
    width = weight_ref.shape[0]
    for start in range(0, width, 512):
        part = nt(values, weight_ref[start : start + 512]).astype(bf16)
        for place, out in enumerate(outs):

            @pl.when(pl.program_id(0) == place)
            def _(out=out, part=part, start=start):
                out[:, start : start + 512] = part


def quarter_products(array, weight, quarters, top):
    width, cols = weight.shape
    rows = array.shape[0] // 4
    return pl.pallas_call(
        quarter_kernel,
        out_shape=[jax.ShapeDtypeStruct((rows, width), bf16)] * 2,
        grid_spec=pltpu.PrefetchScalarGridSpec(
            num_scalar_prefetch=1,
            grid=(2,),
            in_specs=[
                pl.BlockSpec((rows, cols), lambda i, order: (order[top - i], 0)),
                pl.BlockSpec((width, cols), lambda i, order: (0, 0), pipeline_mode=pl.Buffered(1)),
            ],
            out_specs=[pl.BlockSpec((rows, width), lambda i, order: (0, 0))] * 2,
        ),
        compiler_params=params(),
        cost_estimate=cost(4 * rows * width * cols, 4 * rows * width),
    )(quarters, array, weight)


def back_kernel(order_ref, *refs):
    pieces, weight_ref, out_ref = refs[:4], refs[4], refs[5]
    for place, piece in enumerate(pieces):

        @pl.when(pl.program_id(0) == place)
        def _(piece=piece):
            out_ref[...] = nn(piece[...], weight_ref[...]).astype(bf16)


def back_product(pieces, weight, quarters):
    rows, width = pieces[0].shape
    cols = weight.shape[1]
    return pl.pallas_call(
        back_kernel,
        out_shape=jax.ShapeDtypeStruct((4 * rows, cols), bf16),
        grid_spec=pltpu.PrefetchScalarGridSpec(
            num_scalar_prefetch=1,
            grid=(4,),
            in_specs=[pl.BlockSpec((rows, width), lambda i, order: (0, 0), pipeline_mode=pl.Buffered(1))] * 4
            + [pl.BlockSpec((width, cols), lambda i, order: (0, 0), pipeline_mode=pl.Buffered(1))],
            out_specs=pl.BlockSpec((rows, cols), lambda i, order: (order[i], 0)),
        ),
        compiler_params=params(),
        cost_estimate=cost(8 * rows * width * cols, 8 * rows * width),
    )(quarters, *pieces, weight)


def ffn_kernel(step, order_ref, near_ref, core_ref, gmixed_ref, gate_hbm, up_hbm, down_hbm, *refs):
    mixed_ref, ggate_ref, gup_ref, gunit_refs, out_refs = refs[0], refs[1], refs[2], refs[3:5], refs[5:7]
    gate_ref, up_ref, down_ref, unit_ref, sems = refs[7:]
    width, hidden = gate_ref.shape
    rows = width // BLOCKS
    copies = []
    for i in range(BLOCKS):
        start = pl.multiple_of(order_ref[i] * rows, rows)
        for source, held in ((gate_hbm, gate_ref), (up_hbm, up_ref)):
            copies.append((source.at[pl.ds(start, rows)], held.at[pl.ds(i * rows, rows)]))
    copies.append((down_hbm, down_ref))
    copies = [pltpu.make_async_copy(*ends, sems.at[i]) for i, ends in enumerate(copies)]

    @pl.when(pl.program_id(0) == 0)
    def _():
        for copy in copies:
            copy.start()
        unit_ref[...] = near_ref[...]
        for copy in copies:
            copy.wait()

    @pl.when(pl.program_id(0) == 1)
    def _():
        unit_ref[...] = core_ref[...]

    unit = unit_ref[...]
    for start in range(0, hidden, step):
        cols = slice(start, min(start + step, hidden))
        gate = nn(unit, gate_ref[:, cols])
        up = nn(unit, up_ref[:, cols])
        gmixed = gmixed_ref[:, cols].astype(f32)
        sig = jax.nn.sigmoid(gate)
        silu = gate * sig
        mixed_ref[:, cols] = (silu * up).astype(bf16)
        ggate_ref[:, cols] = (gmixed * up * (sig * (1.0 + gate * (1.0 - sig)))).astype(bf16)
        gup_ref[:, cols] = (gmixed * silu).astype(bf16)
    ggate, gup, mixed = ggate_ref[...], gup_ref[...], mixed_ref[...]
    for start in range(0, width, 512):
        cols = slice(start, start + 512)
        gunit = (nt(ggate, gate_ref[cols]) + nt(gup, up_ref[cols])).astype(bf16)
        out = nt(mixed, down_ref[cols]).astype(bf16)
        for place in range(2):

            @pl.when(pl.program_id(0) == place)
            def _(place=place, cols=cols, gunit=gunit, out=out):
                gunit_refs[place][:, cols] = gunit
                out_refs[place][:, cols] = out


def feed_forward(units, gmixed, half, pair, down, order):
    rows, width = units[0].shape
    hidden = down.shape[1]
    anywhere = pl.BlockSpec(memory_space=pl.ANY)
    fixed = pl.BlockSpec((rows, width), lambda i, order: (0, 0))
    line = lambda first=0: pl.BlockSpec((rows, hidden), lambda i, order: (i + first, 0))
    shapes = [jax.ShapeDtypeStruct((2 * rows, hidden), bf16)] * 3 + [jax.ShapeDtypeStruct((rows, width), bf16)] * 4
    once = pl.BlockSpec((rows, width), lambda i, order: (0, 0), pipeline_mode=pl.Buffered(1))
    return pl.pallas_call(
        functools.partial(ffn_kernel, 256),
        out_shape=shapes,
        grid_spec=pltpu.PrefetchScalarGridSpec(
            num_scalar_prefetch=1,
            grid=(2,),
            in_specs=[once, once, line(2 * half), anywhere, anywhere, anywhere],
            out_specs=[line()] * 3 + [fixed] * 4,
            scratch_shapes=[pltpu.VMEM((width, hidden), bf16)] * 3
            + [pltpu.VMEM((rows, width), bf16), pltpu.SemaphoreType.DMA((2 * BLOCKS + 1,))],
        ),
        compiler_params=params(60),
        cost_estimate=cost(20 * rows * width * hidden, 2 * (8 * rows * width + 3 * width * hidden)),
    )(order, *units, gmixed, *pair, down)


def weight_kernel(layout, order_ref, quarters_ref, *refs):
    refs, out = list(refs[:-1]), refs[-1]
    total = None
    for n_left, n_right in layout:
        lefts, rights = [refs.pop(0)[...] for _ in range(n_left)], [refs.pop(0)[...] for _ in range(n_right)]
        left, right = [jnp.concatenate(item, axis=0) if len(item) > 1 else item[0] for item in (lefts, rights)]
        part = nn(left.T, right)
        total = part if total is None else total + part
    out[...] = total.astype(bf16)


def weight_grads(parts, order, quarters):
    width = parts[0][0][0][0].shape[1]
    rows = width // BLOCKS
    cols = parts[0][1][0][0].shape[1]
    arrays, specs, tokens = [], [], 0
    for pieces in parts:
        for side, side_pieces in enumerate(pieces):
            for array, *place in side_pieces:
                n = array.shape[0] // (1 if not place else 4 if place[0] == "q" else 2)

                def index(i, order, quarters, side=side, place=tuple(place)):
                    row = 0 if not place else quarters[place[1]] if place[0] == "q" else place[0]
                    return (row, 0 if side else i)

                mode = {"pipeline_mode": pl.Buffered(1)} if side else {}
                specs.append(pl.BlockSpec((n, cols if side else rows), index, **mode))
                arrays.append(array)
                tokens += n if side else 0
    return pl.pallas_call(
        functools.partial(weight_kernel, tuple((len(lefts), len(rights)) for lefts, rights in parts)),
        out_shape=jax.ShapeDtypeStruct((width, cols), bf16),
        grid_spec=pltpu.PrefetchScalarGridSpec(
            num_scalar_prefetch=2,
            grid=(BLOCKS,),
            in_specs=specs,
            out_specs=pl.BlockSpec((rows, cols), lambda i, order, quarters: (order[i], 0)),
        ),
        compiler_params=params(48),
        cost_estimate=cost(2 * tokens * width * cols, 2 * (tokens + width) * (width + cols)),
    )(order, quarters, *arrays)


def pair_kernel(order_ref, *refs):
    units, (ggate0, gup0, ggate1, gup1), out = refs[:4], refs[4:8], refs[8]
    cols = ggate0.shape[1]
    near = jnp.concatenate([units[0][...], units[1][...]], axis=0).T
    far = jnp.concatenate([units[2][...], units[3][...]], axis=0).T
    out[:, :cols] = (nn(near, ggate0[...]) + nn(far, ggate1[...])).astype(bf16)
    out[:, cols:] = (nn(near, gup0[...]) + nn(far, gup1[...])).astype(bf16)


def pair_grads(units, grads, order):
    quarter, width = units[0].shape
    rows = width // BLOCKS
    cols = grads[0].shape[1]
    held = pl.BlockSpec((2 * quarter, cols), lambda i, order: (0, 0), pipeline_mode=pl.Buffered(1))
    return pl.pallas_call(
        pair_kernel,
        out_shape=jax.ShapeDtypeStruct((width, 2 * cols), bf16),
        grid_spec=pltpu.PrefetchScalarGridSpec(
            num_scalar_prefetch=1,
            grid=(BLOCKS,),
            in_specs=[pl.BlockSpec((quarter, rows), lambda i, order: (0, i))] * 4 + [held] * 4,
            out_specs=pl.BlockSpec((rows, 2 * cols), lambda i, order: (order[i], 0)),
        ),
        compiler_params=params(48),
        cost_estimate=cost(16 * quarter * width * cols, 2 * (4 * quarter + width) * (width + 2 * cols)),
    )(order, *units, *grads)


def per_device(
    n_seq,
    n_head,
    tokens,
    doc_reset,
    gain_attn,
    gain_ffn,
    query_weight,
    key_weight,
    value_weight,
    out_weight,
    gate_weight,
    up_weight,
    down_weight,
    grad_out,
):
    rows, length, width = tokens.shape
    heads = query_weight.shape[1] // FEAT
    count = rows * length
    quarter = count // 4
    half = 2 * quarter
    me = lax.axis_index("seq").astype(jnp.int32)
    head_me = lax.axis_index("head").astype(jnp.int32)
    order = jnp.arange(BLOCKS, dtype=jnp.int32)
    if n_seq == 8:
        order = me ^ order
    quarters = head_me ^ jnp.arange(4, dtype=jnp.int32)

    gain_one = gain_attn.astype(f32)[:, None]
    gain_two = gain_ffn.astype(f32)[:, None]
    scaled = lambda weight, gain: (weight.astype(f32) * gain).astype(bf16)
    qkv_own = jnp.concatenate([query_weight, key_weight, value_weight], axis=1)
    gate_w = lax.all_gather(scaled(gate_weight, gain_two), "seq", axis=0, tiled=True)
    up_w = lax.all_gather(after(scaled(up_weight, gain_two), gate_w), "seq", axis=0, tiled=True)
    pair_w = (gate_w, up_w)
    qkv_pieces = gather_rows(scaled(qkv_own, gain_one), n_seq)
    tie = lambda value, found: after(value, *found) if n_seq == 8 else value
    out_pieces = gather_rows(tie(out_weight.T, qkv_pieces), n_seq)
    down_pieces = gather_rows(tie(down_weight.T, out_pieces[2::2]), n_seq)

    flat = tokens.reshape(count, width)
    unit_one = unit_rows(flat, order, quarter // 2)
    x_own = move_blocks(flat, quarters[:1], order, quarter)
    dy = move_blocks(grad_out.reshape(count, width), quarters, order, quarter)

    docs = jnp.cumsum(doc_reset, axis=1)
    final = docs[:, -1:]
    flag = jnp.broadcast_to(final > 0, docs.shape)
    edges = jnp.stack([docs, docs == 0, docs == final, flag] + [jnp.zeros_like(docs)] * 4, axis=2).astype(f32)
    doc_rows = jnp.broadcast_to(docs[:, None, :], (rows, 8, length)).astype(f32)
    tables, feat_rows, to_key, to_query = feature_tables(heads)

    lanes = 2 * heads * FEAT
    values = heads * VHEAD
    unit_flops = 2 * rows * heads * length * WIDE * VHEAD
    qkv, qkv_w = first_product(unit_one, qkv_pieces, quarter)
    qkv = qkv.reshape(rows, length, lanes + values)
    (states,) = by_row(
        functools.partial(state_kernel, heads),
        rows,
        [(qkv, True), (edges, True), (tables["ka"], False), (tables["kb"], False), (feat_rows, False)],
        [((heads, TALL, VHEAD), bf16)],
        flops=3 * unit_flops,
    )
    numerator, denominator = by_row(
        functools.partial(inside_kernel, heads),
        rows,
        [(qkv, True), (edges, True), (doc_rows, True), (to_key, False)],
        [((length, values), f32), ((length, heads), f32)],
        flops=3 * unit_flops,
    )
    state_in, place = scan_end(scan_begin(states, False, me, n_seq, (gate_w,)), False, me, n_seq)
    query_tables = [(tables["qa"], False), (tables["qb"], False), (feat_rows, False)]
    key_tables = [(tables["ka"], False), (tables["kb"], False), (feat_rows, False)]
    attended, rden = by_row(
        functools.partial(attend_kernel, heads),
        rows,
        [(qkv, True), (edges, True), (numerator, True), (denominator, True), (state_in, False)] + query_tables,
        [((length, values), bf16), ((length, heads), f32)],
        place=place,
        flops=3 * unit_flops,
    )
    attended_flat = attended.reshape(count, values)
    out_w = join_rows(out_pieces)
    far = quarter_products(attended_flat, out_w, quarters, 3)
    near = quarter_products(attended_flat, out_w, quarters, 1)
    branch = [near[1], near[0], far[1], far[0]]

    def grad_mixed(sent):
        down = join_rows(down_pieces)
        return down, nn(after(dy, sent), down).astype(bf16)

    branch, (down_w, gmixed) = scatter_head(branch, beside=grad_mixed)
    hidden, unit_two = on_quarter(add_norm_kernel, [x_own, *branch], quarter, [f32, bf16])
    first_half = []

    def near_rows(units):
        first_half.extend(feed_forward(units, gmixed, 0, pair_w, down_w, order))
        return first_half

    units = gather_head(unit_two, near_rows)
    second_half = feed_forward(units[2:], gmixed, 1, pair_w, down_w, order)
    halves = first_half, second_half
    gunit, ffn_out = [[item[i] for item in halves for i in place] for place in ((3, 4), (5, 6))]

    def ffn_weights(sent):
        first = pair_grads([after(units[0], sent), *units[1:]], [item[i] for item in halves for i in (1, 2)], order)
        left = after(dy, first)
        parts = [([(left, i)], [(item[0],)]) for i, item in enumerate(halves)]
        return first, weight_grads(parts, split_order(order, n_seq), quarters)

    terms, (grad_pair, grad_down) = scatter_head(gunit, beside=ffn_weights)
    grad_pair = lax.psum_scatter(grad_pair, "seq", scatter_dimension=0, tiled=True).astype(f32)
    grad_hidden, grad_branch = on_quarter(norm_back_kernel, [hidden, dy, *terms], quarter, [f32, bf16])
    grad_branch = gather_head(grad_branch)

    grad_att = back_product(grad_branch, out_w, quarters).reshape(rows, length, values)
    carry, gnum, gden = by_row(
        functools.partial(carry_kernel, heads),
        rows,
        [(qkv, True), (edges, True), (grad_att, True), (attended, True), (rden, True)] + query_tables,
        [((heads, TALL, VHEAD), bf16), ((length, values), bf16), ((length, heads), f32)],
        flops=3 * unit_flops,
    )
    gboth, gval = by_row(
        functools.partial(inside_back_kernel, heads),
        rows,
        [(qkv, True), (edges, True), (doc_rows, True), (gnum, True), (gden, True), (state_in, False)]
        + [(to_key, False), (to_query, False)]
        + query_tables,
        [((length, lanes), f32), ((length, values), f32)],
        place=place,
        flops=11 * unit_flops,
    )
    sides = [[(grad_branch[i],), (grad_branch[i + 1],)] for i in (0, 2)]
    parts = [(side, [(attended_flat, "q", i), (attended_flat, "q", i + 1)]) for side, i in zip(sides, (0, 2))]
    grad_out_w = weight_grads(parts, split_order(order, n_seq), quarters)
    found = scan_begin(carry, True, me, n_seq)
    ffn_out[3] = after(ffn_out[3], grad_att)
    terms, _ = scatter_head(ffn_out, beside=lambda _: found)
    block_own = (hidden + (terms[0].astype(f32) + terms[1].astype(f32) + terms[2].astype(f32))).astype(bf16)
    down_pairs = scatter_begin(after(grad_down, *grad_branch), n_seq)
    carry_in, place_back = scan_end(found, True, me, n_seq)
    carry_in = after(carry_in, block_own, *down_pairs)
    out_pairs = scatter_begin(grad_out_w, n_seq)
    block_all = gather_head(block_own)
    down_terms = scatter_sends(down_pairs)
    (gqkv,) = by_row(
        functools.partial(finish_back_kernel, heads),
        rows,
        [(qkv, True), (edges, True), (carry_in, False), (gboth, True), (gval, True)] + key_tables,
        [((length, lanes + values), bf16)],
        place=place_back,
        flops=6 * unit_flops,
    )
    gqkv = after(gqkv.reshape(count, lanes + values), *block_all, *out_pairs)
    far = quarter_products(gqkv, qkv_w, quarters, 3)
    near = quarter_products(gqkv, qkv_w, quarters, 1)
    out_terms = scatter_sends(out_pairs)
    terms, grad_qkv = scatter_head(
        [near[1], near[0], far[1], far[0]],
        beside=lambda sent: weight_grads(
            [([(after(unit_one, sent),)], [(gqkv,)])], split_order(order, n_seq), quarters
        ),
    )
    terms = after(terms, *down_terms[:2], *out_terms)
    (grad_x,) = on_quarter(norm_back_kernel, [x_own, grad_hidden, *terms], quarter, [bf16])
    grad_x_all = gather_head(grad_x)
    grad_x_all[0] = after(grad_x_all[0], *down_terms[2:])
    grad_down = scatter_end(down_pairs, down_terms)
    grad_out_w = scatter_end(out_pairs, out_terms)
    grad_qkv = scatter_begin(grad_qkv, n_seq)
    grad_qkv = (grad_qkv[0],) + tuple(after(pair, grad_x) for pair in grad_qkv[1:])
    grad_qkv = scatter_end(grad_qkv, scatter_sends(grad_qkv))

    back = lambda value, kind: place_quarters(value, quarters, order, kind).reshape(rows, length, width)
    hidden_units = gate_weight.shape[1]
    grad_gate, grad_up = grad_pair[:, :hidden_units], grad_pair[:, hidden_units:]
    gain_sums = jnp.stack(
        [
            jnp.sum(qkv_own.astype(f32) * grad_qkv, axis=1),
            jnp.sum(gate_weight.astype(f32) * grad_gate + up_weight.astype(f32) * grad_up, axis=1),
        ]
    )
    gain_sums = gain_sums + send(gain_sums, "head", CORE, 4)
    gain_sums = gain_sums + send(gain_sums, "head", ACROSS, 4)
    grad_qkv = grad_qkv * gain_one
    narrow = heads * FEAT
    return (
        back(block_all, bf16),
        back(grad_x_all, f32),
        gain_sums[0],
        gain_sums[1],
        grad_qkv[:, :narrow],
        grad_qkv[:, narrow:lanes],
        grad_qkv[:, lanes:],
        grad_out_w.T,
        grad_gate * gain_two,
        grad_up * gain_two,
        grad_down.T,
    )


def solution(mesh):
    placed = (
        P(None, "seq", None),
        P(None, "seq"),
        P("seq"),
        P("seq"),
        P("seq", "head"),
        P("seq", "head"),
        P("seq", "head"),
        P("head", "seq"),
        P("seq", "head"),
        P("seq", "head"),
        P("head", "seq"),
        P(None, "seq", None),
    )
    return jax.shard_map(
        functools.partial(per_device, mesh.shape["seq"], mesh.shape["head"]),
        mesh=mesh,
        in_specs=placed,
        out_specs=(P(None, "seq", None), P(None, "seq", None)) + placed[2:11],
        check_vma=False,
    )
```

```python
import functools

import jax
import jax.numpy as jnp
import numpy as np
from jax import lax
from jax.experimental import pallas as pl
from jax.experimental.pallas import tpu as pltpu
from jax.sharding import PartitionSpec as P

FEAT = 16
VHEAD = 128
EPSILON = 1e-06
PAIRS = [(a, b) for a in range(FEAT + 1) for b in range(a, FEAT + 1)]
WIDE = 256
TALL = 160
NORM_ROW = len(PAIRS)
FLAG_ROW = NORM_ROW + 2
BLOCKS = 8
COST = 2
bf16, f32 = jnp.bfloat16, jnp.float32


def feature_tables(heads):
    lanes = 2 * heads * FEAT
    tables = {name: np.zeros((lanes, heads * WIDE), np.float32) for name in ("qa", "qb", "ka", "kb")}
    rows = np.zeros((8, heads * WIDE), np.float32)
    to_key = np.zeros((lanes, heads * lanes), np.float32)
    to_query = np.zeros((lanes, heads * lanes), np.float32)
    for head in range(heads):
        for place, (a, b) in enumerate(PAIRS):
            column = head * WIDE + place
            for name, entry, row in (("a", a, 0), ("b", b, 1)):
                if entry == 0:
                    rows[row, column] = 1.0
                else:
                    lane = head * FEAT + entry - 1
                    tables["q" + name][lane, column] = 1.0
                    tables["k" + name][heads * FEAT + lane, column] = 1.0
            rows[2, column] = 1.0 if b == 0 else 0.25 if a == 0 else 1 / 32 if a == b else 1 / 16
        for feat in range(FEAT):
            lane = head * FEAT + feat
            to_key[lane, head * lanes + heads * FEAT + lane] = 0.25
            to_query[heads * FEAT + lane, head * lanes + lane] = 0.25
    tables = {name: jnp.asarray(item, bf16) for name, item in tables.items()}
    return tables, jnp.asarray(rows), jnp.asarray(to_key, bf16), jnp.asarray(to_query, bf16)


def nn(left, right):
    return lax.dot_general(left, right, (((1,), (0,)), ((), ())), preferred_element_type=f32)


def nt(left, right):
    return lax.dot_general(left, right, (((1,), (1,)), ((), ())), preferred_element_type=f32)


def tn(left, right):
    return lax.dot_general(left, right, (((0,), (0,)), ((), ())), preferred_element_type=f32)


def params(mib=32):
    return pltpu.CompilerParams(vmem_limit_bytes=mib << 20)


def cost(flops, nbytes):
    return pl.CostEstimate(flops=int(flops) // COST, bytes_accessed=int(nbytes) // COST, transcendentals=0)


def whole_spec(array):
    zeros = (0,) * array.ndim
    return pl.BlockSpec(array.shape, lambda *_: zeros)


def row_spec(array):
    zeros = (0,) * (array.ndim - 1)
    return pl.BlockSpec((1,) + array.shape[1:], lambda row, *_: (row,) + zeros)


def pack_state(state, norm_row, flag):
    place = lax.broadcasted_iota(jnp.int32, (TALL, VHEAD), 0)
    block = state[:TALL]
    block = jnp.where(place == NORM_ROW, norm_row[:, :VHEAD], block)
    block = jnp.where(place == NORM_ROW + 1, norm_row[:, VHEAD:], block)
    return jnp.where(place == FLAG_ROW, flag, block).astype(bf16)


def unpack_state(block):
    tail = block[TALL - 16 :].astype(f32)
    base = TALL - 16
    low = tail[NORM_ROW - base : NORM_ROW - base + 1]
    high = tail[NORM_ROW + 1 - base : NORM_ROW + 2 - base]
    full = jnp.concatenate([block, jnp.zeros((WIDE - TALL, VHEAD), block.dtype)], axis=0)
    return full, jnp.concatenate([low, high], axis=1)


def state_kernel(heads, qkv_ref, edge_ref, ka_ref, kb_ref, rows_ref, out_ref):
    keys = qkv_ref[0, :, : 2 * heads * FEAT]
    edges = edge_ref[0]
    last, flag = edges[:, 2:3], edges[0:1, 3:4]
    for head in range(heads):
        cols = slice(head * WIDE, (head + 1) * WIDE)
        phi = (nn(keys, ka_ref[:, cols]) + rows_ref[0:1, cols]) * (nn(keys, kb_ref[:, cols]) + rows_ref[1:2, cols])
        phi = phi * last
        start = 2 * heads * FEAT + head * VHEAD
        state = tn(phi.astype(bf16), qkv_ref[0, :, start : start + VHEAD])
        out_ref[0, head] = pack_state(state, jnp.sum(phi, axis=0, keepdims=True), flag)


def local_mask(edges, docs):
    length = edges.shape[0]
    later = lax.broadcasted_iota(jnp.int32, (length, length), 0) >= lax.broadcasted_iota(jnp.int32, (length, length), 1)
    return later & (edges[:, 0:1] == docs)


def inside_kernel(heads, qkv_ref, edge_ref, doc_ref, key_ref, num_ref, den_ref):
    lanes = 2 * heads * FEAT
    both = qkv_ref[0, :, :lanes]
    mask = local_mask(edge_ref[0], doc_ref[0, 0:1])
    moved = nn(both, key_ref[...]).astype(bf16)
    dens = []
    for head in range(heads):
        scores = nt(moved[:, head * lanes : (head + 1) * lanes], both)
        weights = jnp.where(mask, 1.0 + scores + 0.5 * scores * scores, 0.0)
        dens.append(jnp.sum(weights, axis=1, keepdims=True))
        start = lanes + head * VHEAD
        num_ref[0, :, head * VHEAD : (head + 1) * VHEAD] = nn(
            weights.astype(bf16), qkv_ref[0, :, start : start + VHEAD]
        )
    den_ref[0] = jnp.concatenate(dens, axis=1)


def block_at(place_ref, states_ref, row, heads, head):
    per = states_ref.shape[1]
    index = row * heads + head
    return states_ref[place_ref[index // per], index % per]


def query_features(both, qa, qb, rows, first):
    left = nn(both, qa) + rows[0:1]
    right = nn(both, qb) + rows[1:2]
    return left, right, left * right * rows[2:3] * first


def attend_kernel(heads, place_ref, qkv_ref, edge_ref, num_ref, den_ref, states_ref, qa_ref, qb_ref, rows_ref, att_ref, rden_ref):
    both = qkv_ref[0, :, : 2 * heads * FEAT]
    first = edge_ref[0][:, 1:2]
    rdens = []
    for head in range(heads):
        cols = slice(head * WIDE, (head + 1) * WIDE)
        _, _, phi = query_features(both, qa_ref[:, cols], qb_ref[:, cols], rows_ref[:, cols], first)
        factor, norm = unpack_state(block_at(place_ref, states_ref, pl.program_id(0), heads, head))
        den = den_ref[0][:, head : head + 1] + jnp.sum(phi * norm, axis=1, keepdims=True)
        rden = 1.0 / den
        out = slice(head * VHEAD, (head + 1) * VHEAD)
        att_ref[0, :, out] = ((num_ref[0, :, out] + nn(phi.astype(bf16), factor)) * rden).astype(bf16)
        rdens.append(rden)
    rden_ref[0] = jnp.concatenate(rdens, axis=1)


def carry_kernel(heads, qkv_ref, edge_ref, ga_ref, att_ref, rden_ref, qa_ref, qb_ref, rows_ref, carry_ref, gnum_ref, gden_ref):
    both = qkv_ref[0, :, : 2 * heads * FEAT]
    edges = edge_ref[0]
    first, flag = edges[:, 1:2], edges[0:1, 3:4]
    gdens = []
    for head in range(heads):
        cols = slice(head * WIDE, (head + 1) * WIDE)
        out = slice(head * VHEAD, (head + 1) * VHEAD)
        _, _, phi = query_features(both, qa_ref[:, cols], qb_ref[:, cols], rows_ref[:, cols], first)
        grad = ga_ref[0, :, out].astype(f32)
        rden = rden_ref[0][:, head : head + 1]
        gnum = (grad * rden).astype(bf16)
        gden = -jnp.sum(grad * att_ref[0, :, out].astype(f32), axis=1, keepdims=True) * rden
        gnum_ref[0, :, out] = gnum
        carry_ref[0, head] = pack_state(
            tn(phi.astype(bf16), gnum), jnp.sum(phi * gden, axis=0, keepdims=True), flag
        )
        gdens.append(gden)
    gden_ref[0] = jnp.concatenate(gdens, axis=1)


def inside_back_kernel(
    heads, place_ref, qkv_ref, edge_ref, doc_ref, gnum_ref, gden_ref, states_ref, key_ref, query_ref, qa_ref, qb_ref,
    rows_ref, gboth_ref, gval_ref,
):
    lanes = 2 * heads * FEAT
    both = qkv_ref[0, :, :lanes]
    edges = edge_ref[0]
    first = edges[:, 1:2]
    mask = local_mask(edges, doc_ref[0, 0:1])
    moved = nn(both, key_ref[...]).astype(bf16)
    back = nn(both, query_ref[...]).astype(bf16)
    total = jnp.zeros((both.shape[0], lanes), f32)
    for head in range(heads):
        cols = slice(head * WIDE, (head + 1) * WIDE)
        out = slice(head * VHEAD, (head + 1) * VHEAD)
        own = slice(head * lanes, (head + 1) * lanes)
        start = lanes + head * VHEAD
        values = qkv_ref[0, :, start : start + VHEAD]
        gnum = gnum_ref[0, :, out]
        gden = gden_ref[0][:, head : head + 1]
        scores = nt(moved[:, own], both)
        weights = jnp.where(mask, 1.0 + scores + 0.5 * scores * scores, 0.0).astype(bf16)
        gval_ref[0, :, out] = tn(weights, gnum)
        gscores = jnp.where(mask, (nt(gnum, values) + gden) * (1.0 + scores), 0.0).astype(bf16)
        total = total + nn(gscores, back[:, own]) + tn(gscores, moved[:, own])
        left, right, _ = query_features(both, qa_ref[:, cols], qb_ref[:, cols], rows_ref[:, cols], first)
        factor, norm = unpack_state(block_at(place_ref, states_ref, pl.program_id(0), heads, head))
        place = lax.broadcasted_iota(jnp.int32, (1, WIDE), 1)
        gphi = jnp.where(place < NORM_ROW, (nt(gnum, factor) + norm * gden) * rows_ref[2:3, cols], 0.0) * first
        total = total + nt((gphi * right).astype(bf16), qa_ref[:, cols]) + nt((gphi * left).astype(bf16), qb_ref[:, cols])
    gboth_ref[0] = total


def finish_back_kernel(
    heads, place_ref, qkv_ref, edge_ref, carry_ref, gboth_ref, gval_ref, ka_ref, kb_ref, rows_ref, out_ref
):
    lanes = 2 * heads * FEAT
    both = qkv_ref[0, :, :lanes]
    last = edge_ref[0][:, 2:3]
    total = gboth_ref[0]
    for head in range(heads):
        cols = slice(head * WIDE, (head + 1) * WIDE)
        start = lanes + head * VHEAD
        values = qkv_ref[0, :, start : start + VHEAD]
        left = nn(both, ka_ref[:, cols]) + rows_ref[0:1, cols]
        right = nn(both, kb_ref[:, cols]) + rows_ref[1:2, cols]
        factor, norm = unpack_state(block_at(place_ref, carry_ref, pl.program_id(0), heads, head))
        phi = (left * right * last).astype(bf16)
        gval = gval_ref[0, :, head * VHEAD : (head + 1) * VHEAD] + nn(phi, factor)
        out_ref[0, :, start : start + VHEAD] = gval.astype(bf16)
        place = lax.broadcasted_iota(jnp.int32, (1, WIDE), 1)
        gphi = jnp.where(place < NORM_ROW, nt(values, factor) + norm, 0.0) * last
        total = total + nt((gphi * right).astype(bf16), ka_ref[:, cols]) + nt((gphi * left).astype(bf16), kb_ref[:, cols])
    out_ref[0, :, :lanes] = total.astype(bf16)


def by_row(kernel, rows, inputs, outputs, place=None, flops=0):
    arrays = [array for array, _ in inputs]
    specs = [row_spec(array) if per_row else whole_spec(array) for array, per_row in inputs]
    shapes = [jax.ShapeDtypeStruct((rows,) + shape, kind) for shape, kind in outputs]
    nbytes = sum(item.size * item.dtype.itemsize for item in arrays + shapes)
    return pl.pallas_call(
        kernel,
        out_shape=shapes,
        grid_spec=pltpu.PrefetchScalarGridSpec(
            num_scalar_prefetch=0 if place is None else 1,
            grid=(rows,),
            in_specs=specs,
            out_specs=[row_spec(shape) for shape in shapes],
        ),
        compiler_params=params(40),
        cost_estimate=cost(flops, nbytes),
    )(*([] if place is None else [place]), *arrays)


def scan_kernel(backward, me_ref, *refs):
    pieces, outs, (held, ahead) = refs[:8], refs[8:16], refs[16:]
    for rel in range(8):
        held[rel] = pieces[rel][...]
    me = me_ref[0]
    for block in range(held.shape[1]):
        run = jnp.zeros(held.shape[2:], f32)
        for step in range(8):
            rel = me ^ (7 - step if backward else step)
            ahead[rel, block] = run.astype(bf16)
            own = held[rel, block].astype(f32)
            run = own + (1.0 - own[FLAG_ROW : FLAG_ROW + 1]) * run
    for rel in range(8):
        outs[rel][...] = ahead[rel]


def scan_begin(states, backward, me, count, earlier=()):
    blocks = states.shape[0] * states.shape[1]
    flat = states.reshape(blocks, TALL, VHEAD)
    if count != 8 or blocks % 8:
        return lax.all_gather(flat, "seq").astype(f32)
    per = blocks // 8
    split = flat.reshape(8, per, TALL, VHEAD)
    parts = [lax.dynamic_index_in_dim(split, me ^ rel, 0, keepdims=False) for rel in range(8)]
    pieces = [after(parts[0], *earlier)] + [send(parts[rel], "seq", rel, 8) for rel in range(1, 8)]
    return pl.pallas_call(
        functools.partial(scan_kernel, backward),
        out_shape=[jax.ShapeDtypeStruct((per, TALL, VHEAD), bf16)] * 8,
        in_specs=[pl.BlockSpec(memory_space=pltpu.SMEM)] + [pl.BlockSpec(memory_space=pltpu.VMEM)] * 8,
        out_specs=[pl.BlockSpec(memory_space=pltpu.VMEM)] * 8,
        scratch_shapes=[pltpu.VMEM((8, per, TALL, VHEAD), bf16)] * 2,
        compiler_params=params(),
    )(me.reshape(1), *pieces)


def scan_end(found, backward, me, count):
    if isinstance(found, (list, tuple)):
        back = [found[0]] + [send(found[rel], "seq", rel, 8) for rel in range(1, 8)]
        return jnp.stack(back), me ^ jnp.arange(8, dtype=jnp.int32)
    keep = 1.0 - found[:, :, FLAG_ROW : FLAG_ROW + 1]
    run = jnp.zeros(found.shape[1:], f32)
    for step in range(count):
        at = count - 1 - step if backward else step
        reached = at > me if backward else at < me
        run = jnp.where(reached, found[at] + keep[at] * run, run)
    return run.astype(bf16)[None], jnp.zeros((1,), jnp.int32)


def send(value, axis, mask, count):
    return lax.ppermute(value, axis, [(i, i ^ mask) for i in range(count)])


def gather_rows(shard, count):
    if count != 8:
        return [lax.all_gather(shard, "seq", axis=0, tiled=True)]
    pieces = [shard, send(shard, "seq", 1, 8)]
    for mask in (2, 4, 6):
        piece = send(shard, "seq", mask, 8)
        pieces += [piece, send(piece, "seq", 1, 8)]
    return pieces


def after(value, *earlier):
    return lax.optimization_barrier((value, earlier))[0]


def swap_blocks(array, order):
    split = array.reshape((BLOCKS, array.shape[0] // BLOCKS) + array.shape[1:])
    return join_rows([lax.dynamic_index_in_dim(split, order[i], 0, keepdims=False) for i in range(BLOCKS)])


def split_order(order, n_seq):
    return jnp.array([0, 4, 1, 5, 2, 6, 3, 7], jnp.int32) if n_seq == 8 else order


def scatter_begin(whole, n_seq):
    if n_seq != 8:
        return (lax.psum_scatter(whole, "seq", scatter_dimension=0, tiled=True).astype(f32),)
    rows = whole.shape[0] // 8
    other = send(whole[4 * rows :], "seq", 1, 8)
    pairs = [
        whole[i * rows : (i + 1) * rows].astype(f32) + other[i * rows : (i + 1) * rows].astype(f32) for i in range(4)
    ]
    return (pairs[0],) + tuple(pair.astype(bf16) for pair in pairs[1:])


def scatter_sends(pairs):
    return [send(pair, "seq", 2 * place + 2, 8) for place, pair in enumerate(pairs[1:])]


def scatter_end(pairs, terms):
    total = pairs[0]
    for term in terms:
        total = total + term.astype(f32)
    return total


def join_rows(pieces):
    return pieces[0] if len(pieces) == 1 else jnp.concatenate(pieces, axis=0)


CORE, ACROSS = 1, 2


def scatter_head(quarters, beside=None):
    core = send(quarters[3], "head", CORE, 4)
    summed = (quarters[2].astype(f32) + core.astype(f32)).astype(bf16)
    across = send(summed, "head", ACROSS, 4)
    near = send(quarters[1], "head", CORE, 4)
    found = () if beside is None else beside(summed)
    return (quarters[0], near, after(across, found)), found


def gather_head(own, between=lambda near: ()):
    near = [own, send(own, "head", CORE, 4)]
    across = after(send(own, "head", ACROSS, 4), *between(near))
    return near + [across, send(across, "head", CORE, 4)]


def move_columns(cols_ref, in_ref, out_ref):
    width = in_ref.shape[1] // BLOCKS
    for block in range(BLOCKS):
        start = pl.multiple_of(cols_ref[block] * width, 128)
        out_ref[:, block * width : (block + 1) * width] = in_ref[:, pl.ds(start, width)].astype(out_ref.dtype)


def move_kernel(rows_ref, cols_ref, in_ref, out_ref):
    move_columns(cols_ref, in_ref, out_ref)


def move_blocks(array, row_blocks, col_blocks, quarter):
    width = array.shape[1]
    split = 2 if quarter % 32 == 0 else 1
    tile = quarter // split
    count = row_blocks.shape[0]
    return pl.pallas_call(
        move_kernel,
        out_shape=jax.ShapeDtypeStruct((count * quarter, width), array.dtype),
        grid_spec=pltpu.PrefetchScalarGridSpec(
            num_scalar_prefetch=2,
            grid=(count, split),
            in_specs=[pl.BlockSpec((tile, width), lambda i, j, rows, cols: (rows[i] * split + j, 0))],
            out_specs=pl.BlockSpec((tile, width), lambda i, j, rows, cols: (i * split + j, 0)),
        ),
        compiler_params=params(),
        cost_estimate=cost(0, 2 * count * quarter * width * array.dtype.itemsize),
    )(row_blocks, col_blocks, array)


def place_kernel(rows_ref, cols_ref, *refs):
    pieces, out_ref = refs[:2], refs[-1]
    for place, piece in enumerate(pieces):
        pl.when(pl.program_id(0) == place)(functools.partial(move_columns, cols_ref, piece, out_ref))


def place_quarters(pieces, row_blocks, col_blocks, out_type):
    quarter, width = pieces[0].shape
    shape = jax.ShapeDtypeStruct((4 * quarter, width), out_type)
    whole = None
    for start in (0, 2):
        held = [] if whole is None else [whole]
        whole = pl.pallas_call(
            place_kernel,
            out_shape=shape,
            grid_spec=pltpu.PrefetchScalarGridSpec(
                num_scalar_prefetch=2,
                grid=(2,),
                in_specs=[pl.BlockSpec((quarter, width), lambda i, rows, cols: (0, 0))] * 2
                + [pl.BlockSpec(memory_space=pl.ANY)] * len(held),
                out_specs=pl.BlockSpec((quarter, width), lambda i, rows, cols, start=start: (rows[start + i], 0)),
            ),
            input_output_aliases={4: 0} if held else {},
            compiler_params=params(40),
            cost_estimate=cost(0, shape.size * 4),
        )(row_blocks, col_blocks, *pieces[start : start + 2], *held)
    return whole


def unit_kernel(cols_ref, in_ref, out_ref):
    values = in_ref[...].astype(f32)
    rstd = lax.rsqrt(jnp.mean(values * values, axis=1, keepdims=True) + EPSILON)
    width = in_ref.shape[1] // BLOCKS
    for block in range(BLOCKS):
        start = pl.multiple_of(cols_ref[block] * width, 128)
        out_ref[:, block * width : (block + 1) * width] = (in_ref[:, pl.ds(start, width)].astype(f32) * rstd).astype(bf16)


def unit_rows(array, col_blocks, tile):
    rows, width = array.shape
    return pl.pallas_call(
        unit_kernel,
        out_shape=jax.ShapeDtypeStruct((rows, width), bf16),
        grid_spec=pltpu.PrefetchScalarGridSpec(
            num_scalar_prefetch=1,
            grid=(rows // tile,),
            in_specs=[pl.BlockSpec((tile, width), lambda i, cols: (i, 0))],
            out_specs=pl.BlockSpec((tile, width), lambda i, cols: (i, 0)),
        ),
        compiler_params=params(),
        cost_estimate=cost(0, 4 * rows * width),
    )(col_blocks, array)


def fit(rows):
    return next(tile for tile in (128, 96, 64, 48, 32, 16) if rows % tile == 0)


def add_norm_kernel(base_ref, a_ref, b_ref, c_ref, sum_ref, unit_ref):
    total = base_ref[...].astype(f32) + (a_ref[...].astype(f32) + b_ref[...].astype(f32) + c_ref[...].astype(f32))
    rstd = lax.rsqrt(jnp.mean(total * total, axis=1, keepdims=True) + EPSILON)
    sum_ref[...] = total
    unit_ref[...] = (total * rstd).astype(bf16)


def norm_back_kernel(base_ref, rest_ref, a_ref, b_ref, c_ref, *outs):
    base = base_ref[...].astype(f32)
    rstd = lax.rsqrt(jnp.mean(base * base, axis=1, keepdims=True) + EPSILON)
    unit = base * rstd
    grad = a_ref[...].astype(f32) + b_ref[...].astype(f32) + c_ref[...].astype(f32)
    total = rest_ref[...].astype(f32) + rstd * (grad - unit * jnp.mean(grad * unit, axis=1, keepdims=True))
    for out in outs:
        out[...] = total.astype(out.dtype)


def on_quarter(kernel, arrays, rows, out_types):
    width = arrays[0].shape[1]
    tile = fit(rows)
    spec = pl.BlockSpec((tile, width), lambda i: (i, 0))
    return pl.pallas_call(
        kernel,
        out_shape=[jax.ShapeDtypeStruct((rows, width), kind) for kind in out_types],
        grid=(rows // tile,),
        in_specs=[spec] * len(arrays),
        out_specs=[spec] * len(out_types),
        compiler_params=params(),
        cost_estimate=cost(0, rows * width * 16),
    )(*arrays)


def first_kernel(n, unit_ref, *refs):
    pieces, (out_ref, joined_ref, held_ref, sems) = refs[:n], refs[n:]
    rows = held_ref.shape[0] // n

    @pl.when(pl.program_id(0) == 0)
    def _():
        copies = [pltpu.make_async_copy(pieces[i], held_ref.at[pl.ds(i * rows, rows)], sems.at[i]) for i in range(n)]
        for copy in copies:
            copy.start()
        for copy in copies:
            copy.wait()
        joined_ref[...] = held_ref[...]

    out_ref[...] = nn(unit_ref[...], held_ref[...]).astype(bf16)


def first_product(unit, pieces, tile):
    tokens, width = unit.shape
    cols = pieces[0].shape[1]
    return pl.pallas_call(
        functools.partial(first_kernel, len(pieces)),
        out_shape=[jax.ShapeDtypeStruct((tokens, cols), bf16), jax.ShapeDtypeStruct((width, cols), bf16)],
        grid=(tokens // tile,),
        in_specs=[pl.BlockSpec((tile, width), lambda i: (i, 0))] + [pl.BlockSpec(memory_space=pl.ANY)] * len(pieces),
        out_specs=[pl.BlockSpec((tile, cols), lambda i: (i, 0)), pl.BlockSpec((width, cols), lambda i: (0, 0))],
        scratch_shapes=[pltpu.VMEM((width, cols), bf16), pltpu.SemaphoreType.DMA((len(pieces),))],
        compiler_params=params(),
        cost_estimate=cost(2 * tokens * width * cols, 2 * (tokens + width) * (width + cols)),
    )(unit, *pieces)


def quarter_kernel(order_ref, in_ref, weight_ref, *outs):
    values = in_ref[...]
    width = weight_ref.shape[0]
    for start in range(0, width, 512):
        part = nt(values, weight_ref[start : start + 512]).astype(bf16)
        for place, out in enumerate(outs):

            @pl.when(pl.program_id(0) == place)
            def _(out=out, part=part, start=start):
                out[:, start : start + 512] = part


def quarter_products(array, weight, quarters, top):
    width, cols = weight.shape
    rows = array.shape[0] // 4
    return pl.pallas_call(
        quarter_kernel,
        out_shape=[jax.ShapeDtypeStruct((rows, width), bf16)] * 2,
        grid_spec=pltpu.PrefetchScalarGridSpec(
            num_scalar_prefetch=1,
            grid=(2,),
            in_specs=[
                pl.BlockSpec((rows, cols), lambda i, order: (order[top - i], 0)),
                pl.BlockSpec((width, cols), lambda i, order: (0, 0), pipeline_mode=pl.Buffered(1)),
            ],
            out_specs=[pl.BlockSpec((rows, width), lambda i, order: (0, 0))] * 2,
        ),
        compiler_params=params(),
        cost_estimate=cost(4 * rows * width * cols, 4 * rows * width),
    )(quarters, array, weight)


def back_kernel(order_ref, *refs):
    pieces, weight_ref, out_ref = refs[:4], refs[4], refs[5]
    for place, piece in enumerate(pieces):

        @pl.when(pl.program_id(0) == place)
        def _(piece=piece):
            out_ref[...] = nn(piece[...], weight_ref[...]).astype(bf16)


def back_product(pieces, weight, quarters):
    rows, width = pieces[0].shape
    cols = weight.shape[1]
    return pl.pallas_call(
        back_kernel,
        out_shape=jax.ShapeDtypeStruct((4 * rows, cols), bf16),
        grid_spec=pltpu.PrefetchScalarGridSpec(
            num_scalar_prefetch=1,
            grid=(4,),
            in_specs=[pl.BlockSpec((rows, width), lambda i, order: (0, 0), pipeline_mode=pl.Buffered(1))] * 4
            + [pl.BlockSpec((width, cols), lambda i, order: (0, 0), pipeline_mode=pl.Buffered(1))],
            out_specs=pl.BlockSpec((rows, cols), lambda i, order: (order[i], 0)),
        ),
        compiler_params=params(),
        cost_estimate=cost(8 * rows * width * cols, 8 * rows * width),
    )(quarters, *pieces, weight)


def ffn_kernel(step, n_units, n_earlier, order_ref, *refs):
    units, dy_ref, weights_hbm = refs[:n_units], refs[n_units], refs[n_units + 1]
    earlier, refs = refs[n_units + 2 : n_units + 2 + n_earlier], refs[-8:]
    mixed_ref, ggate_ref, gup_ref, gunit_ref, out_ref, held_ref, unit_ref, sems = refs
    width, hidden = held_ref.shape[0], held_ref.shape[1] // 3
    rows = width // BLOCKS
    copies = []
    for i in range(BLOCKS):
        start = pl.multiple_of(order_ref[i] * rows, rows)
        source = weights_hbm.at[pl.ds(start, rows)]
        copies.append(pltpu.make_async_copy(source, held_ref.at[pl.ds(i * rows, rows)], sems.at[i]))

    @pl.when(pl.program_id(0) == 0)
    def _():
        for copy in copies:
            copy.start()
        for copy in copies:
            copy.wait()

    for place, unit in enumerate(units):

        @pl.when(pl.program_id(0) == place)
        def _(unit=unit):
            unit_ref[...] = unit[...]

    unit, dy = unit_ref[...], dy_ref[...]
    for start in range(0, hidden, step):
        stop = min(start + step, hidden)
        cols = slice(start, stop)
        gate = nn(unit, held_ref[:, start:stop])
        up = nn(unit, held_ref[:, hidden + start : hidden + stop])
        gmixed = nn(dy, held_ref[:, 2 * hidden + start : 2 * hidden + stop])
        sig = jax.nn.sigmoid(gate)
        silu = gate * sig
        mixed_ref[:, cols] = (silu * up).astype(bf16)
        ggate_ref[:, cols] = (gmixed * up * (sig * (1.0 + gate * (1.0 - sig)))).astype(bf16)
        gup_ref[:, cols] = (gmixed * silu).astype(bf16)
    ggate, gup, mixed = ggate_ref[...], gup_ref[...], mixed_ref[...]
    for start in range(0, width, 512):
        cols = slice(start, start + 512)
        gunit = nt(ggate, held_ref[cols, :hidden]) + nt(gup, held_ref[cols, hidden : 2 * hidden])
        out = nt(mixed, held_ref[cols, 2 * hidden :])
        if earlier:
            gunit = gunit + earlier[0][0, :, cols].astype(f32)
            out = out + earlier[1][0, :, cols].astype(f32)
        gunit_ref[0, :, cols] = gunit.astype(bf16)
        out_ref[0, :, cols] = out.astype(bf16)


def feed_forward(units, dy, start, weights, hidden, order, held=(), earlier=()):
    rows, width = units[0].shape
    line = lambda cols: pl.BlockSpec((rows, cols), lambda i, order: (i + start, 0))
    stacked = pl.BlockSpec((1, rows, width), lambda i, order: (i + start, 0, 0))
    shapes = [jax.ShapeDtypeStruct((4 * rows, hidden), bf16)] * 3 + [jax.ShapeDtypeStruct((4, rows, width), bf16)] * 2
    once = pl.BlockSpec((rows, width), lambda i, order: (0, 0), pipeline_mode=pl.Buffered(1))
    anywhere = pl.BlockSpec(memory_space=pl.ANY)
    steps = len(units)
    first = 3 + steps + len(earlier)
    return pl.pallas_call(
        functools.partial(ffn_kernel, 256, steps, len(earlier)),
        out_shape=shapes,
        grid_spec=pltpu.PrefetchScalarGridSpec(
            num_scalar_prefetch=1,
            grid=(steps,),
            in_specs=[once] * steps + [line(width), anywhere] + [stacked] * len(earlier) + [anywhere] * len(held),
            out_specs=[line(hidden)] * 3 + [stacked] * 2,
            scratch_shapes=[
                pltpu.VMEM((width, 3 * hidden), bf16),
                pltpu.VMEM((rows, width), bf16),
                pltpu.SemaphoreType.DMA((BLOCKS,)),
            ],
        ),
        input_output_aliases={first + i: i for i in range(len(held))},
        compiler_params=params(60),
        cost_estimate=cost(12 * steps * rows * width * hidden, 2 * (4 * steps * rows + 3 * hidden) * width),
    )(order, *units, dy, weights, *earlier, *held)


def weight_kernel(layout, order_ref, quarters_ref, *refs):
    refs, out = list(refs[:-1]), refs[-1]
    total = None
    for n_left, n_right in layout:
        lefts, rights = [refs.pop(0)[...] for _ in range(n_left)], [refs.pop(0)[...] for _ in range(n_right)]
        left, right = [jnp.concatenate(item, axis=0) if len(item) > 1 else item[0] for item in (lefts, rights)]
        part = nn(left.T, right)
        total = part if total is None else total + part
    out[...] = total.astype(bf16)


def weight_grads(parts, order, quarters):
    width = parts[0][0][0][0].shape[1]
    rows = width // BLOCKS
    cols = parts[0][1][0][0].shape[1]
    arrays, specs, tokens = [], [], 0
    for pieces in parts:
        for side, side_pieces in enumerate(pieces):
            for array, *place in side_pieces:
                n = array.shape[0] // (1 if not place else 4 if place[0] == "q" else 2)

                def index(i, order, quarters, side=side, place=tuple(place)):
                    row = 0 if not place else quarters[place[1]] if place[0] == "q" else place[0]
                    return (row, 0 if side else i)

                mode = {"pipeline_mode": pl.Buffered(1)} if side else {}
                specs.append(pl.BlockSpec((n, cols if side else rows), index, **mode))
                arrays.append(array)
                tokens += n if side else 0
    return pl.pallas_call(
        functools.partial(weight_kernel, tuple((len(lefts), len(rights)) for lefts, rights in parts)),
        out_shape=jax.ShapeDtypeStruct((width, cols), bf16),
        grid_spec=pltpu.PrefetchScalarGridSpec(
            num_scalar_prefetch=2,
            grid=(BLOCKS,),
            in_specs=specs,
            out_specs=pl.BlockSpec((rows, cols), lambda i, order, quarters: (order[i], 0)),
        ),
        compiler_params=params(48),
        cost_estimate=cost(2 * tokens * width * cols, 2 * (tokens + width) * (width + cols)),
    )(order, quarters, *arrays)


def ffn_weight_kernel(order_ref, *refs):
    units, (dy_ref, mixed_ref, ggate_ref, gup_ref, out) = refs[:4], refs[4:]
    cols = ggate_ref.shape[1]
    unit = jnp.concatenate([item[...] for item in units], axis=0).T
    out[:, :cols] = nn(unit, ggate_ref[...]).astype(bf16)
    out[:, cols : 2 * cols] = nn(unit, gup_ref[...]).astype(bf16)
    out[:, 2 * cols :] = nn(dy_ref[...].T, mixed_ref[...]).astype(bf16)


def ffn_weight_grads(units, dy, grads, order):
    quarter, width = units[0].shape
    rows = width // BLOCKS
    cols = grads[0].shape[1]
    held = pl.BlockSpec((4 * quarter, cols), lambda i, order: (0, 0), pipeline_mode=pl.Buffered(1))
    return pl.pallas_call(
        ffn_weight_kernel,
        out_shape=jax.ShapeDtypeStruct((width, 3 * cols), bf16),
        grid_spec=pltpu.PrefetchScalarGridSpec(
            num_scalar_prefetch=1,
            grid=(BLOCKS,),
            in_specs=[pl.BlockSpec((quarter, rows), lambda i, order: (0, i))] * 4
            + [pl.BlockSpec((4 * quarter, rows), lambda i, order: (0, i))]
            + [held] * 3,
            out_specs=pl.BlockSpec((rows, 3 * cols), lambda i, order: (order[i], 0)),
        ),
        compiler_params=params(48),
        cost_estimate=cost(24 * quarter * width * cols, 2 * (8 * quarter + width) * (width + 3 * cols)),
    )(order, *units, dy, *grads)


def per_device(
    n_seq,
    n_head,
    tokens,
    doc_reset,
    gain_attn,
    gain_ffn,
    query_weight,
    key_weight,
    value_weight,
    out_weight,
    gate_weight,
    up_weight,
    down_weight,
    grad_out,
):
    rows, length, width = tokens.shape
    heads = query_weight.shape[1] // FEAT
    count = rows * length
    quarter = count // 4
    half = 2 * quarter
    me = lax.axis_index("seq").astype(jnp.int32)
    head_me = lax.axis_index("head").astype(jnp.int32)
    order = jnp.arange(BLOCKS, dtype=jnp.int32)
    if n_seq == 8:
        order = me ^ order
    quarters = head_me ^ jnp.arange(4, dtype=jnp.int32)

    gain_one = gain_attn.astype(f32)[:, None]
    gain_two = gain_ffn.astype(f32)[:, None]
    scaled = lambda weight, gain: (weight.astype(f32) * gain).astype(bf16)
    qkv_own = jnp.concatenate([query_weight, key_weight, value_weight], axis=1)
    gate_own, up_own, down_own = scaled(gate_weight, gain_two), scaled(up_weight, gain_two), down_weight.T
    hidden_units = gate_weight.shape[1]
    cut = (hidden_units + VHEAD) // (2 * VHEAD) * VHEAD
    groups = (slice(0, cut), slice(cut, hidden_units))
    values = heads * VHEAD
    qkv_pieces = gather_rows(scaled(qkv_own, gain_one), n_seq)
    everywhere = lambda value: lax.all_gather(value, "seq", axis=0, tiled=True)
    out_w = everywhere(out_weight.T)
    ffn_w = []
    for group in groups:
        parts = [gate_own[:, group], up_own[:, group], down_own[:, group]]
        ffn_w.append(everywhere(jnp.concatenate(parts, axis=1)))
    out_w = swap_blocks(out_w, order)

    flat = tokens.reshape(count, width)
    x_own = move_blocks(flat, quarters[:1], order, quarter)
    dy = move_blocks(grad_out.reshape(count, width), quarters, order, quarter)
    unit_one = after(unit_rows(flat, order, quarter // 2), x_own, dy)

    docs = jnp.cumsum(doc_reset, axis=1)
    final = docs[:, -1:]
    flag = jnp.broadcast_to(final > 0, docs.shape)
    edges = jnp.stack([docs, docs == 0, docs == final, flag] + [jnp.zeros_like(docs)] * 4, axis=2).astype(f32)
    doc_rows = jnp.broadcast_to(docs[:, None, :], (rows, 8, length)).astype(f32)
    tables, feat_rows, to_key, to_query = feature_tables(heads)

    lanes = 2 * heads * FEAT
    unit_flops = 2 * rows * heads * length * WIDE * VHEAD
    qkv, qkv_w = first_product(unit_one, qkv_pieces, quarter)
    qkv = qkv.reshape(rows, length, lanes + values)
    (states,) = by_row(
        functools.partial(state_kernel, heads),
        rows,
        [(qkv, True), (edges, True), (tables["ka"], False), (tables["kb"], False), (feat_rows, False)],
        [((heads, TALL, VHEAD), bf16)],
        flops=3 * unit_flops,
    )
    numerator, denominator = by_row(
        functools.partial(inside_kernel, heads),
        rows,
        [(qkv, True), (edges, True), (doc_rows, True), (to_key, False)],
        [((length, values), f32), ((length, heads), f32)],
        flops=3 * unit_flops,
    )
    found = scan_begin(states, False, me, n_seq, (numerator,))
    state_in, place = scan_end(found, False, me, n_seq)
    query_tables = [(tables["qa"], False), (tables["qb"], False), (feat_rows, False)]
    key_tables = [(tables["ka"], False), (tables["kb"], False), (feat_rows, False)]
    attended, rden = by_row(
        functools.partial(attend_kernel, heads),
        rows,
        [(qkv, True), (edges, True), (numerator, True), (after(denominator, out_w), True), (state_in, False)]
        + query_tables,
        [((length, values), bf16), ((length, heads), f32)],
        place=place,
        flops=3 * unit_flops,
    )
    attended_flat = attended.reshape(count, values)
    far = quarter_products(attended_flat, out_w, quarters, 3)
    near = quarter_products(attended_flat, out_w, quarters, 1)
    branch = [near[1], near[0], far[1], far[0]]

    branch, _ = scatter_head(branch)
    hidden, unit_two = on_quarter(add_norm_kernel, [x_own, *branch], quarter, [f32, bf16])
    held = []

    def near_rows(units):
        held.extend(feed_forward(units, dy, 0, ffn_w[0], cut, order))
        return held

    units = gather_head(unit_two, near_rows)
    first = feed_forward(units[2:], dy, 2, ffn_w[0], cut, order, held)
    seq_sum = lambda value: lax.psum_scatter(value, "seq", scatter_dimension=0, tiled=True).astype(f32)
    first_grads = ffn_weight_grads(units, dy, first[:3], order)
    ffn_grads = [seq_sum(first_grads)]
    left = [after(units[0], first_grads), *units[1:]]
    second = feed_forward(left, dy, 0, ffn_w[1], hidden_units - cut, order, earlier=first[3:])
    gunit, ffn_out = [[item[i] for i in range(4)] for item in second[3:]]

    def second_grads(sent):
        return ffn_weight_grads([after(units[0], sent), *units[1:]], dy, second[:3], order)

    terms, found = scatter_head(gunit, beside=second_grads)
    grad_hidden, grad_branch = on_quarter(norm_back_kernel, [hidden, dy, *terms], quarter, [f32, bf16])
    ffn_grads.append(seq_sum(after(found, grad_hidden)))
    grad_branch = gather_head(grad_branch)

    grad_att = back_product(grad_branch, out_w, quarters).reshape(rows, length, values)
    carry, gnum, gden = by_row(
        functools.partial(carry_kernel, heads),
        rows,
        [(qkv, True), (edges, True), (grad_att, True), (attended, True), (rden, True)] + query_tables,
        [((heads, TALL, VHEAD), bf16), ((length, values), bf16), ((length, heads), f32)],
        flops=3 * unit_flops,
    )
    gboth, gval = by_row(
        functools.partial(inside_back_kernel, heads),
        rows,
        [(qkv, True), (edges, True), (doc_rows, True), (gnum, True), (gden, True), (state_in, False)]
        + [(to_key, False), (to_query, False)]
        + query_tables,
        [((length, lanes), f32), ((length, values), f32)],
        place=place,
        flops=11 * unit_flops,
    )
    sides = [[(grad_branch[i],), (grad_branch[i + 1],)] for i in (0, 2)]
    parts = [(side, [(attended_flat, "q", i), (attended_flat, "q", i + 1)]) for side, i in zip(sides, (0, 2))]
    grad_out_w = weight_grads(parts, order, quarters)
    found = scan_begin(carry, True, me, n_seq, (gboth, grad_out_w))
    ffn_out[3] = after(ffn_out[3], grad_att)
    terms, _ = scatter_head(ffn_out, beside=lambda _: found)
    block_own = (hidden + (terms[0].astype(f32) + terms[1].astype(f32) + terms[2].astype(f32))).astype(bf16)
    carry_in, place_back = scan_end(found, True, me, n_seq)
    carry_in = after(carry_in, block_own)
    block_all = gather_head(block_own, lambda near: (carry_in,))
    (gqkv,) = by_row(
        functools.partial(finish_back_kernel, heads),
        rows,
        [(qkv, True), (edges, True), (carry_in, False), (gboth, True), (gval, True)] + key_tables,
        [((length, lanes + values), bf16)],
        place=place_back,
        flops=6 * unit_flops,
    )
    gqkv = after(gqkv.reshape(count, lanes + values), *block_all)
    back = lambda value, kind: place_quarters(value, quarters, order, kind).reshape(rows, length, width)

    def sum_head(value):
        value = jnp.broadcast_to(value, (8, width // n_seq))
        pairs = [send(value, "head", mask, 4) for mask in (1, 2, 3)]
        return ((value + pairs[0]) + (pairs[1] + pairs[2]))[0]

    def ffn_outputs(sums):
        parts = [jnp.split(item, 3, axis=1) for item in sums]
        grad_gate, grad_up, grad_down = [jnp.concatenate(items, axis=1) for items in zip(*parts)]
        gain = jnp.sum(gate_weight.astype(f32) * grad_gate + up_weight.astype(f32) * grad_up, axis=1)
        return (grad_gate * gain_two, grad_up * gain_two, grad_down.T), sum_head(gain)

    grad_out_w = seq_sum(grad_out_w)
    far = quarter_products(gqkv, qkv_w, quarters, 3)
    near = quarter_products(gqkv, qkv_w, quarters, 1)
    terms, grad_qkv = scatter_head(
        [near[1], near[0], far[1], far[0]],
        beside=lambda sent: weight_grads(
            [([(after(unit_one, sent),)], [(gqkv,)])], split_order(order, n_seq), quarters
        ),
    )
    (grad_x,) = on_quarter(norm_back_kernel, [x_own, grad_hidden, *terms], quarter, [bf16])
    qkv_pairs = scatter_begin(grad_qkv, n_seq)
    ffn_grads, ffn_gain = ffn_outputs(after(ffn_grads, grad_x))
    block_all = back(block_all, bf16)
    grad_x_all = gather_head(grad_x, lambda near: (block_all, ffn_gain, *ffn_grads, *qkv_pairs))
    qkv_terms = scatter_sends(qkv_pairs)
    grad_x_all[0] = after(grad_x_all[0], *qkv_terms)
    grad_x_all = back(grad_x_all, f32)
    grad_out_w = after(grad_out_w, grad_x_all)
    grad_qkv = scatter_end(qkv_pairs, qkv_terms)
    qkv_gain = sum_head(jnp.sum(qkv_own.astype(f32) * grad_qkv, axis=1))
    grad_qkv = grad_qkv * gain_one
    narrow = heads * FEAT
    return (
        block_all,
        grad_x_all,
        qkv_gain,
        ffn_gain,
        grad_qkv[:, :narrow],
        grad_qkv[:, narrow:lanes],
        grad_qkv[:, lanes:],
        grad_out_w.T,
        *ffn_grads,
    )


def solution(mesh):
    placed = (
        P(None, "seq", None),
        P(None, "seq"),
        P("seq"),
        P("seq"),
        P("seq", "head"),
        P("seq", "head"),
        P("seq", "head"),
        P("head", "seq"),
        P("seq", "head"),
        P("seq", "head"),
        P("head", "seq"),
        P(None, "seq", None),
    )
    return jax.shard_map(
        functools.partial(per_device, mesh.shape["seq"], mesh.shape["head"]),
        mesh=mesh,
        in_specs=placed,
        out_specs=(P(None, "seq", None), P(None, "seq", None)) + placed[2:11],
        check_vma=False,
    )
```

```python
import functools

import jax
import jax.numpy as jnp
import numpy as np
from jax import lax
from jax.experimental import pallas as pl
from jax.experimental.pallas import tpu as pltpu
from jax.sharding import PartitionSpec as P

FEAT = 16
VHEAD = 128
EPSILON = 1e-06
PAIRS = [(a, b) for a in range(FEAT + 1) for b in range(a, FEAT + 1)]
WIDE = 256
TALL = 160
NORM_ROW = len(PAIRS)
FLAG_ROW = NORM_ROW + 2
BLOCKS = 8
COST = 2
bf16, f32 = jnp.bfloat16, jnp.float32


def feature_tables(heads):
    lanes = 2 * heads * FEAT
    tables = {name: np.zeros((lanes, heads * WIDE), np.float32) for name in ("qa", "qb", "ka", "kb")}
    rows = np.zeros((8, heads * WIDE), np.float32)
    to_key = np.zeros((lanes, heads * lanes), np.float32)
    to_query = np.zeros((lanes, heads * lanes), np.float32)
    for head in range(heads):
        for place, (a, b) in enumerate(PAIRS):
            column = head * WIDE + place
            for name, entry, row in (("a", a, 0), ("b", b, 1)):
                if entry == 0:
                    rows[row, column] = 1.0
                else:
                    lane = head * FEAT + entry - 1
                    tables["q" + name][lane, column] = 1.0
                    tables["k" + name][heads * FEAT + lane, column] = 1.0
            rows[2, column] = 1.0 if b == 0 else 0.25 if a == 0 else 1 / 32 if a == b else 1 / 16
        for feat in range(FEAT):
            lane = head * FEAT + feat
            to_key[lane, head * lanes + heads * FEAT + lane] = 0.25
            to_query[heads * FEAT + lane, head * lanes + lane] = 0.25
    tables = {name: jnp.asarray(item, bf16) for name, item in tables.items()}
    return tables, jnp.asarray(rows), jnp.asarray(to_key, bf16), jnp.asarray(to_query, bf16)


def nn(left, right):
    return lax.dot_general(left, right, (((1,), (0,)), ((), ())), preferred_element_type=f32)


def nt(left, right):
    return lax.dot_general(left, right, (((1,), (1,)), ((), ())), preferred_element_type=f32)


def tn(left, right):
    return lax.dot_general(left, right, (((0,), (0,)), ((), ())), preferred_element_type=f32)


def params(mib=32):
    return pltpu.CompilerParams(vmem_limit_bytes=mib << 20)


def cost(flops, nbytes):
    return pl.CostEstimate(flops=int(flops) // COST, bytes_accessed=int(nbytes) // COST, transcendentals=0)


def whole_spec(array):
    zeros = (0,) * array.ndim
    return pl.BlockSpec(array.shape, lambda *_: zeros)


def row_spec(array):
    zeros = (0,) * (array.ndim - 1)
    return pl.BlockSpec((1,) + array.shape[1:], lambda row, *_: (row,) + zeros)


def pack_state(state, norm_row, flag):
    place = lax.broadcasted_iota(jnp.int32, (TALL, VHEAD), 0)
    block = state[:TALL]
    block = jnp.where(place == NORM_ROW, norm_row[:, :VHEAD], block)
    block = jnp.where(place == NORM_ROW + 1, norm_row[:, VHEAD:], block)
    return jnp.where(place == FLAG_ROW, flag, block).astype(bf16)


def unpack_state(block):
    tail = block[TALL - 16 :].astype(f32)
    base = TALL - 16
    low = tail[NORM_ROW - base : NORM_ROW - base + 1]
    high = tail[NORM_ROW + 1 - base : NORM_ROW + 2 - base]
    full = jnp.concatenate([block, jnp.zeros((WIDE - TALL, VHEAD), block.dtype)], axis=0)
    return full, jnp.concatenate([low, high], axis=1)


def state_kernel(heads, qkv_ref, edge_ref, ka_ref, kb_ref, rows_ref, out_ref):
    keys = qkv_ref[0, :, : 2 * heads * FEAT]
    edges = edge_ref[0]
    last, flag = edges[:, 2:3], edges[0:1, 3:4]
    for head in range(heads):
        cols = slice(head * WIDE, (head + 1) * WIDE)
        phi = (nn(keys, ka_ref[:, cols]) + rows_ref[0:1, cols]) * (nn(keys, kb_ref[:, cols]) + rows_ref[1:2, cols])
        phi = phi * last
        start = 2 * heads * FEAT + head * VHEAD
        state = tn(phi.astype(bf16), qkv_ref[0, :, start : start + VHEAD])
        out_ref[0, head] = pack_state(state, jnp.sum(phi, axis=0, keepdims=True), flag)


def local_mask(edges, docs):
    length = edges.shape[0]
    later = lax.broadcasted_iota(jnp.int32, (length, length), 0) >= lax.broadcasted_iota(jnp.int32, (length, length), 1)
    return later & (edges[:, 0:1] == docs)


def inside_kernel(heads, qkv_ref, edge_ref, doc_ref, key_ref, num_ref, den_ref):
    lanes = 2 * heads * FEAT
    both = qkv_ref[0, :, :lanes]
    mask = local_mask(edge_ref[0], doc_ref[0, 0:1])
    moved = nn(both, key_ref[...]).astype(bf16)
    dens = []
    for head in range(heads):
        scores = nt(moved[:, head * lanes : (head + 1) * lanes], both)
        weights = jnp.where(mask, 1.0 + scores + 0.5 * scores * scores, 0.0)
        dens.append(jnp.sum(weights, axis=1, keepdims=True))
        start = lanes + head * VHEAD
        num_ref[0, :, head * VHEAD : (head + 1) * VHEAD] = nn(
            weights.astype(bf16), qkv_ref[0, :, start : start + VHEAD]
        )
    den_ref[0] = jnp.concatenate(dens, axis=1)


def block_at(place_ref, states_ref, row, heads, head):
    per = states_ref.shape[1]
    index = row * heads + head
    return states_ref[place_ref[index // per], index % per]


def query_features(both, qa, qb, rows, first):
    left = nn(both, qa) + rows[0:1]
    right = nn(both, qb) + rows[1:2]
    return left, right, left * right * rows[2:3] * first


def attend_kernel(heads, place_ref, qkv_ref, edge_ref, num_ref, den_ref, states_ref, qa_ref, qb_ref, rows_ref, att_ref, rden_ref):
    both = qkv_ref[0, :, : 2 * heads * FEAT]
    first = edge_ref[0][:, 1:2]
    rdens = []
    for head in range(heads):
        cols = slice(head * WIDE, (head + 1) * WIDE)
        _, _, phi = query_features(both, qa_ref[:, cols], qb_ref[:, cols], rows_ref[:, cols], first)
        factor, norm = unpack_state(block_at(place_ref, states_ref, pl.program_id(0), heads, head))
        den = den_ref[0][:, head : head + 1] + jnp.sum(phi * norm, axis=1, keepdims=True)
        rden = 1.0 / den
        out = slice(head * VHEAD, (head + 1) * VHEAD)
        att_ref[0, :, out] = ((num_ref[0, :, out] + nn(phi.astype(bf16), factor)) * rden).astype(bf16)
        rdens.append(rden)
    rden_ref[0] = jnp.concatenate(rdens, axis=1)


def carry_kernel(heads, qkv_ref, edge_ref, ga_ref, att_ref, rden_ref, qa_ref, qb_ref, rows_ref, carry_ref, gnum_ref, gden_ref):
    both = qkv_ref[0, :, : 2 * heads * FEAT]
    edges = edge_ref[0]
    first, flag = edges[:, 1:2], edges[0:1, 3:4]
    gdens = []
    for head in range(heads):
        cols = slice(head * WIDE, (head + 1) * WIDE)
        out = slice(head * VHEAD, (head + 1) * VHEAD)
        _, _, phi = query_features(both, qa_ref[:, cols], qb_ref[:, cols], rows_ref[:, cols], first)
        grad = ga_ref[0, :, out].astype(f32)
        rden = rden_ref[0][:, head : head + 1]
        gnum = (grad * rden).astype(bf16)
        gden = -jnp.sum(grad * att_ref[0, :, out].astype(f32), axis=1, keepdims=True) * rden
        gnum_ref[0, :, out] = gnum
        carry_ref[0, head] = pack_state(
            tn(phi.astype(bf16), gnum), jnp.sum(phi * gden, axis=0, keepdims=True), flag
        )
        gdens.append(gden)
    gden_ref[0] = jnp.concatenate(gdens, axis=1)


def inside_back_kernel(
    heads, place_ref, qkv_ref, edge_ref, doc_ref, gnum_ref, gden_ref, states_ref, key_ref, query_ref, qa_ref, qb_ref,
    rows_ref, gboth_ref, gval_ref,
):
    lanes = 2 * heads * FEAT
    both = qkv_ref[0, :, :lanes]
    edges = edge_ref[0]
    first = edges[:, 1:2]
    mask = local_mask(edges, doc_ref[0, 0:1])
    moved = nn(both, key_ref[...]).astype(bf16)
    back = nn(both, query_ref[...]).astype(bf16)
    total = jnp.zeros((both.shape[0], lanes), f32)
    for head in range(heads):
        cols = slice(head * WIDE, (head + 1) * WIDE)
        out = slice(head * VHEAD, (head + 1) * VHEAD)
        own = slice(head * lanes, (head + 1) * lanes)
        start = lanes + head * VHEAD
        values = qkv_ref[0, :, start : start + VHEAD]
        gnum = gnum_ref[0, :, out]
        gden = gden_ref[0][:, head : head + 1]
        scores = nt(moved[:, own], both)
        weights = jnp.where(mask, 1.0 + scores + 0.5 * scores * scores, 0.0).astype(bf16)
        gval_ref[0, :, out] = tn(weights, gnum)
        gscores = jnp.where(mask, (nt(gnum, values) + gden) * (1.0 + scores), 0.0).astype(bf16)
        total = total + nn(gscores, back[:, own]) + tn(gscores, moved[:, own])
        left, right, _ = query_features(both, qa_ref[:, cols], qb_ref[:, cols], rows_ref[:, cols], first)
        factor, norm = unpack_state(block_at(place_ref, states_ref, pl.program_id(0), heads, head))
        place = lax.broadcasted_iota(jnp.int32, (1, WIDE), 1)
        gphi = jnp.where(place < NORM_ROW, (nt(gnum, factor) + norm * gden) * rows_ref[2:3, cols], 0.0) * first
        total = total + nt((gphi * right).astype(bf16), qa_ref[:, cols]) + nt((gphi * left).astype(bf16), qb_ref[:, cols])
    gboth_ref[0] = total


def finish_back_kernel(
    heads, place_ref, qkv_ref, edge_ref, carry_ref, gboth_ref, gval_ref, ka_ref, kb_ref, rows_ref, out_ref
):
    lanes = 2 * heads * FEAT
    both = qkv_ref[0, :, :lanes]
    last = edge_ref[0][:, 2:3]
    total = gboth_ref[0]
    for head in range(heads):
        cols = slice(head * WIDE, (head + 1) * WIDE)
        start = lanes + head * VHEAD
        values = qkv_ref[0, :, start : start + VHEAD]
        left = nn(both, ka_ref[:, cols]) + rows_ref[0:1, cols]
        right = nn(both, kb_ref[:, cols]) + rows_ref[1:2, cols]
        factor, norm = unpack_state(block_at(place_ref, carry_ref, pl.program_id(0), heads, head))
        phi = (left * right * last).astype(bf16)
        gval = gval_ref[0, :, head * VHEAD : (head + 1) * VHEAD] + nn(phi, factor)
        out_ref[0, :, start : start + VHEAD] = gval.astype(bf16)
        place = lax.broadcasted_iota(jnp.int32, (1, WIDE), 1)
        gphi = jnp.where(place < NORM_ROW, nt(values, factor) + norm, 0.0) * last
        total = total + nt((gphi * right).astype(bf16), ka_ref[:, cols]) + nt((gphi * left).astype(bf16), kb_ref[:, cols])
    out_ref[0, :, :lanes] = total.astype(bf16)


def by_row(kernel, rows, inputs, outputs, place=None, flops=0):
    arrays = [array for array, _ in inputs]
    specs = [row_spec(array) if per_row else whole_spec(array) for array, per_row in inputs]
    shapes = [jax.ShapeDtypeStruct((rows,) + shape, kind) for shape, kind in outputs]
    nbytes = sum(item.size * item.dtype.itemsize for item in arrays + shapes)
    return pl.pallas_call(
        kernel,
        out_shape=shapes,
        grid_spec=pltpu.PrefetchScalarGridSpec(
            num_scalar_prefetch=0 if place is None else 1,
            grid=(rows,),
            in_specs=specs,
            out_specs=[row_spec(shape) for shape in shapes],
        ),
        compiler_params=params(40),
        cost_estimate=cost(flops, nbytes),
    )(*([] if place is None else [place]), *arrays)


def scan_kernel(backward, me_ref, *refs):
    pieces, outs, (held, ahead) = refs[:8], refs[8:16], refs[16:]
    for rel in range(8):
        held[rel] = pieces[rel][...]
    me = me_ref[0]
    for block in range(held.shape[1]):
        run = jnp.zeros(held.shape[2:], f32)
        for step in range(8):
            rel = me ^ (7 - step if backward else step)
            ahead[rel, block] = run.astype(bf16)
            own = held[rel, block].astype(f32)
            run = own + (1.0 - own[FLAG_ROW : FLAG_ROW + 1]) * run
    for rel in range(8):
        outs[rel][...] = ahead[rel]


def scan_begin(states, backward, me, count, earlier=()):
    blocks = states.shape[0] * states.shape[1]
    flat = states.reshape(blocks, TALL, VHEAD)
    if count != 8 or blocks % 8:
        return lax.all_gather(flat, "seq").astype(f32)
    per = blocks // 8
    split = flat.reshape(8, per, TALL, VHEAD)
    parts = [lax.dynamic_index_in_dim(split, me ^ rel, 0, keepdims=False) for rel in range(8)]
    pieces = [after(parts[0], *earlier)] + [send(parts[rel], "seq", rel, 8) for rel in range(1, 8)]
    return pl.pallas_call(
        functools.partial(scan_kernel, backward),
        out_shape=[jax.ShapeDtypeStruct((per, TALL, VHEAD), bf16)] * 8,
        in_specs=[pl.BlockSpec(memory_space=pltpu.SMEM)] + [pl.BlockSpec(memory_space=pltpu.VMEM)] * 8,
        out_specs=[pl.BlockSpec(memory_space=pltpu.VMEM)] * 8,
        scratch_shapes=[pltpu.VMEM((8, per, TALL, VHEAD), bf16)] * 2,
        compiler_params=params(),
    )(me.reshape(1), *pieces)


def scan_end(found, backward, me, count):
    if isinstance(found, (list, tuple)):
        back = [found[0]] + [send(found[rel], "seq", rel, 8) for rel in range(1, 8)]
        return jnp.stack(back), me ^ jnp.arange(8, dtype=jnp.int32)
    keep = 1.0 - found[:, :, FLAG_ROW : FLAG_ROW + 1]
    run = jnp.zeros(found.shape[1:], f32)
    for step in range(count):
        at = count - 1 - step if backward else step
        reached = at > me if backward else at < me
        run = jnp.where(reached, found[at] + keep[at] * run, run)
    return run.astype(bf16)[None], jnp.zeros((1,), jnp.int32)


def send(value, axis, mask, count):
    return lax.ppermute(value, axis, [(i, i ^ mask) for i in range(count)])


def gather_rows(shard, count):
    if count != 8:
        return [lax.all_gather(shard, "seq", axis=0, tiled=True)]
    pieces = [shard, send(shard, "seq", 1, 8)]
    for mask in (2, 4, 6):
        piece = send(shard, "seq", mask, 8)
        pieces += [piece, send(piece, "seq", 1, 8)]
    return pieces


def after(value, *earlier):
    return lax.optimization_barrier((value, earlier))[0]


def swap_blocks(array, order):
    split = array.reshape((BLOCKS, array.shape[0] // BLOCKS) + array.shape[1:])
    return join_rows([lax.dynamic_index_in_dim(split, order[i], 0, keepdims=False) for i in range(BLOCKS)])


def split_order(order, n_seq):
    return jnp.array([0, 4, 1, 5, 2, 6, 3, 7], jnp.int32) if n_seq == 8 else order


def scatter_begin(whole, n_seq):
    if n_seq != 8:
        return (lax.psum_scatter(whole, "seq", scatter_dimension=0, tiled=True).astype(f32),)
    rows = whole.shape[0] // 8
    other = send(whole[4 * rows :], "seq", 1, 8)
    pairs = [
        whole[i * rows : (i + 1) * rows].astype(f32) + other[i * rows : (i + 1) * rows].astype(f32) for i in range(4)
    ]
    return (pairs[0],) + tuple(pair.astype(bf16) for pair in pairs[1:])


def scatter_sends(pairs):
    return [send(pair, "seq", 2 * place + 2, 8) for place, pair in enumerate(pairs[1:])]


def scatter_end(pairs, terms):
    total = pairs[0]
    for term in terms:
        total = total + term.astype(f32)
    return total


def join_rows(pieces):
    return pieces[0] if len(pieces) == 1 else jnp.concatenate(pieces, axis=0)


CORE, ACROSS = 1, 2


def scatter_core(quarters):
    return (quarters[2].astype(f32) + send(quarters[3], "head", CORE, 4).astype(f32)).astype(bf16)


def scatter_head(quarters, beside=None, summed=None):
    summed = scatter_core(quarters) if summed is None else summed
    across = send(summed, "head", ACROSS, 4)
    near = send(quarters[1], "head", CORE, 4)
    found = () if beside is None else beside(summed)
    return (quarters[0], near, after(across, found)), found


def gather_head(own, between=lambda near: ()):
    near = [own, send(own, "head", CORE, 4)]
    across = after(send(own, "head", ACROSS, 4), *between(near))
    return near + [across, send(across, "head", CORE, 4)]


def move_columns(cols_ref, in_ref, out_ref):
    width = in_ref.shape[1] // BLOCKS
    for block in range(BLOCKS):
        start = pl.multiple_of(cols_ref[block] * width, 128)
        out_ref[:, block * width : (block + 1) * width] = in_ref[:, pl.ds(start, width)].astype(out_ref.dtype)


def move_kernel(rows_ref, cols_ref, in_ref, out_ref):
    move_columns(cols_ref, in_ref, out_ref)


def move_blocks(array, row_blocks, col_blocks, quarter):
    width = array.shape[1]
    split = 2 if quarter % 32 == 0 else 1
    tile = quarter // split
    count = row_blocks.shape[0]
    return pl.pallas_call(
        move_kernel,
        out_shape=jax.ShapeDtypeStruct((count * quarter, width), array.dtype),
        grid_spec=pltpu.PrefetchScalarGridSpec(
            num_scalar_prefetch=2,
            grid=(count, split),
            in_specs=[pl.BlockSpec((tile, width), lambda i, j, rows, cols: (rows[i] * split + j, 0))],
            out_specs=pl.BlockSpec((tile, width), lambda i, j, rows, cols: (i * split + j, 0)),
        ),
        compiler_params=params(),
        cost_estimate=cost(0, 2 * count * quarter * width * array.dtype.itemsize),
    )(row_blocks, col_blocks, array)


def place_kernel(rows_ref, cols_ref, *refs):
    pieces, out_ref = refs[:2], refs[-1]
    for place, piece in enumerate(pieces):
        pl.when(pl.program_id(0) == place)(functools.partial(move_columns, cols_ref, piece, out_ref))


def place_quarters(pieces, row_blocks, col_blocks, out_type):
    quarter, width = pieces[0].shape
    shape = jax.ShapeDtypeStruct((4 * quarter, width), out_type)
    whole = None
    for start in (0, 2):
        held = [] if whole is None else [whole]
        whole = pl.pallas_call(
            place_kernel,
            out_shape=shape,
            grid_spec=pltpu.PrefetchScalarGridSpec(
                num_scalar_prefetch=2,
                grid=(2,),
                in_specs=[pl.BlockSpec((quarter, width), lambda i, rows, cols: (0, 0))] * 2
                + [pl.BlockSpec(memory_space=pl.ANY)] * len(held),
                out_specs=pl.BlockSpec((quarter, width), lambda i, rows, cols, start=start: (rows[start + i], 0)),
            ),
            input_output_aliases={4: 0} if held else {},
            compiler_params=params(40),
            cost_estimate=cost(0, shape.size * 4),
        )(row_blocks, col_blocks, *pieces[start : start + 2], *held)
    return whole


def unit_kernel(cols_ref, in_ref, out_ref):
    values = in_ref[...].astype(f32)
    rstd = lax.rsqrt(jnp.mean(values * values, axis=1, keepdims=True) + EPSILON)
    width = in_ref.shape[1] // BLOCKS
    for block in range(BLOCKS):
        start = pl.multiple_of(cols_ref[block] * width, 128)
        out_ref[:, block * width : (block + 1) * width] = (in_ref[:, pl.ds(start, width)].astype(f32) * rstd).astype(bf16)


def unit_rows(array, col_blocks, tile):
    rows, width = array.shape
    return pl.pallas_call(
        unit_kernel,
        out_shape=jax.ShapeDtypeStruct((rows, width), bf16),
        grid_spec=pltpu.PrefetchScalarGridSpec(
            num_scalar_prefetch=1,
            grid=(rows // tile,),
            in_specs=[pl.BlockSpec((tile, width), lambda i, cols: (i, 0))],
            out_specs=pl.BlockSpec((tile, width), lambda i, cols: (i, 0)),
        ),
        compiler_params=params(),
        cost_estimate=cost(0, 4 * rows * width),
    )(col_blocks, array)


def fit(rows):
    return next(tile for tile in (128, 96, 64, 48, 32, 16) if rows % tile == 0)


def add_norm_kernel(base_ref, a_ref, b_ref, c_ref, sum_ref, unit_ref):
    total = base_ref[...].astype(f32) + (a_ref[...].astype(f32) + b_ref[...].astype(f32) + c_ref[...].astype(f32))
    rstd = lax.rsqrt(jnp.mean(total * total, axis=1, keepdims=True) + EPSILON)
    sum_ref[...] = total
    unit_ref[...] = (total * rstd).astype(bf16)


def norm_back_kernel(base_ref, rest_ref, a_ref, b_ref, c_ref, *outs):
    base = base_ref[...].astype(f32)
    rstd = lax.rsqrt(jnp.mean(base * base, axis=1, keepdims=True) + EPSILON)
    unit = base * rstd
    grad = a_ref[...].astype(f32) + b_ref[...].astype(f32) + c_ref[...].astype(f32)
    total = rest_ref[...].astype(f32) + rstd * (grad - unit * jnp.mean(grad * unit, axis=1, keepdims=True))
    for out in outs:
        out[...] = total.astype(out.dtype)


def on_quarter(kernel, arrays, rows, out_types):
    width = arrays[0].shape[1]
    tile = fit(rows)
    spec = pl.BlockSpec((tile, width), lambda i: (i, 0))
    return pl.pallas_call(
        kernel,
        out_shape=[jax.ShapeDtypeStruct((rows, width), kind) for kind in out_types],
        grid=(rows // tile,),
        in_specs=[spec] * len(arrays),
        out_specs=[spec] * len(out_types),
        compiler_params=params(),
        cost_estimate=cost(0, rows * width * 16),
    )(*arrays)


def first_kernel(n, unit_ref, *refs):
    pieces, (out_ref, joined_ref, held_ref, sems) = refs[:n], refs[n:]
    rows = held_ref.shape[0] // n

    @pl.when(pl.program_id(0) == 0)
    def _():
        copies = [pltpu.make_async_copy(pieces[i], held_ref.at[pl.ds(i * rows, rows)], sems.at[i]) for i in range(n)]
        for copy in copies:
            copy.start()
        for copy in copies:
            copy.wait()
        joined_ref[...] = held_ref[...]

    out_ref[...] = nn(unit_ref[...], held_ref[...]).astype(bf16)


def first_product(unit, pieces, tile):
    tokens, width = unit.shape
    cols = pieces[0].shape[1]
    return pl.pallas_call(
        functools.partial(first_kernel, len(pieces)),
        out_shape=[jax.ShapeDtypeStruct((tokens, cols), bf16), jax.ShapeDtypeStruct((width, cols), bf16)],
        grid=(tokens // tile,),
        in_specs=[pl.BlockSpec((tile, width), lambda i: (i, 0))] + [pl.BlockSpec(memory_space=pl.ANY)] * len(pieces),
        out_specs=[pl.BlockSpec((tile, cols), lambda i: (i, 0)), pl.BlockSpec((width, cols), lambda i: (0, 0))],
        scratch_shapes=[pltpu.VMEM((width, cols), bf16), pltpu.SemaphoreType.DMA((len(pieces),))],
        compiler_params=params(),
        cost_estimate=cost(2 * tokens * width * cols, 2 * (tokens + width) * (width + cols)),
    )(unit, *pieces)


def quarter_kernel(order_ref, in_ref, weight_ref, *outs):
    values = in_ref[...]
    width = weight_ref.shape[0]
    for start in range(0, width, 512):
        part = nt(values, weight_ref[start : start + 512]).astype(bf16)
        for place, out in enumerate(outs):

            @pl.when(pl.program_id(0) == place)
            def _(out=out, part=part, start=start):
                out[:, start : start + 512] = part


def quarter_products(array, weight, quarters, top):
    width, cols = weight.shape
    rows = array.shape[0] // 4
    return pl.pallas_call(
        quarter_kernel,
        out_shape=[jax.ShapeDtypeStruct((rows, width), bf16)] * 2,
        grid_spec=pltpu.PrefetchScalarGridSpec(
            num_scalar_prefetch=1,
            grid=(2,),
            in_specs=[
                pl.BlockSpec((rows, cols), lambda i, order: (order[top - i], 0)),
                pl.BlockSpec((width, cols), lambda i, order: (0, 0), pipeline_mode=pl.Buffered(1)),
            ],
            out_specs=[pl.BlockSpec((rows, width), lambda i, order: (0, 0))] * 2,
        ),
        compiler_params=params(),
        cost_estimate=cost(4 * rows * width * cols, 4 * rows * width),
    )(quarters, array, weight)


def back_kernel(order_ref, *refs):
    pieces, weight_ref, out_ref = refs[:4], refs[4], refs[5]
    for place, piece in enumerate(pieces):

        @pl.when(pl.program_id(0) == place)
        def _(piece=piece):
            out_ref[...] = nn(piece[...], weight_ref[...]).astype(bf16)


def back_product(pieces, weight, quarters):
    rows, width = pieces[0].shape
    cols = weight.shape[1]
    return pl.pallas_call(
        back_kernel,
        out_shape=jax.ShapeDtypeStruct((4 * rows, cols), bf16),
        grid_spec=pltpu.PrefetchScalarGridSpec(
            num_scalar_prefetch=1,
            grid=(4,),
            in_specs=[pl.BlockSpec((rows, width), lambda i, order: (0, 0), pipeline_mode=pl.Buffered(1))] * 4
            + [pl.BlockSpec((width, cols), lambda i, order: (0, 0), pipeline_mode=pl.Buffered(1))],
            out_specs=pl.BlockSpec((rows, cols), lambda i, order: (order[i], 0)),
        ),
        compiler_params=params(),
        cost_estimate=cost(8 * rows * width * cols, 8 * rows * width),
    )(quarters, *pieces, weight)


def ffn_kernel(step, n_units, n_earlier, order_ref, *refs):
    units, dy_ref, weights_hbm = refs[:n_units], refs[n_units], refs[n_units + 1]
    earlier, refs = refs[n_units + 2 : n_units + 2 + n_earlier], refs[-8:]
    mixed_ref, ggate_ref, gup_ref, gunit_ref, out_ref, held_ref, unit_ref, sems = refs
    width, hidden = held_ref.shape[0], held_ref.shape[1] // 3
    rows = width // BLOCKS
    copies = []
    for i in range(BLOCKS):
        start = pl.multiple_of(order_ref[i] * rows, rows)
        source = weights_hbm.at[pl.ds(start, rows)]
        copies.append(pltpu.make_async_copy(source, held_ref.at[pl.ds(i * rows, rows)], sems.at[i]))

    @pl.when(pl.program_id(0) == 0)
    def _():
        for copy in copies:
            copy.start()
        for copy in copies:
            copy.wait()

    for place, unit in enumerate(units):

        @pl.when(pl.program_id(0) == place)
        def _(unit=unit):
            unit_ref[...] = unit[...]

    unit, dy = unit_ref[...], dy_ref[...]
    for start in range(0, hidden, step):
        stop = min(start + step, hidden)
        cols = slice(start, stop)
        gate = nn(unit, held_ref[:, start:stop])
        up = nn(unit, held_ref[:, hidden + start : hidden + stop])
        gmixed = nn(dy, held_ref[:, 2 * hidden + start : 2 * hidden + stop])
        sig = jax.nn.sigmoid(gate)
        silu = gate * sig
        mixed_ref[:, cols] = (silu * up).astype(bf16)
        ggate_ref[:, cols] = (gmixed * up * (sig * (1.0 + gate * (1.0 - sig)))).astype(bf16)
        gup_ref[:, cols] = (gmixed * silu).astype(bf16)
    ggate, gup, mixed = ggate_ref[...], gup_ref[...], mixed_ref[...]
    for start in range(0, width, 512):
        cols = slice(start, start + 512)
        gunit = nt(ggate, held_ref[cols, :hidden]) + nt(gup, held_ref[cols, hidden : 2 * hidden])
        out = nt(mixed, held_ref[cols, 2 * hidden :])
        if earlier:
            gunit = gunit + earlier[0][0, :, cols].astype(f32)
            out = out + earlier[1][0, :, cols].astype(f32)
        gunit_ref[0, :, cols] = gunit.astype(bf16)
        out_ref[0, :, cols] = out.astype(bf16)


def feed_forward(units, dy, start, weights, hidden, order, held=(), earlier=()):
    rows, width = units[0].shape
    line = lambda cols: pl.BlockSpec((rows, cols), lambda i, order: (i + start, 0))
    stacked = pl.BlockSpec((1, rows, width), lambda i, order: (i + start, 0, 0))
    shapes = [jax.ShapeDtypeStruct((4 * rows, hidden), bf16)] * 3 + [jax.ShapeDtypeStruct((4, rows, width), bf16)] * 2
    once = pl.BlockSpec((rows, width), lambda i, order: (0, 0), pipeline_mode=pl.Buffered(1))
    anywhere = pl.BlockSpec(memory_space=pl.ANY)
    steps = len(units)
    first = 3 + steps + len(earlier)
    return pl.pallas_call(
        functools.partial(ffn_kernel, 256, steps, len(earlier)),
        out_shape=shapes,
        grid_spec=pltpu.PrefetchScalarGridSpec(
            num_scalar_prefetch=1,
            grid=(steps,),
            in_specs=[once] * steps + [line(width), anywhere] + [stacked] * len(earlier) + [anywhere] * len(held),
            out_specs=[line(hidden)] * 3 + [stacked] * 2,
            scratch_shapes=[
                pltpu.VMEM((width, 3 * hidden), bf16),
                pltpu.VMEM((rows, width), bf16),
                pltpu.SemaphoreType.DMA((BLOCKS,)),
            ],
        ),
        input_output_aliases={first + i: i for i in range(len(held))},
        compiler_params=params(60),
        cost_estimate=cost(12 * steps * rows * width * hidden, 2 * (4 * steps * rows + 3 * hidden) * width),
    )(order, *units, dy, weights, *earlier, *held)


def weight_kernel(layout, order_ref, quarters_ref, *refs):
    refs, out = list(refs[:-1]), refs[-1]
    total = None
    for n_left, n_right in layout:
        lefts, rights = [refs.pop(0)[...] for _ in range(n_left)], [refs.pop(0)[...] for _ in range(n_right)]
        left, right = [jnp.concatenate(item, axis=0) if len(item) > 1 else item[0] for item in (lefts, rights)]
        part = nn(left.T, right)
        total = part if total is None else total + part
    out[...] = total.astype(bf16)


def weight_grads(parts, order, quarters):
    width = parts[0][0][0][0].shape[1]
    rows = width // BLOCKS
    cols = parts[0][1][0][0].shape[1]
    arrays, specs, tokens = [], [], 0
    for pieces in parts:
        for side, side_pieces in enumerate(pieces):
            for array, *place in side_pieces:
                n = array.shape[0] // (1 if not place else 4 if place[0] == "q" else 2)

                def index(i, order, quarters, side=side, place=tuple(place)):
                    row = 0 if not place else quarters[place[1]] if place[0] == "q" else place[0]
                    return (row, 0 if side else i)

                mode = {"pipeline_mode": pl.Buffered(1)} if side else {}
                specs.append(pl.BlockSpec((n, cols if side else rows), index, **mode))
                arrays.append(array)
                tokens += n if side else 0
    return pl.pallas_call(
        functools.partial(weight_kernel, tuple((len(lefts), len(rights)) for lefts, rights in parts)),
        out_shape=jax.ShapeDtypeStruct((width, cols), bf16),
        grid_spec=pltpu.PrefetchScalarGridSpec(
            num_scalar_prefetch=2,
            grid=(BLOCKS,),
            in_specs=specs,
            out_specs=pl.BlockSpec((rows, cols), lambda i, order, quarters: (order[i], 0)),
        ),
        compiler_params=params(48),
        cost_estimate=cost(2 * tokens * width * cols, 2 * (tokens + width) * (width + cols)),
    )(order, quarters, *arrays)


def ffn_weight_kernel(order_ref, down_order_ref, *refs):
    units, (dy_ref, mixed_ref, ggate_ref, gup_ref), outs = refs[:4], refs[4:8], refs[8:]
    cols = ggate_ref.shape[1]
    unit = jnp.concatenate([item[...] for item in units], axis=0).T
    outs[0][:, :cols] = nn(unit, ggate_ref[...]).astype(bf16)
    outs[0][:, cols : 2 * cols] = nn(unit, gup_ref[...]).astype(bf16)
    down = nn(dy_ref[...].T, mixed_ref[...]).astype(bf16)
    if len(outs) == 2:
        outs[1][...] = down
    else:
        outs[0][:, 2 * cols :] = down


def ffn_weight_grads(units, dy, grads, order, down_order=None):
    quarter, width = units[0].shape
    rows = width // BLOCKS
    cols = grads[0].shape[1]
    held = pl.BlockSpec((4 * quarter, cols), lambda i, *orders: (0, 0), pipeline_mode=pl.Buffered(1))
    sizes = [3 * cols] if down_order is None else [2 * cols, cols]
    results = pl.pallas_call(
        ffn_weight_kernel,
        out_shape=[jax.ShapeDtypeStruct((width, n), bf16) for n in sizes],
        grid_spec=pltpu.PrefetchScalarGridSpec(
            num_scalar_prefetch=2,
            grid=(BLOCKS,),
            in_specs=[pl.BlockSpec((quarter, rows), lambda i, *orders: (0, i))] * 4
            + [pl.BlockSpec((4 * quarter, rows), lambda i, *orders: (0, i))]
            + [held] * 3,
            out_specs=[
                pl.BlockSpec((rows, n), lambda i, *orders, place=place: (orders[place][i], 0))
                for place, n in enumerate(sizes)
            ],
        ),
        compiler_params=params(48),
        cost_estimate=cost(24 * quarter * width * cols, 2 * (8 * quarter + width) * (width + 3 * cols)),
    )(order, order if down_order is None else down_order, *units, dy, *grads)
    return results[0] if down_order is None else results


def per_device(
    n_seq,
    n_head,
    tokens,
    doc_reset,
    gain_attn,
    gain_ffn,
    query_weight,
    key_weight,
    value_weight,
    out_weight,
    gate_weight,
    up_weight,
    down_weight,
    grad_out,
):
    rows, length, width = tokens.shape
    heads = query_weight.shape[1] // FEAT
    count = rows * length
    quarter = count // 4
    half = 2 * quarter
    me = lax.axis_index("seq").astype(jnp.int32)
    head_me = lax.axis_index("head").astype(jnp.int32)
    order = jnp.arange(BLOCKS, dtype=jnp.int32)
    if n_seq == 8:
        order = me ^ order
    quarters = head_me ^ jnp.arange(4, dtype=jnp.int32)

    gain_one = gain_attn.astype(f32)[:, None]
    gain_two = gain_ffn.astype(f32)[:, None]
    scaled = lambda weight, gain: (weight.astype(f32) * gain).astype(bf16)
    qkv_own = jnp.concatenate([query_weight, key_weight, value_weight], axis=1)
    gate_own, up_own, down_own = scaled(gate_weight, gain_two), scaled(up_weight, gain_two), down_weight.T
    hidden_units = gate_weight.shape[1]
    cut = (hidden_units + VHEAD) // (2 * VHEAD) * VHEAD
    groups = (slice(0, cut), slice(cut, hidden_units))
    values = heads * VHEAD
    qkv_pieces = gather_rows(scaled(qkv_own, gain_one), n_seq)
    everywhere = lambda value: lax.all_gather(value, "seq", axis=0, tiled=True)
    out_w = everywhere(out_weight.T)
    ffn_w = []
    for group in groups:
        parts = [gate_own[:, group], up_own[:, group], down_own[:, group]]
        ffn_w.append(everywhere(jnp.concatenate(parts, axis=1)))
    out_w = swap_blocks(out_w, order)

    flat = tokens.reshape(count, width)
    x_own = move_blocks(flat, quarters[:1], order, quarter)
    dy = move_blocks(grad_out.reshape(count, width), quarters, order, quarter)
    unit_one = after(unit_rows(flat, order, quarter // 2), x_own, dy)

    docs = jnp.cumsum(doc_reset, axis=1)
    final = docs[:, -1:]
    flag = jnp.broadcast_to(final > 0, docs.shape)
    edges = jnp.stack([docs, docs == 0, docs == final, flag] + [jnp.zeros_like(docs)] * 4, axis=2).astype(f32)
    doc_rows = jnp.broadcast_to(docs[:, None, :], (rows, 8, length)).astype(f32)
    tables, feat_rows, to_key, to_query = feature_tables(heads)

    lanes = 2 * heads * FEAT
    unit_flops = 2 * rows * heads * length * WIDE * VHEAD
    qkv, qkv_w = first_product(unit_one, qkv_pieces, quarter)
    qkv = qkv.reshape(rows, length, lanes + values)
    (states,) = by_row(
        functools.partial(state_kernel, heads),
        rows,
        [(qkv, True), (edges, True), (tables["ka"], False), (tables["kb"], False), (feat_rows, False)],
        [((heads, TALL, VHEAD), bf16)],
        flops=3 * unit_flops,
    )
    numerator, denominator = by_row(
        functools.partial(inside_kernel, heads),
        rows,
        [(qkv, True), (edges, True), (doc_rows, True), (to_key, False)],
        [((length, values), f32), ((length, heads), f32)],
        flops=3 * unit_flops,
    )
    found = scan_begin(states, False, me, n_seq, (numerator, out_w))
    state_in, place = scan_end(found, False, me, n_seq)
    query_tables = [(tables["qa"], False), (tables["qb"], False), (feat_rows, False)]
    key_tables = [(tables["ka"], False), (tables["kb"], False), (feat_rows, False)]
    attended, rden = by_row(
        functools.partial(attend_kernel, heads),
        rows,
        [(qkv, True), (edges, True), (numerator, True), (after(denominator, out_w), True), (state_in, False)]
        + query_tables,
        [((length, values), bf16), ((length, heads), f32)],
        place=place,
        flops=3 * unit_flops,
    )
    attended_flat = attended.reshape(count, values)
    far = quarter_products(attended_flat, out_w, quarters, 3)
    near = quarter_products(attended_flat, out_w, quarters, 1)
    branch = [near[1], near[0], far[1], far[0]]

    branch, _ = scatter_head(branch)
    hidden, unit_two = on_quarter(add_norm_kernel, [x_own, *branch], quarter, [f32, bf16])
    held = []

    def near_rows(units):
        held.extend(feed_forward(units, dy, 0, ffn_w[0], cut, order))
        return held

    units = gather_head(unit_two, near_rows)
    first = feed_forward(units[2:], dy, 2, ffn_w[0], cut, order, held)
    seq_sum = lambda value: lax.psum_scatter(value, "seq", scatter_dimension=0, tiled=True).astype(f32)
    first_grads = ffn_weight_grads(units, dy, first[:3], order, split_order(order, n_seq))
    ffn_grads = [seq_sum(first_grads[0])]
    left = [after(units[0], first_grads), *units[1:]]
    second = feed_forward(left, dy, 0, ffn_w[1], hidden_units - cut, order, earlier=first[3:])
    gunit, ffn_out = [[item[i] for i in range(4)] for item in second[3:]]

    down_pairs = scatter_begin(first_grads[1], n_seq)
    gunit[3] = after(gunit[3], *down_pairs)

    def second_grads(sent):
        left = [after(units[0], sent), *units[1:]]
        return ffn_weight_grads(left, dy, second[:3], order)

    terms, found = scatter_head(gunit, beside=second_grads)
    down_terms = scatter_sends(down_pairs)
    terms = after(terms, *down_terms)
    grad_hidden, grad_branch = on_quarter(norm_back_kernel, [hidden, dy, *terms], quarter, [f32, bf16])
    ffn_grads.append(seq_sum(after(found, grad_hidden)))
    block_sum = []

    def block_core(near):
        block_sum.append(scatter_core(ffn_out))
        return block_sum

    grad_branch = gather_head(grad_branch, block_core)

    grad_att = back_product(grad_branch, out_w, quarters).reshape(rows, length, values)
    carry, gnum, gden = by_row(
        functools.partial(carry_kernel, heads),
        rows,
        [(qkv, True), (edges, True), (grad_att, True), (attended, True), (rden, True)] + query_tables,
        [((heads, TALL, VHEAD), bf16), ((length, values), bf16), ((length, heads), f32)],
        flops=3 * unit_flops,
    )
    gboth, gval = by_row(
        functools.partial(inside_back_kernel, heads),
        rows,
        [(qkv, True), (edges, True), (doc_rows, True), (gnum, True), (gden, True), (state_in, False)]
        + [(to_key, False), (to_query, False)]
        + query_tables,
        [((length, lanes), f32), ((length, values), f32)],
        place=place,
        flops=11 * unit_flops,
    )
    sides = [[(grad_branch[i],), (grad_branch[i + 1],)] for i in (0, 2)]
    parts = [(side, [(attended_flat, "q", i), (attended_flat, "q", i + 1)]) for side, i in zip(sides, (0, 2))]
    grad_out_w = weight_grads(parts, split_order(order, n_seq), quarters)
    found = scan_begin(carry, True, me, n_seq, (gboth, grad_out_w))
    terms, _ = scatter_head(ffn_out, beside=lambda _: gboth, summed=block_sum[0])
    block_own = (hidden + (terms[0].astype(f32) + terms[1].astype(f32) + terms[2].astype(f32))).astype(bf16)
    carry_in, place_back = scan_end(found, True, me, n_seq)
    carry_in = after(carry_in, block_own)
    block_all = gather_head(block_own, lambda near: (carry_in,))
    (gqkv,) = by_row(
        functools.partial(finish_back_kernel, heads),
        rows,
        [(qkv, True), (edges, True), (carry_in, False), (gboth, True), (gval, True)] + key_tables,
        [((length, lanes + values), bf16)],
        place=place_back,
        flops=6 * unit_flops,
    )
    gqkv = after(gqkv.reshape(count, lanes + values), block_all[2])
    back = lambda value, kind: place_quarters(value, quarters, order, kind).reshape(rows, length, width)

    rest = hidden_units - cut

    def sum_head(value, earlier):
        pairs = after([send(value, "head", mask, 4) for mask in (1, 2, 3)], earlier)
        return (value + pairs[0]) + (pairs[1] + pairs[2])

    def ffn_outputs(sums):
        sums = jnp.concatenate(sums, axis=1)
        parts = jnp.split(sums, np.cumsum([cut, cut, cut, rest, rest]), axis=1)
        grad_gate, grad_up, grad_down = [jnp.concatenate([parts[i], parts[i + 3]], axis=1) for i in range(3)]
        gain = jnp.sum(gate_weight.astype(f32) * grad_gate + up_weight.astype(f32) * grad_up, axis=1)
        return (grad_gate * gain_two, grad_up * gain_two, grad_down.T), gain

    far = quarter_products(gqkv, qkv_w, quarters, 3)
    near = quarter_products(gqkv, qkv_w, quarters, 1)
    terms, grad_qkv = scatter_head(
        [near[1], near[0], far[1], far[0]],
        beside=lambda sent: weight_grads(
            [([(after(unit_one, sent),)], [(gqkv,)])], split_order(order, n_seq), quarters
        ),
    )
    (grad_x,) = on_quarter(norm_back_kernel, [x_own, grad_hidden, *after(terms, ffn_grads[0])], quarter, [bf16])
    qkv_pairs = scatter_begin(grad_qkv, n_seq)
    qkv_terms = scatter_sends(qkv_pairs)
    out_pairs = scatter_begin(after(grad_out_w, grad_x), n_seq)
    ffn_grads, ffn_gain = ffn_outputs([ffn_grads[0], scatter_end(down_pairs, down_terms), after(ffn_grads[1], grad_x)])
    block_all = back(after(block_all, grad_x), bf16)
    grad_x_all = gather_head(grad_x, lambda near: (*qkv_terms, *out_pairs, ffn_gain, *ffn_grads, block_all))
    out_terms = scatter_sends(out_pairs)
    grad_qkv = scatter_end(qkv_pairs, qkv_terms)
    qkv_gain = jnp.sum(qkv_own.astype(f32) * grad_qkv, axis=1)
    grad_x_all[2] = after(grad_x_all[2], *out_terms)
    grad_x_all = back(grad_x_all, f32)
    gains = sum_head(jnp.stack([qkv_gain, ffn_gain]), grad_x_all)
    grad_out_w = scatter_end(out_pairs, out_terms)
    grad_qkv = grad_qkv * gain_one
    narrow = heads * FEAT
    return (
        block_all,
        grad_x_all,
        gains[0],
        gains[1],
        grad_qkv[:, :narrow],
        grad_qkv[:, narrow:lanes],
        grad_qkv[:, lanes:],
        grad_out_w.T,
        *ffn_grads,
    )


def solution(mesh):
    placed = (
        P(None, "seq", None),
        P(None, "seq"),
        P("seq"),
        P("seq"),
        P("seq", "head"),
        P("seq", "head"),
        P("seq", "head"),
        P("head", "seq"),
        P("seq", "head"),
        P("seq", "head"),
        P("head", "seq"),
        P(None, "seq", None),
    )
    return jax.shard_map(
        functools.partial(per_device, mesh.shape["seq"], mesh.shape["head"]),
        mesh=mesh,
        in_specs=placed,
        out_specs=(P(None, "seq", None), P(None, "seq", None)) + placed[2:11],
        check_vma=False,
    )
```

```python
import functools

import jax
import jax.numpy as jnp
import numpy as np
from jax import lax
from jax.experimental import pallas as pl
from jax.experimental.pallas import tpu as pltpu
from jax.sharding import PartitionSpec as P

FEAT = 16
VHEAD = 128
EPSILON = 1e-06
PAIRS = [(a, b) for a in range(FEAT + 1) for b in range(a, FEAT + 1)]
WIDE = 256
TALL = 160
NORM_ROW = len(PAIRS)
FLAG_ROW = NORM_ROW + 2
BLOCKS = 8
COST = 2
bf16, f32 = jnp.bfloat16, jnp.float32


def feature_tables(heads):
    lanes = 2 * heads * FEAT
    tables = {name: np.zeros((lanes, heads * WIDE), np.float32) for name in ("qa", "qb", "ka", "kb")}
    rows = np.zeros((8, heads * WIDE), np.float32)
    to_key = np.zeros((lanes, heads * lanes), np.float32)
    to_query = np.zeros((lanes, heads * lanes), np.float32)
    for head in range(heads):
        for place, (a, b) in enumerate(PAIRS):
            column = head * WIDE + place
            for name, entry, row in (("a", a, 0), ("b", b, 1)):
                if entry == 0:
                    rows[row, column] = 1.0
                else:
                    lane = head * FEAT + entry - 1
                    tables["q" + name][lane, column] = 1.0
                    tables["k" + name][heads * FEAT + lane, column] = 1.0
            rows[2, column] = 1.0 if b == 0 else 0.25 if a == 0 else 1 / 32 if a == b else 1 / 16
        for feat in range(FEAT):
            lane = head * FEAT + feat
            to_key[lane, head * lanes + heads * FEAT + lane] = 0.25
            to_query[heads * FEAT + lane, head * lanes + lane] = 0.25
    tables = {name: jnp.asarray(item, bf16) for name, item in tables.items()}
    return tables, jnp.asarray(rows), jnp.asarray(to_key, bf16), jnp.asarray(to_query, bf16)


def nn(left, right):
    return lax.dot_general(left, right, (((1,), (0,)), ((), ())), preferred_element_type=f32)


def nt(left, right):
    return lax.dot_general(left, right, (((1,), (1,)), ((), ())), preferred_element_type=f32)


def tn(left, right):
    return lax.dot_general(left, right, (((0,), (0,)), ((), ())), preferred_element_type=f32)


def params(mib=32):
    return pltpu.CompilerParams(vmem_limit_bytes=mib << 20)


def cost(flops, nbytes):
    return pl.CostEstimate(flops=int(flops) // COST, bytes_accessed=int(nbytes) // COST, transcendentals=0)


def whole_spec(array):
    zeros = (0,) * array.ndim
    return pl.BlockSpec(array.shape, lambda *_: zeros)


def pack_state(state, norm_row, flag):
    place = lax.broadcasted_iota(jnp.int32, (TALL, VHEAD), 0)
    block = state[:TALL]
    block = jnp.where(place == NORM_ROW, norm_row[:, :VHEAD], block)
    block = jnp.where(place == NORM_ROW + 1, norm_row[:, VHEAD:], block)
    return jnp.where(place == FLAG_ROW, flag, block).astype(bf16)


def unpack_state(block):
    tail = block[TALL - 16 :].astype(f32)
    base = TALL - 16
    low = tail[NORM_ROW - base : NORM_ROW - base + 1]
    high = tail[NORM_ROW + 1 - base : NORM_ROW + 2 - base]
    full = jnp.concatenate([block, jnp.zeros((WIDE - TALL, VHEAD), block.dtype)], axis=0)
    return full, jnp.concatenate([low, high], axis=1)


def state_kernel(heads, place_ref, qkv_ref, edge_ref, ka_ref, kb_ref, rows_ref, out_ref):
    keys = qkv_ref[0, :, : 2 * heads * FEAT]
    edges = edge_ref[0]
    last, flag = edges[:, 2:3], edges[0:1, 3:4]
    for head in range(heads):
        cols = slice(head * WIDE, (head + 1) * WIDE)
        phi = (nn(keys, ka_ref[:, cols]) + rows_ref[0:1, cols]) * (nn(keys, kb_ref[:, cols]) + rows_ref[1:2, cols])
        phi = phi * last
        start = 2 * heads * FEAT + head * VHEAD
        state = tn(phi.astype(bf16), qkv_ref[0, :, start : start + VHEAD])
        out_ref[0, head] = pack_state(state, jnp.sum(phi, axis=0, keepdims=True), flag)


def local_mask(edges, docs):
    length = edges.shape[0]
    later = lax.broadcasted_iota(jnp.int32, (length, length), 0) >= lax.broadcasted_iota(jnp.int32, (length, length), 1)
    return later & (edges[:, 0:1] == docs)


def inside_kernel(heads, place_ref, qkv_ref, edge_ref, doc_ref, key_ref, num_ref, den_ref):
    lanes = 2 * heads * FEAT
    both = qkv_ref[0, :, :lanes]
    mask = local_mask(edge_ref[0], doc_ref[0, 0:1])
    moved = nn(both, key_ref[...]).astype(bf16)
    dens = []
    for head in range(heads):
        scores = nt(moved[:, head * lanes : (head + 1) * lanes], both)
        weights = jnp.where(mask, 1.0 + scores + 0.5 * scores * scores, 0.0)
        dens.append(jnp.sum(weights, axis=1, keepdims=True))
        start = lanes + head * VHEAD
        num_ref[0, :, head * VHEAD : (head + 1) * VHEAD] = nn(
            weights.astype(bf16), qkv_ref[0, :, start : start + VHEAD]
        )
    den_ref[0] = jnp.concatenate(dens, axis=1)


def block_at(place_ref, states_ref, row, heads, head):
    per = states_ref.shape[1]
    index = (place_ref[0] + row) * heads + head
    return states_ref[place_ref[1 + index // per], index % per]


def query_features(both, qa, qb, rows, first):
    left = nn(both, qa) + rows[0:1]
    right = nn(both, qb) + rows[1:2]
    return left, right, left * right * rows[2:3] * first


def attend_kernel(heads, place_ref, qkv_ref, edge_ref, num_ref, den_ref, states_ref, qa_ref, qb_ref, rows_ref, att_ref, rden_ref):
    both = qkv_ref[0, :, : 2 * heads * FEAT]
    first = edge_ref[0][:, 1:2]
    rdens = []
    for head in range(heads):
        cols = slice(head * WIDE, (head + 1) * WIDE)
        _, _, phi = query_features(both, qa_ref[:, cols], qb_ref[:, cols], rows_ref[:, cols], first)
        factor, norm = unpack_state(block_at(place_ref, states_ref, pl.program_id(0), heads, head))
        den = den_ref[0][:, head : head + 1] + jnp.sum(phi * norm, axis=1, keepdims=True)
        rden = 1.0 / den
        out = slice(head * VHEAD, (head + 1) * VHEAD)
        att_ref[0, :, out] = ((num_ref[0, :, out] + nn(phi.astype(bf16), factor)) * rden).astype(bf16)
        rdens.append(rden)
    rden_ref[0] = jnp.concatenate(rdens, axis=1)


def carry_kernel(
    heads, place_ref, qkv_ref, edge_ref, ga_ref, att_ref, rden_ref, qa_ref, qb_ref, rows_ref, carry_ref, gnum_ref, gden_ref
):
    both = qkv_ref[0, :, : 2 * heads * FEAT]
    edges = edge_ref[0]
    first, flag = edges[:, 1:2], edges[0:1, 3:4]
    gdens = []
    for head in range(heads):
        cols = slice(head * WIDE, (head + 1) * WIDE)
        out = slice(head * VHEAD, (head + 1) * VHEAD)
        _, _, phi = query_features(both, qa_ref[:, cols], qb_ref[:, cols], rows_ref[:, cols], first)
        grad = ga_ref[0, :, out].astype(f32)
        rden = rden_ref[0][:, head : head + 1]
        gnum = (grad * rden).astype(bf16)
        gden = -jnp.sum(grad * att_ref[0, :, out].astype(f32), axis=1, keepdims=True) * rden
        gnum_ref[0, :, out] = gnum
        carry_ref[0, head] = pack_state(
            tn(phi.astype(bf16), gnum), jnp.sum(phi * gden, axis=0, keepdims=True), flag
        )
        gdens.append(gden)
    gden_ref[0] = jnp.concatenate(gdens, axis=1)


def inside_back_kernel(
    heads, place_ref, qkv_ref, edge_ref, doc_ref, gnum_ref, gden_ref, states_ref, key_ref, query_ref, qa_ref, qb_ref,
    rows_ref, gboth_ref, gval_ref,
):
    lanes = 2 * heads * FEAT
    both = qkv_ref[0, :, :lanes]
    edges = edge_ref[0]
    first = edges[:, 1:2]
    mask = local_mask(edges, doc_ref[0, 0:1])
    moved = nn(both, key_ref[...]).astype(bf16)
    back = nn(both, query_ref[...]).astype(bf16)
    total = jnp.zeros((both.shape[0], lanes), f32)
    for head in range(heads):
        cols = slice(head * WIDE, (head + 1) * WIDE)
        out = slice(head * VHEAD, (head + 1) * VHEAD)
        own = slice(head * lanes, (head + 1) * lanes)
        start = lanes + head * VHEAD
        values = qkv_ref[0, :, start : start + VHEAD]
        gnum = gnum_ref[0, :, out]
        gden = gden_ref[0][:, head : head + 1]
        scores = nt(moved[:, own], both)
        weights = jnp.where(mask, 1.0 + scores + 0.5 * scores * scores, 0.0).astype(bf16)
        gval_ref[0, :, out] = tn(weights, gnum)
        gscores = jnp.where(mask, (nt(gnum, values) + gden) * (1.0 + scores), 0.0).astype(bf16)
        total = total + nn(gscores, back[:, own]) + tn(gscores, moved[:, own])
        left, right, _ = query_features(both, qa_ref[:, cols], qb_ref[:, cols], rows_ref[:, cols], first)
        factor, norm = unpack_state(block_at(place_ref, states_ref, pl.program_id(0), heads, head))
        place = lax.broadcasted_iota(jnp.int32, (1, WIDE), 1)
        gphi = jnp.where(place < NORM_ROW, (nt(gnum, factor) + norm * gden) * rows_ref[2:3, cols], 0.0) * first
        total = total + nt((gphi * right).astype(bf16), qa_ref[:, cols]) + nt((gphi * left).astype(bf16), qb_ref[:, cols])
    gboth_ref[0] = total


def finish_back_kernel(
    heads, place_ref, qkv_ref, edge_ref, carry_ref, gboth_ref, gval_ref, ka_ref, kb_ref, rows_ref, out_ref
):
    lanes = 2 * heads * FEAT
    both = qkv_ref[0, :, :lanes]
    last = edge_ref[0][:, 2:3]
    total = gboth_ref[0]
    for head in range(heads):
        cols = slice(head * WIDE, (head + 1) * WIDE)
        start = lanes + head * VHEAD
        values = qkv_ref[0, :, start : start + VHEAD]
        left = nn(both, ka_ref[:, cols]) + rows_ref[0:1, cols]
        right = nn(both, kb_ref[:, cols]) + rows_ref[1:2, cols]
        factor, norm = unpack_state(block_at(place_ref, carry_ref, pl.program_id(0), heads, head))
        phi = (left * right * last).astype(bf16)
        gval = gval_ref[0, :, head * VHEAD : (head + 1) * VHEAD] + nn(phi, factor)
        out_ref[0, :, start : start + VHEAD] = gval.astype(bf16)
        place = lax.broadcasted_iota(jnp.int32, (1, WIDE), 1)
        gphi = jnp.where(place < NORM_ROW, nt(values, factor) + norm, 0.0) * last
        total = total + nt((gphi * right).astype(bf16), ka_ref[:, cols]) + nt((gphi * left).astype(bf16), kb_ref[:, cols])
    out_ref[0, :, :lanes] = total.astype(bf16)


def by_row(kernel, rows, inputs, outputs, place=None, flops=0, base=0, count=None):
    count = rows if count is None else count
    arrays = [array for array, _ in inputs]

    def spec_of(array):
        zeros = (0,) * (array.ndim - 1)
        return pl.BlockSpec((1,) + array.shape[1:], lambda row, scalars: (row + scalars[0],) + zeros)

    shapes = [jax.ShapeDtypeStruct((rows,) + shape, kind) for shape, kind in outputs]
    nbytes = sum(item.size * item.dtype.itemsize for item in arrays + shapes)
    scalars = jnp.asarray(base, jnp.int32).reshape(1)
    if place is not None:
        scalars = jnp.concatenate([scalars, place])
    return pl.pallas_call(
        kernel,
        out_shape=shapes,
        grid_spec=pltpu.PrefetchScalarGridSpec(
            num_scalar_prefetch=1,
            grid=(count,),
            in_specs=[spec_of(array) if per_row else whole_spec(array) for array, per_row in inputs],
            out_specs=[spec_of(shape) for shape in shapes],
        ),
        compiler_params=params(40),
        cost_estimate=cost(flops * count // rows, nbytes * count // rows),
    )(scalars, *arrays)


def scan_kernel(backward, me_ref, *refs):
    pieces, outs, (held, ahead) = refs[:8], refs[8:16], refs[16:]
    for rel in range(8):
        held[rel] = pieces[rel][...]
    me = me_ref[0]
    for block in range(held.shape[1]):
        run = jnp.zeros(held.shape[2:], f32)
        for step in range(8):
            rel = me ^ (7 - step if backward else step)
            ahead[rel, block] = run.astype(bf16)
            own = held[rel, block].astype(f32)
            run = own + (1.0 - own[FLAG_ROW : FLAG_ROW + 1]) * run
    for rel in range(8):
        outs[rel][...] = ahead[rel]


def scan_begin(states, backward, me, count, earlier=()):
    blocks = states.shape[0] * states.shape[1]
    flat = states.reshape(blocks, TALL, VHEAD)
    if count != 8 or blocks % 8:
        return lax.all_gather(flat, "seq").astype(f32)
    per = blocks // 8
    split = flat.reshape(8, per, TALL, VHEAD)
    parts = [lax.dynamic_index_in_dim(split, me ^ rel, 0, keepdims=False) for rel in range(8)]
    pieces = [after(parts[0], *earlier)] + [send(parts[rel], "seq", rel, 8) for rel in range(1, 8)]
    return pl.pallas_call(
        functools.partial(scan_kernel, backward),
        out_shape=[jax.ShapeDtypeStruct((per, TALL, VHEAD), bf16)] * 8,
        in_specs=[pl.BlockSpec(memory_space=pltpu.SMEM)] + [pl.BlockSpec(memory_space=pltpu.VMEM)] * 8,
        out_specs=[pl.BlockSpec(memory_space=pltpu.VMEM)] * 8,
        scratch_shapes=[pltpu.VMEM((8, per, TALL, VHEAD), bf16)] * 2,
        compiler_params=params(),
    )(me.reshape(1), *pieces)


def scan_end(found, backward, me, count):
    if isinstance(found, (list, tuple)):
        back = [found[0]] + [send(found[rel], "seq", rel, 8) for rel in range(1, 8)]
        return jnp.stack(back), me ^ jnp.arange(8, dtype=jnp.int32)
    keep = 1.0 - found[:, :, FLAG_ROW : FLAG_ROW + 1]
    run = jnp.zeros(found.shape[1:], f32)
    for step in range(count):
        at = count - 1 - step if backward else step
        reached = at > me if backward else at < me
        run = jnp.where(reached, found[at] + keep[at] * run, run)
    return run.astype(bf16)[None], jnp.zeros((1,), jnp.int32)


def send(value, axis, mask, count):
    return lax.ppermute(value, axis, [(i, i ^ mask) for i in range(count)])


def gather_rows(shard, count, earlier):
    if count != 8:
        return [lax.all_gather(shard, "seq", axis=0, tiled=True)]
    pieces = [shard, send(shard, "seq", 1, 8)]
    for mask in (2, 4, 6):
        piece = send(shard, "seq", mask, 8)
        piece = after(piece, *earlier) if mask == 2 else piece
        pieces += [piece, send(piece, "seq", 1, 8)]
    return pieces


def after(value, *earlier):
    return lax.optimization_barrier((value, earlier))[0]


def swap_blocks(array, me, count):
    if count != 8:
        return array
    split = array.reshape((BLOCKS, array.shape[0] // BLOCKS) + array.shape[1:])
    return join_rows([lax.dynamic_index_in_dim(split, me ^ i, 0, keepdims=False) for i in range(BLOCKS)])


def split_order(order, n_seq):
    return jnp.array([0, 4, 1, 5, 2, 6, 3, 7], jnp.int32) if n_seq == 8 else order


def scatter_begin(whole, n_seq):
    if n_seq != 8:
        return (lax.psum_scatter(whole, "seq", scatter_dimension=0, tiled=True).astype(f32),)
    return scatter_pairs(whole, send(whole[whole.shape[0] // 2 :], "seq", 1, 8))


def scatter_pairs(whole, other):
    rows = whole.shape[0] // 8
    pairs = [
        whole[i * rows : (i + 1) * rows].astype(f32) + other[i * rows : (i + 1) * rows].astype(f32) for i in range(4)
    ]
    return (pairs[0],) + tuple(pair.astype(bf16) for pair in pairs[1:])


def scatter_sends(pairs):
    return [send(pair, "seq", 2 * place + 2, 8) for place, pair in enumerate(pairs[1:])]


def scatter_end(pairs, terms):
    total = pairs[0]
    for term in terms:
        total = total + term.astype(f32)
    return total


def join_rows(pieces):
    return pieces[0] if len(pieces) == 1 else jnp.concatenate(pieces, axis=0)


CORE, ACROSS = 1, 2


def scatter_core(quarters):
    return (quarters[2].astype(f32) + send(quarters[3], "head", CORE, 4).astype(f32)).astype(bf16)


def scatter_head(quarters, beside=None, summed=None):
    summed = scatter_core(quarters) if summed is None else summed
    across = send(summed, "head", ACROSS, 4)
    near = send(quarters[1], "head", CORE, 4)
    found = () if beside is None else beside(summed)
    return (quarters[0], near, after(across, found)), found


def gather_head(own, between=lambda near: ()):
    near = [own, send(own, "head", CORE, 4)]
    across = after(send(own, "head", ACROSS, 4), *between(near))
    return near + [across, send(across, "head", CORE, 4)]


def move_columns(cols_ref, in_ref, out_ref):
    width = in_ref.shape[1] // BLOCKS
    for block in range(BLOCKS):
        start = pl.multiple_of(cols_ref[block] * width, 128)
        out_ref[:, block * width : (block + 1) * width] = in_ref[:, pl.ds(start, width)].astype(out_ref.dtype)


def move_kernel(rows_ref, cols_ref, in_ref, out_ref):
    move_columns(cols_ref, in_ref, out_ref)


def move_blocks(array, row_blocks, col_blocks, quarter):
    width = array.shape[1]
    split = 2 if quarter % 32 == 0 else 1
    tile = quarter // split
    count = row_blocks.shape[0]
    return pl.pallas_call(
        move_kernel,
        out_shape=jax.ShapeDtypeStruct((count * quarter, width), array.dtype),
        grid_spec=pltpu.PrefetchScalarGridSpec(
            num_scalar_prefetch=2,
            grid=(count, split),
            in_specs=[pl.BlockSpec((tile, width), lambda i, j, rows, cols: (rows[i] * split + j, 0))],
            out_specs=pl.BlockSpec((tile, width), lambda i, j, rows, cols: (i * split + j, 0)),
        ),
        compiler_params=params(),
        cost_estimate=cost(0, 2 * count * quarter * width * array.dtype.itemsize),
    )(row_blocks, col_blocks, array)


def place_kernel(rows_ref, cols_ref, *refs):
    pieces, out_ref = refs[:2], refs[-1]
    for place, piece in enumerate(pieces):
        pl.when(pl.program_id(0) == place)(functools.partial(move_columns, cols_ref, piece, out_ref))


def place_quarters(pieces, row_blocks, col_blocks, out_type, start, whole=None):
    quarter, width = pieces[0].shape
    shape = jax.ShapeDtypeStruct((4 * quarter, width), out_type)
    held = [] if whole is None else [whole]
    return pl.pallas_call(
        place_kernel,
        out_shape=shape,
        grid_spec=pltpu.PrefetchScalarGridSpec(
            num_scalar_prefetch=2,
            grid=(2,),
            in_specs=[pl.BlockSpec((quarter, width), lambda i, rows, cols: (0, 0))] * 2
            + [pl.BlockSpec(memory_space=pl.ANY)] * len(held),
            out_specs=pl.BlockSpec((quarter, width), lambda i, rows, cols: (rows[start + i], 0)),
        ),
        input_output_aliases={4: 0} if held else {},
        compiler_params=params(40),
        cost_estimate=cost(0, shape.size * 4),
    )(row_blocks, col_blocks, *pieces, *held)


def unit_kernel(cols_ref, in_ref, out_ref):
    values = in_ref[...].astype(f32)
    rstd = lax.rsqrt(jnp.mean(values * values, axis=1, keepdims=True) + EPSILON)
    width = in_ref.shape[1] // BLOCKS
    for block in range(BLOCKS):
        start = pl.multiple_of(cols_ref[block] * width, 128)
        out_ref[:, block * width : (block + 1) * width] = (in_ref[:, pl.ds(start, width)].astype(f32) * rstd).astype(bf16)


def unit_rows(array, col_blocks, tile):
    rows, width = array.shape
    return pl.pallas_call(
        unit_kernel,
        out_shape=jax.ShapeDtypeStruct((rows, width), bf16),
        grid_spec=pltpu.PrefetchScalarGridSpec(
            num_scalar_prefetch=1,
            grid=(rows // tile,),
            in_specs=[pl.BlockSpec((tile, width), lambda i, cols: (i, 0))],
            out_specs=pl.BlockSpec((tile, width), lambda i, cols: (i, 0)),
        ),
        compiler_params=params(),
        cost_estimate=cost(0, 4 * rows * width),
    )(col_blocks, array)


def fit(rows):
    return next(tile for tile in (128, 96, 64, 48, 32, 16) if rows % tile == 0)


def add_norm_kernel(base_ref, a_ref, b_ref, c_ref, sum_ref, unit_ref):
    total = base_ref[...].astype(f32) + (a_ref[...].astype(f32) + b_ref[...].astype(f32) + c_ref[...].astype(f32))
    rstd = lax.rsqrt(jnp.mean(total * total, axis=1, keepdims=True) + EPSILON)
    sum_ref[...] = total
    unit_ref[...] = (total * rstd).astype(bf16)


def norm_back_kernel(base_ref, rest_ref, a_ref, b_ref, c_ref, *outs):
    base = base_ref[...].astype(f32)
    rstd = lax.rsqrt(jnp.mean(base * base, axis=1, keepdims=True) + EPSILON)
    unit = base * rstd
    grad = a_ref[...].astype(f32) + b_ref[...].astype(f32) + c_ref[...].astype(f32)
    total = rest_ref[...].astype(f32) + rstd * (grad - unit * jnp.mean(grad * unit, axis=1, keepdims=True))
    for out in outs:
        out[...] = total.astype(out.dtype)


def on_quarter(kernel, arrays, rows, out_types):
    width = arrays[0].shape[1]
    tile = fit(rows)
    spec = pl.BlockSpec((tile, width), lambda i: (i, 0))
    return pl.pallas_call(
        kernel,
        out_shape=[jax.ShapeDtypeStruct((rows, width), kind) for kind in out_types],
        grid=(rows // tile,),
        in_specs=[spec] * len(arrays),
        out_specs=[spec] * len(out_types),
        compiler_params=params(),
        cost_estimate=cost(0, rows * width * 16),
    )(*arrays)


def first_kernel(n, unit_ref, *refs):
    pieces, (out_ref, joined_ref, held_ref, sems) = refs[:n], refs[n:]
    rows = held_ref.shape[0] // n

    @pl.when(pl.program_id(0) == 0)
    def _():
        copies = [pltpu.make_async_copy(pieces[i], held_ref.at[pl.ds(i * rows, rows)], sems.at[i]) for i in range(n)]
        for copy in copies:
            copy.start()
        for copy in copies:
            copy.wait()
        joined_ref[...] = held_ref[...]

    out_ref[...] = nn(unit_ref[...], held_ref[...]).astype(bf16)


def first_product(unit, pieces, tile):
    tokens, width = unit.shape
    cols = pieces[0].shape[1]
    return pl.pallas_call(
        functools.partial(first_kernel, len(pieces)),
        out_shape=[jax.ShapeDtypeStruct((tokens, cols), bf16), jax.ShapeDtypeStruct((width, cols), bf16)],
        grid=(tokens // tile,),
        in_specs=[pl.BlockSpec((tile, width), lambda i: (i, 0))] + [pl.BlockSpec(memory_space=pl.ANY)] * len(pieces),
        out_specs=[pl.BlockSpec((tile, cols), lambda i: (i, 0)), pl.BlockSpec((width, cols), lambda i: (0, 0))],
        scratch_shapes=[pltpu.VMEM((width, cols), bf16), pltpu.SemaphoreType.DMA((len(pieces),))],
        compiler_params=params(),
        cost_estimate=cost(2 * tokens * width * cols, 2 * (tokens + width) * (width + cols)),
    )(unit, *pieces)


def quarter_kernel(order_ref, in_ref, weight_ref, *outs):
    values = in_ref[...]
    width = weight_ref.shape[0]
    for start in range(0, width, 512):
        part = nt(values, weight_ref[start : start + 512]).astype(bf16)
        for place, out in enumerate(outs):

            @pl.when(pl.program_id(0) == place)
            def _(out=out, part=part, start=start):
                out[:, start : start + 512] = part


def quarter_products(array, weight, quarters, top):
    width, cols = weight.shape
    rows = array.shape[0] // 4
    return pl.pallas_call(
        quarter_kernel,
        out_shape=[jax.ShapeDtypeStruct((rows, width), bf16)] * 2,
        grid_spec=pltpu.PrefetchScalarGridSpec(
            num_scalar_prefetch=1,
            grid=(2,),
            in_specs=[
                pl.BlockSpec((rows, cols), lambda i, order: (order[top - i], 0)),
                pl.BlockSpec((width, cols), lambda i, order: (0, 0), pipeline_mode=pl.Buffered(1)),
            ],
            out_specs=[pl.BlockSpec((rows, width), lambda i, order: (0, 0))] * 2,
        ),
        compiler_params=params(),
        cost_estimate=cost(4 * rows * width * cols, 4 * rows * width),
    )(quarters, array, weight)


def back_kernel(order_ref, *refs):
    pieces, weight_ref, out_ref = refs[:4], refs[4], refs[5]
    for place, piece in enumerate(pieces):

        @pl.when(pl.program_id(0) == place)
        def _(piece=piece):
            out_ref[...] = nn(piece[...], weight_ref[...]).astype(bf16)


def back_product(pieces, weight, quarters):
    rows, width = pieces[0].shape
    cols = weight.shape[1]
    return pl.pallas_call(
        back_kernel,
        out_shape=jax.ShapeDtypeStruct((4 * rows, cols), bf16),
        grid_spec=pltpu.PrefetchScalarGridSpec(
            num_scalar_prefetch=1,
            grid=(4,),
            in_specs=[pl.BlockSpec((rows, width), lambda i, order: (0, 0), pipeline_mode=pl.Buffered(1))] * 4
            + [pl.BlockSpec((width, cols), lambda i, order: (0, 0), pipeline_mode=pl.Buffered(1))],
            out_specs=pl.BlockSpec((rows, cols), lambda i, order: (order[i], 0)),
        ),
        compiler_params=params(),
        cost_estimate=cost(8 * rows * width * cols, 8 * rows * width),
    )(quarters, *pieces, weight)


def ffn_kernel(step, n_units, n_earlier, order_ref, *refs):
    units, dy_ref, weights_hbm = refs[:n_units], refs[n_units], refs[n_units + 1]
    earlier, refs = refs[n_units + 2 : n_units + 2 + n_earlier], refs[-8:]
    mixed_ref, ggate_ref, gup_ref, gunit_ref, out_ref, held_ref, unit_ref, sems = refs
    width, hidden = held_ref.shape[0], held_ref.shape[1] // 3
    rows = width // BLOCKS
    copies = []
    for i in range(BLOCKS):
        start = pl.multiple_of(order_ref[i] * rows, rows)
        source = weights_hbm.at[pl.ds(start, rows), pl.ds(weights_hbm.shape[1] - 3 * hidden, 3 * hidden)]
        copies.append(pltpu.make_async_copy(source, held_ref.at[pl.ds(i * rows, rows)], sems.at[i]))

    @pl.when(pl.program_id(0) == 0)
    def _():
        for copy in copies:
            copy.start()
        for copy in copies:
            copy.wait()

    for place, unit in enumerate(units):

        @pl.when(pl.program_id(0) == place)
        def _(unit=unit):
            unit_ref[...] = unit[...]

    unit, dy = unit_ref[...], dy_ref[...]
    for start in range(0, hidden, step):
        stop = min(start + step, hidden)
        cols = slice(start, stop)
        gate = nn(unit, held_ref[:, start:stop])
        up = nn(unit, held_ref[:, hidden + start : hidden + stop])
        gmixed = nn(dy, held_ref[:, 2 * hidden + start : 2 * hidden + stop])
        sig = jax.nn.sigmoid(gate)
        silu = gate * sig
        mixed_ref[:, cols] = (silu * up).astype(bf16)
        ggate_ref[:, cols] = (gmixed * up * (sig * (1.0 + gate * (1.0 - sig)))).astype(bf16)
        gup_ref[:, cols] = (gmixed * silu).astype(bf16)
    ggate, gup, mixed = ggate_ref[...], gup_ref[...], mixed_ref[...]
    for start in range(0, width, 512):
        cols = slice(start, start + 512)
        gunit = nt(ggate, held_ref[cols, :hidden]) + nt(gup, held_ref[cols, hidden : 2 * hidden])
        out = nt(mixed, held_ref[cols, 2 * hidden :])
        if earlier:
            gunit = gunit + earlier[0][0, :, cols].astype(f32)
            out = out + earlier[1][0, :, cols].astype(f32)
        gunit_ref[0, :, cols] = gunit.astype(bf16)
        out_ref[0, :, cols] = out.astype(bf16)


def feed_forward(units, dy, start, weights, hidden, order, held=(), earlier=()):
    rows, width = units[0].shape
    line = lambda cols: pl.BlockSpec((rows, cols), lambda i, order: (i + start, 0))
    stacked = pl.BlockSpec((1, rows, width), lambda i, order: (i + start, 0, 0))
    shapes = [jax.ShapeDtypeStruct((4 * rows, hidden), bf16)] * 3 + [jax.ShapeDtypeStruct((4, rows, width), bf16)] * 2
    once = pl.BlockSpec((rows, width), lambda i, order: (0, 0), pipeline_mode=pl.Buffered(1))
    anywhere = pl.BlockSpec(memory_space=pl.ANY)
    steps = len(units)
    first = 3 + steps + len(earlier)
    return pl.pallas_call(
        functools.partial(ffn_kernel, 256, steps, len(earlier)),
        out_shape=shapes,
        grid_spec=pltpu.PrefetchScalarGridSpec(
            num_scalar_prefetch=1,
            grid=(steps,),
            in_specs=[once] * steps + [line(width), anywhere] + [stacked] * len(earlier) + [anywhere] * len(held),
            out_specs=[line(hidden)] * 3 + [stacked] * 2,
            scratch_shapes=[
                pltpu.VMEM((width, 3 * hidden), bf16),
                pltpu.VMEM((rows, width), bf16),
                pltpu.SemaphoreType.DMA((BLOCKS,)),
            ],
        ),
        input_output_aliases={first + i: i for i in range(len(held))},
        compiler_params=params(60),
        cost_estimate=cost(12 * steps * rows * width * hidden, 2 * (4 * steps * rows + 3 * hidden) * width),
    )(order, *units, dy, weights, *earlier, *held)


def weight_kernel(layout, order_ref, quarters_ref, *refs):
    refs, out = list(refs[:-1]), refs[-1]
    total = None
    for n_left, n_right in layout:
        lefts, rights = [refs.pop(0)[...] for _ in range(n_left)], [refs.pop(0)[...] for _ in range(n_right)]
        left, right = [jnp.concatenate(item, axis=0) if len(item) > 1 else item[0] for item in (lefts, rights)]
        part = nn(left.T, right)
        total = part if total is None else total + part
    out[...] = total.astype(bf16)


def weight_grads(parts, order, quarters):
    width = parts[0][0][0][0].shape[1]
    rows = width // BLOCKS
    cols = parts[0][1][0][0].shape[1]
    arrays, specs, tokens = [], [], 0
    for pieces in parts:
        for side, side_pieces in enumerate(pieces):
            for array, *place in side_pieces:
                n = array.shape[0] // (1 if not place else 4 if place[0] == "q" else 2)

                def index(i, order, quarters, side=side, place=tuple(place)):
                    row = 0 if not place else quarters[place[1]] if place[0] == "q" else place[0]
                    return (row, 0 if side else i)

                mode = {"pipeline_mode": pl.Buffered(1)} if side else {}
                specs.append(pl.BlockSpec((n, cols if side else rows), index, **mode))
                arrays.append(array)
                tokens += n if side else 0
    return pl.pallas_call(
        functools.partial(weight_kernel, tuple((len(lefts), len(rights)) for lefts, rights in parts)),
        out_shape=jax.ShapeDtypeStruct((width, cols), bf16),
        grid_spec=pltpu.PrefetchScalarGridSpec(
            num_scalar_prefetch=2,
            grid=(BLOCKS,),
            in_specs=specs,
            out_specs=pl.BlockSpec((rows, cols), lambda i, order, quarters: (order[i], 0)),
        ),
        compiler_params=params(48),
        cost_estimate=cost(2 * tokens * width * cols, 2 * (tokens + width) * (width + cols)),
    )(order, quarters, *arrays)


def ffn_weight_kernel(order_ref, down_order_ref, *refs):
    units, (dy_ref, mixed_ref, ggate_ref, gup_ref), outs = refs[:4], refs[4:8], refs[8:]
    cols = ggate_ref.shape[1]
    unit = jnp.concatenate([item[...] for item in units], axis=0).T
    outs[0][:, :cols] = nn(unit, ggate_ref[...]).astype(bf16)
    outs[0][:, cols : 2 * cols] = nn(unit, gup_ref[...]).astype(bf16)
    down = nn(dy_ref[...].T, mixed_ref[...]).astype(bf16)
    if len(outs) == 2:
        outs[1][...] = down
    else:
        outs[0][:, 2 * cols :] = down


def ffn_weight_grads(units, dy, grads, order, down_order=None):
    quarter, width = units[0].shape
    rows = width // BLOCKS
    cols = grads[0].shape[1]
    held = pl.BlockSpec((4 * quarter, cols), lambda i, *orders: (0, 0), pipeline_mode=pl.Buffered(1))
    sizes = [3 * cols] if down_order is None else [2 * cols, cols]
    results = pl.pallas_call(
        ffn_weight_kernel,
        out_shape=[jax.ShapeDtypeStruct((width, n), bf16) for n in sizes],
        grid_spec=pltpu.PrefetchScalarGridSpec(
            num_scalar_prefetch=2,
            grid=(BLOCKS,),
            in_specs=[pl.BlockSpec((quarter, rows), lambda i, *orders: (0, i))] * 4
            + [pl.BlockSpec((4 * quarter, rows), lambda i, *orders: (0, i))]
            + [held] * 3,
            out_specs=[
                pl.BlockSpec((rows, n), lambda i, *orders, place=place: (orders[place][i], 0))
                for place, n in enumerate(sizes)
            ],
        ),
        compiler_params=params(48),
        cost_estimate=cost(24 * quarter * width * cols, 2 * (8 * quarter + width) * (width + 3 * cols)),
    )(order, order if down_order is None else down_order, *units, dy, *grads)
    return results[0] if down_order is None else results


def per_device(
    n_seq,
    n_head,
    tokens,
    doc_reset,
    gain_attn,
    gain_ffn,
    query_weight,
    key_weight,
    value_weight,
    out_weight,
    gate_weight,
    up_weight,
    down_weight,
    grad_out,
):
    rows, length, width = tokens.shape
    heads = query_weight.shape[1] // FEAT
    count = rows * length
    quarter = count // 4
    half = 2 * quarter
    me = lax.axis_index("seq").astype(jnp.int32)
    head_me = lax.axis_index("head").astype(jnp.int32)
    order = jnp.arange(BLOCKS, dtype=jnp.int32)
    if n_seq == 8:
        order = me ^ order
    quarters = head_me ^ jnp.arange(4, dtype=jnp.int32)

    gain_one = gain_attn.astype(f32)[:, None]
    gain_two = gain_ffn.astype(f32)[:, None]
    scaled = lambda weight, gain: (weight.astype(f32) * gain).astype(bf16)
    qkv_own = jnp.concatenate([query_weight, key_weight, value_weight], axis=1)
    gate_own, up_own, down_own = scaled(gate_weight, gain_two), scaled(up_weight, gain_two), down_weight.T
    hidden_units = gate_weight.shape[1]
    cut = hidden_units // (2 * VHEAD) * VHEAD
    groups = (slice(0, cut), slice(cut, hidden_units))
    values = heads * VHEAD
    everywhere = lambda value: lax.all_gather(value, "seq", axis=0, tiled=True)
    ffn_w = []
    for group in groups:
        parts = [gate_own[:, group], up_own[:, group], down_own[:, group]]
        ffn_w.append(everywhere(jnp.concatenate(parts if ffn_w else [out_weight.T] + parts, axis=1)))
    out_w = swap_blocks(ffn_w[0][:, :values], me, n_seq)

    flat = tokens.reshape(count, width)
    x_own = move_blocks(flat, quarters[:1], order, quarter)
    dy = move_blocks(grad_out.reshape(count, width), quarters, order, quarter)
    unit_one = after(unit_rows(flat, order, quarter // 2), x_own, dy)

    docs = jnp.cumsum(doc_reset, axis=1)
    final = docs[:, -1:]
    flag = jnp.broadcast_to(final > 0, docs.shape)
    edges = jnp.stack([docs, docs == 0, docs == final, flag] + [jnp.zeros_like(docs)] * 4, axis=2).astype(f32)
    doc_rows = jnp.broadcast_to(docs[:, None, :], (rows, 8, length)).astype(f32)
    tables, feat_rows, to_key, to_query = feature_tables(heads)
    qkv_pieces = gather_rows(scaled(qkv_own, gain_one), n_seq, (unit_one, edges, doc_rows))

    lanes = 2 * heads * FEAT
    unit_flops = 2 * rows * heads * length * WIDE * VHEAD
    qkv, qkv_w = first_product(unit_one, qkv_pieces, quarter)
    qkv = qkv.reshape(rows, length, lanes + values)
    (states,) = by_row(
        functools.partial(state_kernel, heads),
        rows,
        [(qkv, True), (edges, True), (tables["ka"], False), (tables["kb"], False), (feat_rows, False)],
        [((heads, TALL, VHEAD), bf16)],
        flops=3 * unit_flops,
    )
    numerator, denominator = by_row(
        functools.partial(inside_kernel, heads),
        rows,
        [(qkv, True), (edges, True), (doc_rows, True), (to_key, False)],
        [((length, values), f32), ((length, heads), f32)],
        flops=3 * unit_flops,
    )
    found = scan_begin(states, False, me, n_seq, (numerator,))
    state_in, place = scan_end(found, False, me, n_seq)
    query_tables = [(tables["qa"], False), (tables["qb"], False), (feat_rows, False)]
    key_tables = [(tables["ka"], False), (tables["kb"], False), (feat_rows, False)]
    attended, rden = by_row(
        functools.partial(attend_kernel, heads),
        rows,
        [(qkv, True), (edges, True), (numerator, True), (after(denominator, out_w), True), (state_in, False)]
        + query_tables,
        [((length, values), bf16), ((length, heads), f32)],
        place=place,
        flops=3 * unit_flops,
    )
    attended_flat = attended.reshape(count, values)
    far = quarter_products(attended_flat, out_w, quarters, 3)
    near = quarter_products(attended_flat, out_w, quarters, 1)
    branch = [near[1], near[0], far[1], far[0]]

    branch, _ = scatter_head(branch)
    hidden, unit_two = on_quarter(add_norm_kernel, [x_own, *branch], quarter, [f32, bf16])
    held = []

    def near_rows(units):
        held.extend(feed_forward(units, dy, 0, ffn_w[0], cut, order))
        return held

    units = gather_head(unit_two, near_rows)
    first = feed_forward(units[2:], dy, 2, ffn_w[0], cut, order, held)
    seq_sum = lambda value: lax.psum_scatter(value, "seq", scatter_dimension=0, tiled=True).astype(f32)
    first_grads = ffn_weight_grads(units, dy, first[:3], order, split_order(order, n_seq))
    ffn_grads = [seq_sum(first_grads[0])]
    left = [after(units[0], first_grads), *units[1:]]
    second = feed_forward(left, dy, 0, ffn_w[1], hidden_units - cut, order, earlier=first[3:])
    gunit, ffn_out = [[item[i] for i in range(4)] for item in second[3:]]

    down_pairs = ()
    if n_seq == 8:
        down_other = send(first_grads[1][width // 2 :], "seq", 1, 8)
        gunit[3] = after(gunit[3], down_other)
    else:
        down_pairs = scatter_begin(first_grads[1], n_seq)

    def second_grads(sent):
        pairs = down_pairs or scatter_pairs(after(first_grads[1], sent), down_other)
        left = [after(units[0], sent, *pairs), *units[1:]]
        return ffn_weight_grads(left, dy, second[:3], order), pairs

    terms, (found, down_pairs) = scatter_head(gunit, beside=second_grads)
    down_terms = scatter_sends(down_pairs)
    terms = after(terms, *down_terms)
    grad_hidden, grad_branch = on_quarter(norm_back_kernel, [hidden, dy, *terms], quarter, [f32, bf16])
    ffn_grads.append(seq_sum(after(found, grad_hidden)))
    block_sum = []

    def block_core(near):
        block_sum.append(scatter_core(ffn_out))
        return block_sum

    grad_branch = gather_head(grad_branch, block_core)

    grad_att = back_product(grad_branch, out_w, quarters).reshape(rows, length, values)
    carry, gnum, gden = by_row(
        functools.partial(carry_kernel, heads),
        rows,
        [(qkv, True), (edges, True), (grad_att, True), (attended, True), (rden, True)] + query_tables,
        [((heads, TALL, VHEAD), bf16), ((length, values), bf16), ((length, heads), f32)],
        flops=3 * unit_flops,
    )
    gboth, gval = by_row(
        functools.partial(inside_back_kernel, heads),
        rows,
        [(qkv, True), (edges, True), (doc_rows, True), (gnum, True), (gden, True), (state_in, False)]
        + [(to_key, False), (to_query, False)]
        + query_tables,
        [((length, lanes), f32), ((length, values), f32)],
        place=place,
        flops=11 * unit_flops,
    )
    sides = [[(grad_branch[i],), (grad_branch[i + 1],)] for i in (0, 2)]
    parts = [(side, [(attended_flat, "q", i), (attended_flat, "q", i + 1)]) for side, i in zip(sides, (0, 2))]
    grad_out_w = weight_grads(parts, split_order(order, n_seq), quarters)
    found = scan_begin(carry, True, me, n_seq, (gboth, grad_out_w))
    terms, _ = scatter_head(ffn_out, beside=lambda _: gboth, summed=block_sum[0])
    block_own = (hidden + (terms[0].astype(f32) + terms[1].astype(f32) + terms[2].astype(f32))).astype(bf16)
    carry_in, place_back = scan_end(found, True, me, n_seq)
    carry_in = after(carry_in, block_own)
    block_all = gather_head(block_own, lambda near: (carry_in,))
    far_rows, near_rows = [(head_me // 2 ^ i) * (rows // 2) for i in (1, 0)]

    def finish_back(gval, base):
        (grads,) = by_row(
            functools.partial(finish_back_kernel, heads),
            rows,
            [(qkv, True), (edges, True), (carry_in, False), (gboth, True), (gval, True)] + key_tables,
            [((length, lanes + values), bf16)],
            place=place_back,
            flops=6 * unit_flops,
            base=base,
            count=rows // 2,
        )
        return grads.reshape(count, lanes + values)

    gqkv_far = after(finish_back(gval, far_rows), block_all[2])
    far = quarter_products(gqkv_far, qkv_w, quarters, 3)
    gqkv_near = finish_back(after(gval, far), near_rows)
    near = quarter_products(gqkv_near, qkv_w, quarters, 1)

    def back(value, kind):
        whole = place_quarters(value[:2], quarters, order, kind, 0)
        return place_quarters(value[2:], quarters, order, kind, 2, whole).reshape(rows, length, width)

    rest = hidden_units - cut

    def sum_head(value, earlier):
        pairs = after([send(value, "head", mask, 4) for mask in (1, 2, 3)], earlier)
        return (value + pairs[0]) + (pairs[1] + pairs[2])

    def ffn_outputs(sums):
        sums = jnp.concatenate(sums, axis=1)
        parts = jnp.split(sums, np.cumsum([cut, cut, cut, rest, rest]), axis=1)
        grad_gate, grad_up, grad_down = [jnp.concatenate([parts[i], parts[i + 3]], axis=1) for i in range(3)]
        gain = jnp.sum(gate_weight.astype(f32) * grad_gate + up_weight.astype(f32) * grad_up, axis=1)
        return (grad_gate * gain_two, grad_up * gain_two, grad_down.T), gain

    terms, grad_qkv = scatter_head(
        [near[1], near[0], far[1], far[0]],
        beside=lambda sent: weight_grads(
            [
                ([(after(unit_one, sent), "q", i), (unit_one, "q", i + 1)], [(grads, "q", i), (grads, "q", i + 1)])
                for grads, i in ((gqkv_near, 0), (gqkv_far, 2))
            ],
            split_order(order, n_seq),
            quarters,
        ),
    )
    (grad_x,) = on_quarter(norm_back_kernel, [x_own, grad_hidden, *after(terms, ffn_grads[0])], quarter, [bf16])
    qkv_pairs = scatter_begin(grad_qkv, n_seq)
    qkv_terms = scatter_sends(qkv_pairs)
    out_pairs = scatter_begin(after(grad_out_w, grad_x), n_seq)
    ffn_grads, ffn_gain = ffn_outputs([ffn_grads[0], scatter_end(down_pairs, down_terms), after(ffn_grads[1], grad_x)])
    block_all = back(after(block_all, grad_x), bf16)
    grad_x_all = gather_head(grad_x, lambda near: (*qkv_terms, *out_pairs, ffn_gain, *ffn_grads, block_all))
    out_terms = scatter_sends(out_pairs)
    grad_qkv = scatter_end(qkv_pairs, qkv_terms)
    qkv_gain = jnp.sum(qkv_own.astype(f32) * grad_qkv, axis=1)
    near_placed = place_quarters(grad_x_all[:2], quarters, order, f32, 0)
    out_terms = after(out_terms, near_placed)
    grad_x_all[2] = after(grad_x_all[2], *out_terms)
    grad_x_all = place_quarters(grad_x_all[2:], quarters, order, f32, 2, near_placed).reshape(rows, length, width)
    gains = sum_head(jnp.stack([qkv_gain, ffn_gain]), grad_x_all)
    grad_out_w = scatter_end(out_pairs, out_terms)
    grad_qkv = grad_qkv * gain_one
    narrow = heads * FEAT
    return (
        block_all,
        grad_x_all,
        gains[0],
        gains[1],
        grad_qkv[:, :narrow],
        grad_qkv[:, narrow:lanes],
        grad_qkv[:, lanes:],
        grad_out_w.T,
        *ffn_grads,
    )


def solution(mesh):
    placed = (
        P(None, "seq", None),
        P(None, "seq"),
        P("seq"),
        P("seq"),
        P("seq", "head"),
        P("seq", "head"),
        P("seq", "head"),
        P("head", "seq"),
        P("seq", "head"),
        P("seq", "head"),
        P("head", "seq"),
        P(None, "seq", None),
    )
    return jax.shard_map(
        functools.partial(per_device, mesh.shape["seq"], mesh.shape["head"]),
        mesh=mesh,
        in_specs=placed,
        out_specs=(P(None, "seq", None), P(None, "seq", None)) + placed[2:11],
        check_vma=False,
    )
```

```python
import functools

import jax
import jax.numpy as jnp
import numpy as np
from jax import lax
from jax.experimental import pallas as pl
from jax.experimental.pallas import tpu as pltpu
from jax.sharding import PartitionSpec as P

FEAT = 16
VHEAD = 128
EPSILON = 1e-06
PAIRS = [(a, b) for a in range(FEAT + 1) for b in range(a, FEAT + 1)]
WIDE = 256
TALL = 160
NORM_ROW = len(PAIRS)
FLAG_ROW = NORM_ROW + 2
BLOCKS = 8
COST = 2
bf16, f32 = jnp.bfloat16, jnp.float32


def feature_tables(heads):
    lanes = 2 * heads * FEAT
    tables = {name: np.zeros((lanes, heads * WIDE), np.float32) for name in ("qa", "qb", "ka", "kb")}
    rows = np.zeros((8, heads * WIDE), np.float32)
    to_key = np.zeros((lanes, heads * lanes), np.float32)
    to_query = np.zeros((lanes, heads * lanes), np.float32)
    for head in range(heads):
        for place, (a, b) in enumerate(PAIRS):
            column = head * WIDE + place
            for name, entry, row in (("a", a, 0), ("b", b, 1)):
                if entry == 0:
                    rows[row, column] = 1.0
                else:
                    lane = head * FEAT + entry - 1
                    tables["q" + name][lane, column] = 1.0
                    tables["k" + name][heads * FEAT + lane, column] = 1.0
            rows[2, column] = 1.0 if b == 0 else 0.25 if a == 0 else 1 / 32 if a == b else 1 / 16
        for feat in range(FEAT):
            lane = head * FEAT + feat
            to_key[lane, head * lanes + heads * FEAT + lane] = 0.25
            to_query[heads * FEAT + lane, head * lanes + lane] = 0.25
    tables = {name: jnp.asarray(item, bf16) for name, item in tables.items()}
    return tables, jnp.asarray(rows), jnp.asarray(to_key, bf16), jnp.asarray(to_query, bf16)


def nn(left, right):
    return lax.dot_general(left, right, (((1,), (0,)), ((), ())), preferred_element_type=f32)


def nt(left, right):
    return lax.dot_general(left, right, (((1,), (1,)), ((), ())), preferred_element_type=f32)


def tn(left, right):
    return lax.dot_general(left, right, (((0,), (0,)), ((), ())), preferred_element_type=f32)


def params(mib=32):
    return pltpu.CompilerParams(vmem_limit_bytes=mib << 20)


def cost(flops, nbytes):
    return pl.CostEstimate(flops=int(flops) // COST, bytes_accessed=int(nbytes) // COST, transcendentals=0)


def whole_spec(array):
    zeros = (0,) * array.ndim
    return pl.BlockSpec(array.shape, lambda *_: zeros)


def pack_state(state, norm_row, flag):
    place = lax.broadcasted_iota(jnp.int32, (TALL, VHEAD), 0)
    block = state[:TALL]
    block = jnp.where(place == NORM_ROW, norm_row[:, :VHEAD], block)
    block = jnp.where(place == NORM_ROW + 1, norm_row[:, VHEAD:], block)
    return jnp.where(place == FLAG_ROW, flag, block).astype(bf16)


def unpack_state(block):
    tail = block[TALL - 16 :].astype(f32)
    base = TALL - 16
    low = tail[NORM_ROW - base : NORM_ROW - base + 1]
    high = tail[NORM_ROW + 1 - base : NORM_ROW + 2 - base]
    full = jnp.concatenate([block, jnp.zeros((WIDE - TALL, VHEAD), block.dtype)], axis=0)
    return full, jnp.concatenate([low, high], axis=1)


def state_kernel(heads, place_ref, qkv_ref, edge_ref, ka_ref, kb_ref, rows_ref, out_ref):
    keys = qkv_ref[0, :, : 2 * heads * FEAT]
    edges = edge_ref[0]
    last, flag = edges[:, 2:3], edges[0:1, 3:4]
    for head in range(heads):
        cols = slice(head * WIDE, (head + 1) * WIDE)
        phi = (nn(keys, ka_ref[:, cols]) + rows_ref[0:1, cols]) * (nn(keys, kb_ref[:, cols]) + rows_ref[1:2, cols])
        phi = phi * last
        start = 2 * heads * FEAT + head * VHEAD
        state = tn(phi.astype(bf16), qkv_ref[0, :, start : start + VHEAD])
        out_ref[0, head] = pack_state(state, jnp.sum(phi, axis=0, keepdims=True), flag)


def local_mask(edges, docs):
    length = edges.shape[0]
    later = lax.broadcasted_iota(jnp.int32, (length, length), 0) >= lax.broadcasted_iota(jnp.int32, (length, length), 1)
    return later & (edges[:, 0:1] == docs)


def inside_kernel(heads, place_ref, qkv_ref, edge_ref, doc_ref, key_ref, num_ref, den_ref):
    lanes = 2 * heads * FEAT
    both = qkv_ref[0, :, :lanes]
    mask = local_mask(edge_ref[0], doc_ref[0, 0:1])
    moved = nn(both, key_ref[...]).astype(bf16)
    dens = []
    for head in range(heads):
        scores = nt(moved[:, head * lanes : (head + 1) * lanes], both)
        weights = jnp.where(mask, 1.0 + scores + 0.5 * scores * scores, 0.0)
        dens.append(jnp.sum(weights, axis=1, keepdims=True))
        start = lanes + head * VHEAD
        num_ref[0, :, head * VHEAD : (head + 1) * VHEAD] = nn(
            weights.astype(bf16), qkv_ref[0, :, start : start + VHEAD]
        )
    den_ref[0] = jnp.concatenate(dens, axis=1)


def block_at(place_ref, states_ref, row, heads, head):
    per = states_ref.shape[1]
    index = (place_ref[0] + row) * heads + head
    return states_ref[place_ref[1 + index // per], index % per]


def query_features(both, qa, qb, rows, first):
    left = nn(both, qa) + rows[0:1]
    right = nn(both, qb) + rows[1:2]
    return left, right, left * right * rows[2:3] * first


def attend_kernel(heads, place_ref, qkv_ref, edge_ref, num_ref, den_ref, states_ref, qa_ref, qb_ref, rows_ref, att_ref, rden_ref):
    both = qkv_ref[0, :, : 2 * heads * FEAT]
    first = edge_ref[0][:, 1:2]
    rdens = []
    for head in range(heads):
        cols = slice(head * WIDE, (head + 1) * WIDE)
        _, _, phi = query_features(both, qa_ref[:, cols], qb_ref[:, cols], rows_ref[:, cols], first)
        factor, norm = unpack_state(block_at(place_ref, states_ref, pl.program_id(0), heads, head))
        den = den_ref[0][:, head : head + 1] + jnp.sum(phi * norm, axis=1, keepdims=True)
        rden = 1.0 / den
        out = slice(head * VHEAD, (head + 1) * VHEAD)
        att_ref[0, :, out] = ((num_ref[0, :, out] + nn(phi.astype(bf16), factor)) * rden).astype(bf16)
        rdens.append(rden)
    rden_ref[0] = jnp.concatenate(rdens, axis=1)


def carry_kernel(
    heads, place_ref, qkv_ref, edge_ref, ga_ref, att_ref, rden_ref, qa_ref, qb_ref, rows_ref, carry_ref, gnum_ref, gden_ref
):
    both = qkv_ref[0, :, : 2 * heads * FEAT]
    edges = edge_ref[0]
    first, flag = edges[:, 1:2], edges[0:1, 3:4]
    gdens = []
    for head in range(heads):
        cols = slice(head * WIDE, (head + 1) * WIDE)
        out = slice(head * VHEAD, (head + 1) * VHEAD)
        _, _, phi = query_features(both, qa_ref[:, cols], qb_ref[:, cols], rows_ref[:, cols], first)
        grad = ga_ref[0, :, out].astype(f32)
        rden = rden_ref[0][:, head : head + 1]
        gnum = (grad * rden).astype(bf16)
        gden = -jnp.sum(grad * att_ref[0, :, out].astype(f32), axis=1, keepdims=True) * rden
        gnum_ref[0, :, out] = gnum
        carry_ref[0, head] = pack_state(
            tn(phi.astype(bf16), gnum), jnp.sum(phi * gden, axis=0, keepdims=True), flag
        )
        gdens.append(gden)
    gden_ref[0] = jnp.concatenate(gdens, axis=1)


def inside_back_kernel(
    heads, place_ref, qkv_ref, edge_ref, doc_ref, gnum_ref, gden_ref, states_ref, key_ref, query_ref, qa_ref, qb_ref,
    rows_ref, gboth_ref, gval_ref,
):
    lanes = 2 * heads * FEAT
    both = qkv_ref[0, :, :lanes]
    edges = edge_ref[0]
    first = edges[:, 1:2]
    mask = local_mask(edges, doc_ref[0, 0:1])
    moved = nn(both, key_ref[...]).astype(bf16)
    back = nn(both, query_ref[...]).astype(bf16)
    total = jnp.zeros((both.shape[0], lanes), f32)
    for head in range(heads):
        cols = slice(head * WIDE, (head + 1) * WIDE)
        out = slice(head * VHEAD, (head + 1) * VHEAD)
        own = slice(head * lanes, (head + 1) * lanes)
        start = lanes + head * VHEAD
        values = qkv_ref[0, :, start : start + VHEAD]
        gnum = gnum_ref[0, :, out]
        gden = gden_ref[0][:, head : head + 1]
        scores = nt(moved[:, own], both)
        weights = jnp.where(mask, 1.0 + scores + 0.5 * scores * scores, 0.0).astype(bf16)
        gval_ref[0, :, out] = tn(weights, gnum)
        gscores = jnp.where(mask, (nt(gnum, values) + gden) * (1.0 + scores), 0.0).astype(bf16)
        total = total + nn(gscores, back[:, own]) + tn(gscores, moved[:, own])
        left, right, _ = query_features(both, qa_ref[:, cols], qb_ref[:, cols], rows_ref[:, cols], first)
        factor, norm = unpack_state(block_at(place_ref, states_ref, pl.program_id(0), heads, head))
        place = lax.broadcasted_iota(jnp.int32, (1, WIDE), 1)
        gphi = jnp.where(place < NORM_ROW, (nt(gnum, factor) + norm * gden) * rows_ref[2:3, cols], 0.0) * first
        total = total + nt((gphi * right).astype(bf16), qa_ref[:, cols]) + nt((gphi * left).astype(bf16), qb_ref[:, cols])
    gboth_ref[0] = total


def finish_back_kernel(
    heads, place_ref, qkv_ref, edge_ref, carry_ref, gboth_ref, gval_ref, ka_ref, kb_ref, rows_ref, out_ref
):
    lanes = 2 * heads * FEAT
    both = qkv_ref[0, :, :lanes]
    last = edge_ref[0][:, 2:3]
    total = gboth_ref[0]
    for head in range(heads):
        cols = slice(head * WIDE, (head + 1) * WIDE)
        start = lanes + head * VHEAD
        values = qkv_ref[0, :, start : start + VHEAD]
        left = nn(both, ka_ref[:, cols]) + rows_ref[0:1, cols]
        right = nn(both, kb_ref[:, cols]) + rows_ref[1:2, cols]
        factor, norm = unpack_state(block_at(place_ref, carry_ref, pl.program_id(0), heads, head))
        phi = (left * right * last).astype(bf16)
        gval = gval_ref[0, :, head * VHEAD : (head + 1) * VHEAD] + nn(phi, factor)
        out_ref[0, :, start : start + VHEAD] = gval.astype(bf16)
        place = lax.broadcasted_iota(jnp.int32, (1, WIDE), 1)
        gphi = jnp.where(place < NORM_ROW, nt(values, factor) + norm, 0.0) * last
        total = total + nt((gphi * right).astype(bf16), ka_ref[:, cols]) + nt((gphi * left).astype(bf16), kb_ref[:, cols])
    out_ref[0, :, :lanes] = total.astype(bf16)


def by_row(kernel, rows, inputs, outputs, place=None, flops=0, base=0, count=None):
    count = rows if count is None else count
    arrays = [array for array, _ in inputs]

    def spec_of(array):
        zeros = (0,) * (array.ndim - 1)
        return pl.BlockSpec((1,) + array.shape[1:], lambda row, scalars: (row + scalars[0],) + zeros)

    shapes = [jax.ShapeDtypeStruct((rows,) + shape, kind) for shape, kind in outputs]
    nbytes = sum(item.size * item.dtype.itemsize for item in arrays + shapes)
    scalars = jnp.asarray(base, jnp.int32).reshape(1)
    if place is not None:
        scalars = jnp.concatenate([scalars, place])
    return pl.pallas_call(
        kernel,
        out_shape=shapes,
        grid_spec=pltpu.PrefetchScalarGridSpec(
            num_scalar_prefetch=1,
            grid=(count,),
            in_specs=[spec_of(array) if per_row else whole_spec(array) for array, per_row in inputs],
            out_specs=[spec_of(shape) for shape in shapes],
        ),
        compiler_params=params(40),
        cost_estimate=cost(flops * count // rows, nbytes * count // rows),
    )(scalars, *arrays)


def scan_kernel(backward, me_ref, *refs):
    pieces, outs, (held, ahead) = refs[:8], refs[8:16], refs[16:]
    for rel in range(8):
        held[rel] = pieces[rel][...]
    me = me_ref[0]
    for block in range(held.shape[1]):
        run = jnp.zeros(held.shape[2:], f32)
        for step in range(8):
            rel = me ^ (7 - step if backward else step)
            ahead[rel, block] = run.astype(bf16)
            own = held[rel, block].astype(f32)
            run = own + (1.0 - own[FLAG_ROW : FLAG_ROW + 1]) * run
    for rel in range(8):
        outs[rel][...] = ahead[rel]


def scan_begin(states, backward, me, count, earlier=()):
    blocks = states.shape[0] * states.shape[1]
    flat = states.reshape(blocks, TALL, VHEAD)
    if count != 8 or blocks % 8:
        return lax.all_gather(flat, "seq").astype(f32)
    per = blocks // 8
    split = flat.reshape(8, per, TALL, VHEAD)
    parts = [lax.dynamic_index_in_dim(split, me ^ rel, 0, keepdims=False) for rel in range(8)]
    pieces = [after(parts[0], *earlier)] + [send(parts[rel], "seq", rel, 8) for rel in range(1, 8)]
    return pl.pallas_call(
        functools.partial(scan_kernel, backward),
        out_shape=[jax.ShapeDtypeStruct((per, TALL, VHEAD), bf16)] * 8,
        in_specs=[pl.BlockSpec(memory_space=pltpu.SMEM)] + [pl.BlockSpec(memory_space=pltpu.VMEM)] * 8,
        out_specs=[pl.BlockSpec(memory_space=pltpu.VMEM)] * 8,
        scratch_shapes=[pltpu.VMEM((8, per, TALL, VHEAD), bf16)] * 2,
        compiler_params=params(),
    )(me.reshape(1), *pieces)


def scan_end(found, backward, me, count):
    if isinstance(found, (list, tuple)):
        back = [found[0]] + [send(found[rel], "seq", rel, 8) for rel in range(1, 8)]
        return jnp.stack(back), me ^ jnp.arange(8, dtype=jnp.int32)
    keep = 1.0 - found[:, :, FLAG_ROW : FLAG_ROW + 1]
    run = jnp.zeros(found.shape[1:], f32)
    for step in range(count):
        at = count - 1 - step if backward else step
        reached = at > me if backward else at < me
        run = jnp.where(reached, found[at] + keep[at] * run, run)
    return run.astype(bf16)[None], jnp.zeros((1,), jnp.int32)


def send(value, axis, mask, count):
    return lax.ppermute(value, axis, [(i, i ^ mask) for i in range(count)])


def gather_rows(shard, count, earlier):
    if count != 8:
        return [lax.all_gather(shard, "seq", axis=0, tiled=True)]
    pieces = [shard, send(shard, "seq", 1, 8)]
    for mask in (2, 4, 6):
        piece = send(shard, "seq", mask, 8)
        piece = after(piece, *earlier) if mask == 2 else piece
        pieces += [piece, send(piece, "seq", 1, 8)]
    return pieces


def after(value, *earlier):
    return lax.optimization_barrier((value, earlier))[0]


def swap_blocks(array, me, count):
    if count != 8:
        return array
    split = array.reshape((BLOCKS, array.shape[0] // BLOCKS) + array.shape[1:])
    return join_rows([lax.dynamic_index_in_dim(split, me ^ i, 0, keepdims=False) for i in range(BLOCKS)])


def split_order(order, n_seq):
    return jnp.array([0, 4, 1, 5, 2, 6, 3, 7], jnp.int32) if n_seq == 8 else order


def scatter_begin(whole, n_seq):
    if n_seq != 8:
        return (lax.psum_scatter(whole, "seq", scatter_dimension=0, tiled=True).astype(f32),)
    return scatter_pairs(whole, send(whole[whole.shape[0] // 2 :], "seq", 1, 8))


def scatter_pairs(whole, other):
    rows = whole.shape[0] // 8
    pairs = [
        whole[i * rows : (i + 1) * rows].astype(f32) + other[i * rows : (i + 1) * rows].astype(f32) for i in range(4)
    ]
    return (pairs[0],) + tuple(pair.astype(bf16) for pair in pairs[1:])


def scatter_sends(pairs):
    return [send(pair, "seq", 2 * place + 2, 8) for place, pair in enumerate(pairs[1:])]


def scatter_end(pairs, terms):
    total = pairs[0]
    for term in terms:
        total = total + term.astype(f32)
    return total


def join_rows(pieces):
    return pieces[0] if len(pieces) == 1 else jnp.concatenate(pieces, axis=0)


CORE, ACROSS = 1, 2


def scatter_core(quarters):
    return (quarters[2].astype(f32) + send(quarters[3], "head", CORE, 4).astype(f32)).astype(bf16)


def scatter_head(quarters, beside=None, summed=None):
    summed = scatter_core(quarters) if summed is None else summed
    across = send(summed, "head", ACROSS, 4)
    near = send(quarters[1], "head", CORE, 4)
    found = () if beside is None else beside(summed)
    return (quarters[0], near, after(across, found)), found


def gather_head(own, between=lambda near: ()):
    near = [own, send(own, "head", CORE, 4)]
    across = after(send(own, "head", ACROSS, 4), *between(near))
    return near + [across, send(across, "head", CORE, 4)]


def move_columns(cols_ref, in_ref, out_ref):
    width = in_ref.shape[1] // BLOCKS
    for block in range(BLOCKS):
        start = pl.multiple_of(cols_ref[block] * width, 128)
        out_ref[:, block * width : (block + 1) * width] = in_ref[:, pl.ds(start, width)].astype(out_ref.dtype)


def move_kernel(rows_ref, cols_ref, in_ref, out_ref):
    move_columns(cols_ref, in_ref, out_ref)


def move_blocks(array, row_blocks, col_blocks, quarter):
    width = array.shape[1]
    split = 2 if quarter % 32 == 0 else 1
    tile = quarter // split
    count = row_blocks.shape[0]
    return pl.pallas_call(
        move_kernel,
        out_shape=jax.ShapeDtypeStruct((count * quarter, width), array.dtype),
        grid_spec=pltpu.PrefetchScalarGridSpec(
            num_scalar_prefetch=2,
            grid=(count, split),
            in_specs=[pl.BlockSpec((tile, width), lambda i, j, rows, cols: (rows[i] * split + j, 0))],
            out_specs=pl.BlockSpec((tile, width), lambda i, j, rows, cols: (i * split + j, 0)),
        ),
        compiler_params=params(),
        cost_estimate=cost(0, 2 * count * quarter * width * array.dtype.itemsize),
    )(row_blocks, col_blocks, array)


def place_kernel(rows_ref, cols_ref, *refs):
    pieces, out_ref = refs[:2], refs[-1]
    for place, piece in enumerate(pieces):
        pl.when(pl.program_id(0) == place)(functools.partial(move_columns, cols_ref, piece, out_ref))


def place_quarters(pieces, row_blocks, col_blocks, out_type, start, whole=None):
    quarter, width = pieces[0].shape
    shape = jax.ShapeDtypeStruct((4 * quarter, width), out_type)
    held = [] if whole is None else [whole]
    return pl.pallas_call(
        place_kernel,
        out_shape=shape,
        grid_spec=pltpu.PrefetchScalarGridSpec(
            num_scalar_prefetch=2,
            grid=(2,),
            in_specs=[pl.BlockSpec((quarter, width), lambda i, rows, cols: (0, 0))] * 2
            + [pl.BlockSpec(memory_space=pl.ANY)] * len(held),
            out_specs=pl.BlockSpec((quarter, width), lambda i, rows, cols: (rows[start + i], 0)),
        ),
        input_output_aliases={4: 0} if held else {},
        compiler_params=params(40),
        cost_estimate=cost(0, shape.size * 4),
    )(row_blocks, col_blocks, *pieces, *held)


def unit_kernel(cols_ref, in_ref, out_ref):
    values = in_ref[...].astype(f32)
    rstd = lax.rsqrt(jnp.mean(values * values, axis=1, keepdims=True) + EPSILON)
    width = in_ref.shape[1] // BLOCKS
    for block in range(BLOCKS):
        start = pl.multiple_of(cols_ref[block] * width, 128)
        out_ref[:, block * width : (block + 1) * width] = (in_ref[:, pl.ds(start, width)].astype(f32) * rstd).astype(bf16)


def unit_rows(array, col_blocks, tile):
    rows, width = array.shape
    return pl.pallas_call(
        unit_kernel,
        out_shape=jax.ShapeDtypeStruct((rows, width), bf16),
        grid_spec=pltpu.PrefetchScalarGridSpec(
            num_scalar_prefetch=1,
            grid=(rows // tile,),
            in_specs=[pl.BlockSpec((tile, width), lambda i, cols: (i, 0))],
            out_specs=pl.BlockSpec((tile, width), lambda i, cols: (i, 0)),
        ),
        compiler_params=params(),
        cost_estimate=cost(0, 4 * rows * width),
    )(col_blocks, array)


def fit(rows):
    return next(tile for tile in (128, 96, 64, 48, 32, 16) if rows % tile == 0)


def add_norm_kernel(base_ref, a_ref, b_ref, c_ref, sum_ref, unit_ref):
    total = base_ref[...].astype(f32) + (a_ref[...].astype(f32) + b_ref[...].astype(f32) + c_ref[...].astype(f32))
    rstd = lax.rsqrt(jnp.mean(total * total, axis=1, keepdims=True) + EPSILON)
    sum_ref[...] = total
    unit_ref[...] = (total * rstd).astype(bf16)


def norm_back_kernel(base_ref, rest_ref, a_ref, b_ref, c_ref, *outs):
    base = base_ref[...].astype(f32)
    rstd = lax.rsqrt(jnp.mean(base * base, axis=1, keepdims=True) + EPSILON)
    unit = base * rstd
    grad = a_ref[...].astype(f32) + b_ref[...].astype(f32) + c_ref[...].astype(f32)
    total = rest_ref[...].astype(f32) + rstd * (grad - unit * jnp.mean(grad * unit, axis=1, keepdims=True))
    for out in outs:
        out[...] = total.astype(out.dtype)


def on_quarter(kernel, arrays, rows, out_types):
    width = arrays[0].shape[1]
    tile = fit(rows)
    spec = pl.BlockSpec((tile, width), lambda i: (i, 0))
    return pl.pallas_call(
        kernel,
        out_shape=[jax.ShapeDtypeStruct((rows, width), kind) for kind in out_types],
        grid=(rows // tile,),
        in_specs=[spec] * len(arrays),
        out_specs=[spec] * len(out_types),
        compiler_params=params(),
        cost_estimate=cost(0, rows * width * 16),
    )(*arrays)


def first_kernel(n, unit_ref, *refs):
    pieces, (out_ref, joined_ref, held_ref, sems) = refs[:n], refs[n:]
    rows = held_ref.shape[0] // n

    @pl.when(pl.program_id(0) == 0)
    def _():
        copies = [pltpu.make_async_copy(pieces[i], held_ref.at[pl.ds(i * rows, rows)], sems.at[i]) for i in range(n)]
        for copy in copies:
            copy.start()
        for copy in copies:
            copy.wait()
        joined_ref[...] = held_ref[...]

    out_ref[...] = nn(unit_ref[...], held_ref[...]).astype(bf16)


def first_product(unit, pieces, tile):
    tokens, width = unit.shape
    cols = pieces[0].shape[1]
    return pl.pallas_call(
        functools.partial(first_kernel, len(pieces)),
        out_shape=[jax.ShapeDtypeStruct((tokens, cols), bf16), jax.ShapeDtypeStruct((width, cols), bf16)],
        grid=(tokens // tile,),
        in_specs=[pl.BlockSpec((tile, width), lambda i: (i, 0))] + [pl.BlockSpec(memory_space=pl.ANY)] * len(pieces),
        out_specs=[pl.BlockSpec((tile, cols), lambda i: (i, 0)), pl.BlockSpec((width, cols), lambda i: (0, 0))],
        scratch_shapes=[pltpu.VMEM((width, cols), bf16), pltpu.SemaphoreType.DMA((len(pieces),))],
        compiler_params=params(),
        cost_estimate=cost(2 * tokens * width * cols, 2 * (tokens + width) * (width + cols)),
    )(unit, *pieces)


def quarter_kernel(order_ref, in_ref, weight_ref, *outs):
    values = in_ref[...]
    width = weight_ref.shape[0]
    for start in range(0, width, 512):
        part = nt(values, weight_ref[start : start + 512]).astype(bf16)
        for place, out in enumerate(outs):

            @pl.when(pl.program_id(0) == place)
            def _(out=out, part=part, start=start):
                out[:, start : start + 512] = part


def quarter_products(array, weight, quarters, top):
    width, cols = weight.shape
    rows = array.shape[0] // 4
    return pl.pallas_call(
        quarter_kernel,
        out_shape=[jax.ShapeDtypeStruct((rows, width), bf16)] * 2,
        grid_spec=pltpu.PrefetchScalarGridSpec(
            num_scalar_prefetch=1,
            grid=(2,),
            in_specs=[
                pl.BlockSpec((rows, cols), lambda i, order: (order[top - i], 0)),
                pl.BlockSpec((width, cols), lambda i, order: (0, 0), pipeline_mode=pl.Buffered(1)),
            ],
            out_specs=[pl.BlockSpec((rows, width), lambda i, order: (0, 0))] * 2,
        ),
        compiler_params=params(),
        cost_estimate=cost(4 * rows * width * cols, 4 * rows * width),
    )(quarters, array, weight)


def back_kernel(order_ref, *refs):
    pieces, weight_ref, out_ref = refs[:4], refs[4], refs[5]
    for place, piece in enumerate(pieces):

        @pl.when(pl.program_id(0) == place)
        def _(piece=piece):
            out_ref[...] = nn(piece[...], weight_ref[...]).astype(bf16)


def back_product(pieces, weight, quarters):
    rows, width = pieces[0].shape
    cols = weight.shape[1]
    return pl.pallas_call(
        back_kernel,
        out_shape=jax.ShapeDtypeStruct((4 * rows, cols), bf16),
        grid_spec=pltpu.PrefetchScalarGridSpec(
            num_scalar_prefetch=1,
            grid=(4,),
            in_specs=[pl.BlockSpec((rows, width), lambda i, order: (0, 0), pipeline_mode=pl.Buffered(1))] * 4
            + [pl.BlockSpec((width, cols), lambda i, order: (0, 0), pipeline_mode=pl.Buffered(1))],
            out_specs=pl.BlockSpec((rows, cols), lambda i, order: (order[i], 0)),
        ),
        compiler_params=params(),
        cost_estimate=cost(8 * rows * width * cols, 8 * rows * width),
    )(quarters, *pieces, weight)


def ffn_kernel(step, n_units, n_earlier, order_ref, *refs):
    units, dy_ref, weights_hbm = refs[:n_units], refs[n_units], refs[n_units + 1]
    earlier, refs = refs[n_units + 2 : n_units + 2 + n_earlier], refs[-8:]
    mixed_ref, ggate_ref, gup_ref, gunit_ref, out_ref, held_ref, unit_ref, sems = refs
    width, hidden = held_ref.shape[0], held_ref.shape[1] // 3
    rows = width // BLOCKS
    copies = []
    for i in range(BLOCKS):
        start = pl.multiple_of(order_ref[i] * rows, rows)
        source = weights_hbm.at[pl.ds(start, rows), pl.ds(weights_hbm.shape[1] - 3 * hidden, 3 * hidden)]
        copies.append(pltpu.make_async_copy(source, held_ref.at[pl.ds(i * rows, rows)], sems.at[i]))

    @pl.when(pl.program_id(0) == 0)
    def _():
        for copy in copies:
            copy.start()
        for copy in copies:
            copy.wait()

    for place, unit in enumerate(units):

        @pl.when(pl.program_id(0) == place)
        def _(unit=unit):
            unit_ref[...] = unit[...]

    unit, dy = unit_ref[...], dy_ref[...]
    for start in range(0, hidden, step):
        stop = min(start + step, hidden)
        cols = slice(start, stop)
        gate = nn(unit, held_ref[:, start:stop])
        up = nn(unit, held_ref[:, hidden + start : hidden + stop])
        gmixed = nn(dy, held_ref[:, 2 * hidden + start : 2 * hidden + stop])
        sig = jax.nn.sigmoid(gate)
        silu = gate * sig
        mixed_ref[:, cols] = (silu * up).astype(bf16)
        ggate_ref[:, cols] = (gmixed * up * (sig * (1.0 + gate * (1.0 - sig)))).astype(bf16)
        gup_ref[:, cols] = (gmixed * silu).astype(bf16)
    ggate, gup, mixed = ggate_ref[...], gup_ref[...], mixed_ref[...]
    for start in range(0, width, 512):
        cols = slice(start, start + 512)
        gunit = nt(ggate, held_ref[cols, :hidden]) + nt(gup, held_ref[cols, hidden : 2 * hidden])
        out = nt(mixed, held_ref[cols, 2 * hidden :])
        if earlier:
            gunit = gunit + earlier[0][0, :, cols].astype(f32)
            out = out + earlier[1][0, :, cols].astype(f32)
        gunit_ref[0, :, cols] = gunit.astype(bf16)
        out_ref[0, :, cols] = out.astype(bf16)


def feed_forward(units, dy, start, weights, hidden, order, held=(), earlier=()):
    rows, width = units[0].shape
    line = lambda cols: pl.BlockSpec((rows, cols), lambda i, order: (i + start, 0))
    stacked = pl.BlockSpec((1, rows, width), lambda i, order: (i + start, 0, 0))
    shapes = [jax.ShapeDtypeStruct((4 * rows, hidden), bf16)] * 3 + [jax.ShapeDtypeStruct((4, rows, width), bf16)] * 2
    once = pl.BlockSpec((rows, width), lambda i, order: (0, 0), pipeline_mode=pl.Buffered(1))
    anywhere = pl.BlockSpec(memory_space=pl.ANY)
    steps = len(units)
    first = 3 + steps + len(earlier)
    return pl.pallas_call(
        functools.partial(ffn_kernel, 256, steps, len(earlier)),
        out_shape=shapes,
        grid_spec=pltpu.PrefetchScalarGridSpec(
            num_scalar_prefetch=1,
            grid=(steps,),
            in_specs=[once] * steps + [line(width), anywhere] + [stacked] * len(earlier) + [anywhere] * len(held),
            out_specs=[line(hidden)] * 3 + [stacked] * 2,
            scratch_shapes=[
                pltpu.VMEM((width, 3 * hidden), bf16),
                pltpu.VMEM((rows, width), bf16),
                pltpu.SemaphoreType.DMA((BLOCKS,)),
            ],
        ),
        input_output_aliases={first + i: i for i in range(len(held))},
        compiler_params=params(60),
        cost_estimate=cost(12 * steps * rows * width * hidden, 2 * (4 * steps * rows + 3 * hidden) * width),
    )(order, *units, dy, weights, *earlier, *held)


def weight_kernel(layout, order_ref, quarters_ref, *refs):
    refs, out = list(refs[:-1]), refs[-1]
    total = None
    for n_left, n_right in layout:
        lefts, rights = [refs.pop(0)[...] for _ in range(n_left)], [refs.pop(0)[...] for _ in range(n_right)]
        left, right = [jnp.concatenate(item, axis=0) if len(item) > 1 else item[0] for item in (lefts, rights)]
        part = nn(left.T, right)
        total = part if total is None else total + part
    out[...] = total.astype(bf16)


def weight_grads(parts, order, quarters):
    width = parts[0][0][0][0].shape[1]
    rows = width // BLOCKS
    cols = parts[0][1][0][0].shape[1]
    arrays, specs, tokens = [], [], 0
    for pieces in parts:
        for side, side_pieces in enumerate(pieces):
            for array, *place in side_pieces:
                n = array.shape[0] // (1 if not place else 4 if place[0] == "q" else 2)

                def index(i, order, quarters, side=side, place=tuple(place)):
                    row = 0 if not place else quarters[place[1]] if place[0] == "q" else place[0]
                    return (row, 0 if side else i)

                mode = {"pipeline_mode": pl.Buffered(1)} if side else {}
                specs.append(pl.BlockSpec((n, cols if side else rows), index, **mode))
                arrays.append(array)
                tokens += n if side else 0
    return pl.pallas_call(
        functools.partial(weight_kernel, tuple((len(lefts), len(rights)) for lefts, rights in parts)),
        out_shape=jax.ShapeDtypeStruct((width, cols), bf16),
        grid_spec=pltpu.PrefetchScalarGridSpec(
            num_scalar_prefetch=2,
            grid=(BLOCKS,),
            in_specs=specs,
            out_specs=pl.BlockSpec((rows, cols), lambda i, order, quarters: (order[i], 0)),
        ),
        compiler_params=params(48),
        cost_estimate=cost(2 * tokens * width * cols, 2 * (tokens + width) * (width + cols)),
    )(order, quarters, *arrays)


def ffn_weight_kernel(order_ref, down_order_ref, *refs):
    units, (dy_ref, mixed_ref, ggate_ref, gup_ref), outs = refs[:4], refs[4:8], refs[8:]
    cols = ggate_ref.shape[1]
    unit = jnp.concatenate([item[...] for item in units], axis=0).T
    outs[0][:, :cols] = nn(unit, ggate_ref[...]).astype(bf16)
    outs[0][:, cols : 2 * cols] = nn(unit, gup_ref[...]).astype(bf16)
    down = nn(dy_ref[...].T, mixed_ref[...]).astype(bf16)
    if len(outs) == 2:
        outs[1][...] = down
    else:
        outs[0][:, 2 * cols :] = down


def ffn_weight_grads(units, dy, grads, order, down_order=None):
    quarter, width = units[0].shape
    rows = width // BLOCKS
    cols = grads[0].shape[1]
    held = pl.BlockSpec((4 * quarter, cols), lambda i, *orders: (0, 0), pipeline_mode=pl.Buffered(1))
    sizes = [3 * cols] if down_order is None else [2 * cols, cols]
    results = pl.pallas_call(
        ffn_weight_kernel,
        out_shape=[jax.ShapeDtypeStruct((width, n), bf16) for n in sizes],
        grid_spec=pltpu.PrefetchScalarGridSpec(
            num_scalar_prefetch=2,
            grid=(BLOCKS,),
            in_specs=[pl.BlockSpec((quarter, rows), lambda i, *orders: (0, i))] * 4
            + [pl.BlockSpec((4 * quarter, rows), lambda i, *orders: (0, i))]
            + [held] * 3,
            out_specs=[
                pl.BlockSpec((rows, n), lambda i, *orders, place=place: (orders[place][i], 0))
                for place, n in enumerate(sizes)
            ],
        ),
        compiler_params=params(48),
        cost_estimate=cost(24 * quarter * width * cols, 2 * (8 * quarter + width) * (width + 3 * cols)),
    )(order, order if down_order is None else down_order, *units, dy, *grads)
    return results[0] if down_order is None else results


def per_device(
    n_seq,
    n_head,
    tokens,
    doc_reset,
    gain_attn,
    gain_ffn,
    query_weight,
    key_weight,
    value_weight,
    out_weight,
    gate_weight,
    up_weight,
    down_weight,
    grad_out,
):
    rows, length, width = tokens.shape
    heads = query_weight.shape[1] // FEAT
    count = rows * length
    quarter = count // 4
    half = 2 * quarter
    me = lax.axis_index("seq").astype(jnp.int32)
    head_me = lax.axis_index("head").astype(jnp.int32)
    order = jnp.arange(BLOCKS, dtype=jnp.int32)
    if n_seq == 8:
        order = me ^ order
    quarters = head_me ^ jnp.arange(4, dtype=jnp.int32)

    gain_one = gain_attn.astype(f32)[:, None]
    gain_two = gain_ffn.astype(f32)[:, None]
    scaled = lambda weight, gain: (weight.astype(f32) * gain).astype(bf16)
    qkv_own = jnp.concatenate([query_weight, key_weight, value_weight], axis=1)
    gate_own, up_own, down_own = scaled(gate_weight, gain_two), scaled(up_weight, gain_two), down_weight.T
    hidden_units = gate_weight.shape[1]
    cut = hidden_units // (2 * VHEAD) * VHEAD
    groups = (slice(0, cut), slice(cut, hidden_units))
    values = heads * VHEAD
    everywhere = lambda value: lax.all_gather(value, "seq", axis=0, tiled=True)
    ffn_w = []
    for group in groups:
        parts = [gate_own[:, group], up_own[:, group], down_own[:, group]]
        ffn_w.append(everywhere(jnp.concatenate(parts if ffn_w else [out_weight.T] + parts, axis=1)))
    out_w = swap_blocks(ffn_w[0][:, :values], me, n_seq)

    flat = tokens.reshape(count, width)
    x_own = move_blocks(flat, quarters[:1], order, quarter)
    dy = move_blocks(grad_out.reshape(count, width), quarters, order, quarter)
    unit_one = after(unit_rows(flat, order, quarter // 2), x_own, dy)

    docs = jnp.cumsum(doc_reset, axis=1)
    final = docs[:, -1:]
    flag = jnp.broadcast_to(final > 0, docs.shape)
    edges = jnp.stack([docs, docs == 0, docs == final, flag] + [jnp.zeros_like(docs)] * 4, axis=2).astype(f32)
    doc_rows = jnp.broadcast_to(docs[:, None, :], (rows, 8, length)).astype(f32)
    tables, feat_rows, to_key, to_query = feature_tables(heads)
    qkv_pieces = gather_rows(scaled(qkv_own, gain_one), n_seq, (unit_one, edges, doc_rows))

    lanes = 2 * heads * FEAT
    unit_flops = 2 * rows * heads * length * WIDE * VHEAD
    qkv, qkv_w = first_product(unit_one, qkv_pieces, quarter)
    qkv = qkv.reshape(rows, length, lanes + values)
    (states,) = by_row(
        functools.partial(state_kernel, heads),
        rows,
        [(qkv, True), (edges, True), (tables["ka"], False), (tables["kb"], False), (feat_rows, False)],
        [((heads, TALL, VHEAD), bf16)],
        flops=3 * unit_flops,
    )
    numerator, denominator = by_row(
        functools.partial(inside_kernel, heads),
        rows,
        [(qkv, True), (edges, True), (doc_rows, True), (to_key, False)],
        [((length, values), f32), ((length, heads), f32)],
        flops=3 * unit_flops,
    )
    found = scan_begin(states, False, me, n_seq, (numerator,))
    state_in, place = scan_end(found, False, me, n_seq)
    query_tables = [(tables["qa"], False), (tables["qb"], False), (feat_rows, False)]
    key_tables = [(tables["ka"], False), (tables["kb"], False), (feat_rows, False)]
    attended, rden = by_row(
        functools.partial(attend_kernel, heads),
        rows,
        [(qkv, True), (edges, True), (numerator, True), (after(denominator, out_w), True), (state_in, False)]
        + query_tables,
        [((length, values), bf16), ((length, heads), f32)],
        place=place,
        flops=3 * unit_flops,
    )
    attended_flat = attended.reshape(count, values)
    far = quarter_products(attended_flat, out_w, quarters, 3)
    near = quarter_products(attended_flat, out_w, quarters, 1)
    branch = [near[1], near[0], far[1], far[0]]

    branch, _ = scatter_head(branch)
    hidden, unit_two = on_quarter(add_norm_kernel, [x_own, *branch], quarter, [f32, bf16])
    held = []

    def near_rows(units):
        held.extend(feed_forward(units, dy, 0, ffn_w[0], cut, order))
        return held

    units = gather_head(unit_two, near_rows)
    first = feed_forward(units[2:], dy, 2, ffn_w[0], cut, order, held)
    seq_sum = lambda value: lax.psum_scatter(value, "seq", scatter_dimension=0, tiled=True).astype(f32)
    first_grads = ffn_weight_grads(units, dy, first[:3], order, split_order(order, n_seq))
    ffn_grads = [seq_sum(first_grads[0])]
    left = [after(units[0], first_grads), *units[1:]]
    second = feed_forward(left, dy, 0, ffn_w[1], hidden_units - cut, order, earlier=first[3:])
    gunit = [None, None, second[3][2], second[3][3]]
    ffn_out = [second[4][i] for i in range(4)]

    down_pairs = ()
    if n_seq == 8:
        down_other = send(first_grads[1][width // 2 :], "seq", 1, 8)
        gunit[3] = after(gunit[3], down_other)
    else:
        down_pairs = scatter_begin(first_grads[1], n_seq)

    def second_grads(sent):
        pairs = down_pairs or scatter_pairs(after(first_grads[1], sent), down_other)
        left = [after(units[0], sent, *pairs), *units[1:]]
        return ffn_weight_grads(left, dy, second[:3], order), pairs

    summed = scatter_core(gunit)
    near_sums = after(second[3], summed)
    gunit = [near_sums[0], near_sums[1], *gunit[2:]]
    terms, (found, down_pairs) = scatter_head(gunit, beside=second_grads, summed=summed)
    down_terms = scatter_sends(down_pairs)
    terms = after(terms, *down_terms)
    grad_hidden, grad_branch = on_quarter(norm_back_kernel, [hidden, dy, *terms], quarter, [f32, bf16])
    ffn_grads.append(seq_sum(after(found, grad_hidden)))
    block_sum = []

    def block_core(near):
        block_sum.append(scatter_core(ffn_out))
        return block_sum

    grad_branch = gather_head(grad_branch, block_core)

    grad_att = back_product(grad_branch, out_w, quarters).reshape(rows, length, values)
    carry, gnum, gden = by_row(
        functools.partial(carry_kernel, heads),
        rows,
        [(qkv, True), (edges, True), (grad_att, True), (attended, True), (rden, True)] + query_tables,
        [((heads, TALL, VHEAD), bf16), ((length, values), bf16), ((length, heads), f32)],
        flops=3 * unit_flops,
    )
    gboth, gval = by_row(
        functools.partial(inside_back_kernel, heads),
        rows,
        [(qkv, True), (edges, True), (doc_rows, True), (gnum, True), (gden, True), (state_in, False)]
        + [(to_key, False), (to_query, False)]
        + query_tables,
        [((length, lanes), f32), ((length, values), f32)],
        place=place,
        flops=11 * unit_flops,
    )
    sides = [[(grad_branch[i],), (grad_branch[i + 1],)] for i in (0, 2)]
    parts = [(side, [(attended_flat, "q", i), (attended_flat, "q", i + 1)]) for side, i in zip(sides, (0, 2))]
    grad_out_w = weight_grads(parts, split_order(order, n_seq), quarters)
    found = scan_begin(carry, True, me, n_seq, (gboth, grad_out_w))
    terms, _ = scatter_head(ffn_out, beside=lambda _: gboth, summed=block_sum[0])
    block_own = (hidden + (terms[0].astype(f32) + terms[1].astype(f32) + terms[2].astype(f32))).astype(bf16)
    carry_in, place_back = scan_end(found, True, me, n_seq)
    carry_in = after(carry_in, block_own)
    block_all = gather_head(block_own, lambda near: (carry_in,))
    far_rows, near_rows = [(head_me // 2 ^ i) * (rows // 2) for i in (1, 0)]

    def finish_back(gval, base):
        (grads,) = by_row(
            functools.partial(finish_back_kernel, heads),
            rows,
            [(qkv, True), (edges, True), (carry_in, False), (gboth, True), (gval, True)] + key_tables,
            [((length, lanes + values), bf16)],
            place=place_back,
            flops=6 * unit_flops,
            base=base,
            count=rows // 2,
        )
        return grads.reshape(count, lanes + values)

    gqkv_far = after(finish_back(gval, far_rows), block_all[2])
    far = quarter_products(gqkv_far, qkv_w, quarters, 3)
    gqkv_near = finish_back(after(gval, far), near_rows)
    near = quarter_products(gqkv_near, qkv_w, quarters, 1)

    def back(value, kind):
        whole = place_quarters(value[:2], quarters, order, kind, 0)
        return place_quarters(value[2:], quarters, order, kind, 2, whole).reshape(rows, length, width)

    rest = hidden_units - cut

    def sum_head(value, earlier):
        pairs = after([send(value, "head", mask, 4) for mask in (1, 2, 3)], earlier)
        return (value + pairs[0]) + (pairs[1] + pairs[2])

    def ffn_outputs(sums):
        sums = jnp.concatenate(sums, axis=1)
        parts = jnp.split(sums, np.cumsum([cut, cut, cut, rest, rest]), axis=1)
        grad_gate, grad_up, grad_down = [jnp.concatenate([parts[i], parts[i + 3]], axis=1) for i in range(3)]
        gain = jnp.sum(gate_weight.astype(f32) * grad_gate + up_weight.astype(f32) * grad_up, axis=1)
        return (grad_gate * gain_two, grad_up * gain_two, grad_down.T), gain

    terms, grad_qkv = scatter_head(
        [near[1], near[0], far[1], far[0]],
        beside=lambda sent: weight_grads(
            [
                ([(after(unit_one, sent), "q", i), (unit_one, "q", i + 1)], [(grads, "q", i), (grads, "q", i + 1)])
                for grads, i in ((gqkv_near, 0), (gqkv_far, 2))
            ],
            split_order(order, n_seq),
            quarters,
        ),
    )
    (grad_x,) = on_quarter(norm_back_kernel, [x_own, grad_hidden, *after(terms, ffn_grads[0])], quarter, [bf16])
    qkv_pairs = scatter_begin(grad_qkv, n_seq)
    qkv_terms = scatter_sends(qkv_pairs)
    out_pairs = scatter_begin(after(grad_out_w, grad_x), n_seq)
    ffn_grads, ffn_gain = ffn_outputs([ffn_grads[0], scatter_end(down_pairs, down_terms), after(ffn_grads[1], grad_x)])
    block_all = back(after(block_all, grad_x), bf16)
    grad_x_all = gather_head(grad_x, lambda near: (*qkv_terms, *out_pairs, ffn_gain, *ffn_grads, block_all))
    out_terms = scatter_sends(out_pairs)
    grad_qkv = scatter_end(qkv_pairs, qkv_terms)
    qkv_gain = jnp.sum(qkv_own.astype(f32) * grad_qkv, axis=1)
    near_placed = place_quarters(grad_x_all[:2], quarters, order, f32, 0)
    out_terms = after(out_terms, near_placed)
    grad_x_all[2] = after(grad_x_all[2], *out_terms)
    grad_x_all = place_quarters(grad_x_all[2:], quarters, order, f32, 2, near_placed).reshape(rows, length, width)
    gains = sum_head(jnp.stack([qkv_gain, ffn_gain]), grad_x_all)
    grad_out_w = scatter_end(out_pairs, out_terms)
    grad_qkv = grad_qkv * gain_one
    narrow = heads * FEAT
    return (
        block_all,
        grad_x_all,
        gains[0],
        gains[1],
        grad_qkv[:, :narrow],
        grad_qkv[:, narrow:lanes],
        grad_qkv[:, lanes:],
        grad_out_w.T,
        *ffn_grads,
    )


def solution(mesh):
    placed = (
        P(None, "seq", None),
        P(None, "seq"),
        P("seq"),
        P("seq"),
        P("seq", "head"),
        P("seq", "head"),
        P("seq", "head"),
        P("head", "seq"),
        P("seq", "head"),
        P("seq", "head"),
        P("head", "seq"),
        P(None, "seq", None),
    )
    return jax.shard_map(
        functools.partial(per_device, mesh.shape["seq"], mesh.shape["head"]),
        mesh=mesh,
        in_specs=placed,
        out_specs=(P(None, "seq", None), P(None, "seq", None)) + placed[2:11],
        check_vma=False,
    )
```
